32 devices in a mesh: rep: 2 (over y), ctx: 4 (over z), ch: 2 (over x), sub: 2 (over core).
Axes of the slice: x: 2, y: 2, z: 4, core: 2. Of those that a mesh axis runs over, the one named last changes fastest.
Arguments:
- hyena_query: bfloat16 [3072, 8192], P(('rep', 'ctx'), ('ch', 'sub')), parts along dimension 0, may hold values from -6 to 6
- hyena_key: bfloat16 [3072, 8192], P(('rep', 'ctx'), ('ch', 'sub')), parts along dimension 0, may hold values from -6 to 6
- hyena_value: bfloat16 [3072, 8192], P(('rep', 'ctx'), ('ch', 'sub')), parts along dimension 0, may hold values from -6 to 6
- filters: bfloat16 [512, 128], P(('ch', 'sub')), may hold values from -0.5 to 0.5
- skip_gain: float32 [8192], P(('ch', 'sub')), may hold values from 0.5 to 1.5
- attn_query: bfloat16 [3072, 8192], P(('rep', 'ctx'), ('ch', 'sub')), parts along dimension 0, may hold values from -40 to 40
- attn_key: bfloat16 [3072, 8192], P(('rep', 'ctx'), ('ch', 'sub')), parts along dimension 0, may hold values from -5 to 5
- genome_starts: int32 [8], P('rep'), parts along dimension 0, may hold values from 0 to 1408, as said below
Outputs:
- hyena_mix: bfloat16 [3072, 8192], P(('rep', 'ctx'), ('ch', 'sub')), parts along dimension 0
- attended: bfloat16 [3072, 8192], P(('rep', 'ctx'), ('ch', 'sub')), parts along dimension 0
The draws below stay inside these ranges and needn't reach their ends.
There are 2 independent parts, one for each index of `rep`. The reference program is written for one: setup_inputs(seed, part) draws one part's arguments, and reference() takes and returns one part's arrays. A program takes and returns all parts, laid end to end along the dimension named above; an argument that names none is the same for every part. Nothing has to cross between parts.
Inputs may be any that keep to these rules, and one draw needn't show every extreme that they name: genome_starts[0] is 0; the entries rise, each by 128 or more, and the last genome holds exactly 128 positions.
All inputs are finite; a program needn't handle non-finite values.
Results may differ from the reference program's by a relative error of at most 0.0059.
Values may be sent and summed in bfloat16 or wider, within the bound.
No kernel may reach another device: no remote copies, remote signals or barrier semaphores. Data moves between devices by JAX's collectives and lax.ppermute only.
A program may use at most 128 MiB of HBM per device.

```python
import math
import jax
import jax.numpy as jnp
from jax import lax

D = 8192
HEAD_DIM = 128
FILTER = 128
GROUP = 16
GENOMES = 4
TOKENS = 1536


def shared_keys(key):
    return jnp.clip(jax.random.normal(jax.random.fold_in(key, 101), (TOKENS, D), jnp.float32), -4.0, 4.0)


def draw_attn_key(key, part):
    return shared_keys(key).astype(jnp.bfloat16)


def draw_attn_query(key, part):
    drawn = 2.0 * jax.random.normal(jax.random.fold_in(key, 201), (TOKENS, D), jnp.float32)
    return jnp.clip(drawn, -8.0, 8.0).astype(jnp.bfloat16)


def draw_genome_starts(key, part):
    cuts = jax.random.randint(jax.random.fold_in(key, 301), (GENOMES - 2,), 0, TOKENS - GENOMES * FILTER + 1, dtype=jnp.int32)
    ordered = jnp.sort(cuts) + FILTER * jnp.arange(1, GENOMES - 1, dtype=jnp.int32)
    last = jnp.full((1,), TOKENS - FILTER, jnp.int32)
    return jnp.concatenate([jnp.zeros((1,), jnp.int32), ordered.astype(jnp.int32), last])


def steps_of(rng, shape, split, smallest, largest):
    loudness, own = 1.0, jax.random.fold_in(rng, 6)
    for dim, blocks in split:
        steps = jnp.exp(jax.random.uniform(jax.random.fold_in(own, dim), (blocks,), jnp.float32, smallest / len(split), largest / len(split)))
        loudness = loudness * jnp.repeat(steps, shape[dim] // blocks).reshape([-1 if axis == dim else 1 for axis in range(len(shape))])
    return loudness


def scatter_about(key, shape, spread, most, shards=(), held_as=jnp.bfloat16):
    values = spread * jax.random.normal(key, shape, jnp.float32)
    if shards:
        values = values * steps_of(key, shape, shards, -0.22, 0.18)
    return jnp.clip(values, -most, most).astype(held_as)


def setup_inputs(seed: int = 0, part: int = 0) -> dict:
    seeds = jax.random.split(jax.random.key(seed), 9)
    part_splits = jax.random.split(jax.random.fold_in(seeds[8], part), 9)
    return {
        "hyena_query": scatter_about(part_splits[0], (TOKENS, D), 1.0, 6.0, ((0, 4), (1, 4))),
        "hyena_key": scatter_about(part_splits[1], (TOKENS, D), 1.0, 6.0, ((0, 4), (1, 4))),
        "hyena_value": scatter_about(part_splits[2], (TOKENS, D), 1.0, 6.0, ((0, 4), (1, 4))),
        "filters": scatter_about(seeds[3], (D // GROUP, FILTER), FILTER ** -0.5, 0.5, ((0, 4),)),
        "skip_gain": jnp.clip(0.5 + 1.0 * jax.random.uniform(seeds[4], (D,), jnp.float32) ** steps_of(seeds[4], (D,), ((0, 4),), -0.2, 0.2), 0.5, 1.5),
        "attn_query": draw_attn_query(jax.random.fold_in(jax.random.fold_in(seeds[8], part), 71), part),
        "attn_key": draw_attn_key(jax.random.fold_in(jax.random.fold_in(seeds[8], part), 71), part),
        "genome_starts": draw_genome_starts(jax.random.fold_in(jax.random.fold_in(seeds[8], part), 71), part),
    }


def genome_begin(positions, genome_starts):
    inside = genome_starts[None, :] <= positions[:, None]
    return lax.optimization_barrier(jnp.max(jnp.where(inside, genome_starts[None, :], 0), axis=1))

def reference(hyena_query, hyena_key, hyena_value, filters, skip_gain, attn_query, attn_key, genome_starts):
    product = lax.optimization_barrier((hyena_key.astype(jnp.float32) * hyena_value.astype(jnp.float32)).astype(jnp.bfloat16))
    positions = jnp.arange(TOKENS, dtype=jnp.int32)
    begins = genome_begin(positions, genome_starts)
    product_wide = product.astype(jnp.float32)
    padded = jnp.concatenate([jnp.zeros((FILTER - 1, D), jnp.float32), product_wide], axis=0)
    filters_wide = filters.astype(jnp.float32)

    def one_tap(total, tap):
        start = (FILTER - 1 - tap).astype(jnp.int32)
        shifted = lax.dynamic_slice_in_dim(padded, start, TOKENS, 0)
        column = lax.dynamic_slice_in_dim(filters_wide, tap.astype(jnp.int32), 1, 1)[:, 0]
        gains = jnp.repeat(column, GROUP)
        valid = positions - tap >= begins
        return (total + jnp.where(valid[:, None], shifted * gains[None, :], jnp.zeros((), jnp.float32)), None)
    filtered, unused = lax.scan(one_tap, jnp.zeros((TOKENS, D), jnp.float32), jnp.arange(FILTER, dtype=jnp.int32))
    hyena_mix = (hyena_query.astype(jnp.float32) * (filtered + skip_gain[None, :] * product_wide)).astype(jnp.bfloat16)
    score_scale = 1.0 / math.sqrt(HEAD_DIM)
    head_count = D // HEAD_DIM
    block = math.gcd(TOKENS, 512)
    blocks = TOKENS // block
    query_heads = attn_query.reshape(TOKENS, head_count, HEAD_DIM).transpose(1, 0, 2)
    key_heads = attn_key.reshape(TOKENS, head_count, HEAD_DIM).transpose(1, 0, 2)
    value_heads = hyena_mix.reshape(TOKENS, head_count, HEAD_DIM).transpose(1, 0, 2)
    pos_blocks = positions.reshape(blocks, block)
    begin_blocks = begins.reshape(blocks, block)

    def one_head(operands):
        query_head, key_head, value_head = operands

        def one_block(block_ops):
            query_block, query_pos, query_begin = block_ops
            visible = (positions[None, :] <= query_pos[:, None]) & (positions[None, :] >= query_begin[:, None])
            scores = jnp.dot(query_block, key_head.T, preferred_element_type=jnp.float32) * score_scale
            highest = lax.optimization_barrier(jnp.max(jnp.where(visible, scores, -1e+30), axis=1, keepdims=True))
            weights = jnp.exp(jnp.where(visible, scores - highest, -1e+30))
            weight_sum = lax.optimization_barrier(jnp.sum(weights, axis=1, keepdims=True))
            mixed = jnp.dot(weights.astype(jnp.bfloat16), value_head, preferred_element_type=jnp.float32) / weight_sum
            return mixed.astype(jnp.bfloat16)
        pieces = lax.map(one_block, (query_head.reshape(blocks, block, HEAD_DIM), pos_blocks, begin_blocks))
        return pieces.reshape(TOKENS, HEAD_DIM)
    outputs = lax.map(one_head, (query_heads, key_heads, value_heads))
    attended = outputs.transpose(1, 0, 2).reshape(TOKENS, D)
    return (hyena_mix, attended)
```

```python
from functools import partial
import math

import jax
import jax.numpy as jnp
from jax import lax
from jax.experimental import pallas as pl
from jax.experimental.pallas import tpu as pltpu
from jax.sharding import PartitionSpec as P

HEAD_DIM = 128
BLOCK = 128
FAR = -1e30
TO_LOG2 = math.log2(math.e) / math.sqrt(HEAD_DIM)
VMEM_LIMIT = 48 * 1024 * 1024
CHUNKS = 4


def begin_of(pos, starts):
    begin = jnp.zeros_like(pos)
    for start in starts:
        begin = jnp.where(pos >= start, start, begin)
    return begin


def hyena_kernel(genomes, group, info, hq, hk, hv, halo, taps, gain, *rest):
    out, full, ext, tall, mask = rest[-5:]
    rows, width = out.shape
    blocks = rows // BLOCK
    groups = width // group
    starts = [info[1 + i] for i in range(genomes)]

    @pl.when(pl.program_id(0) == 0)
    def _():
        for b in range(blocks):
            here = info[0] + b * BLOCK
            row = here + lax.broadcasted_iota(jnp.int32, (BLOCK, 2 * BLOCK), 0)
            col = here - BLOCK + lax.broadcasted_iota(jnp.int32, (BLOCK, 2 * BLOCK), 1)
            same = col >= begin_of(row, starts)
            mask[b] = jnp.where(same, 1.0, 0.0).astype(jnp.bfloat16)

    product = (hk[...].astype(jnp.float32) * hv[...].astype(jnp.float32)).astype(jnp.bfloat16)
    ext[:BLOCK] = halo[...]
    ext[BLOCK:] = product
    for g in range(groups):
        line = jnp.broadcast_to(taps[g : g + 1, :], (BLOCK, 2 * BLOCK))
        tall[g] = pltpu.roll(line, 0, 1, stride=1, stride_axis=0).astype(jnp.bfloat16)
    lane_group = lax.broadcasted_iota(jnp.int32, (BLOCK, width), 1) // group
    for b in range(blocks):
        window = ext[b * BLOCK : (b + 2) * BLOCK, :]
        filtered = jnp.zeros((BLOCK, width), jnp.float32)
        for g in range(groups):
            one = jnp.dot(tall[g] * mask[b], window, preferred_element_type=jnp.float32)
            filtered = jnp.where(lane_group == g, one, filtered)
        at = pl.ds(b * BLOCK, BLOCK)
        direct = ext[(b + 1) * BLOCK : (b + 2) * BLOCK, :].astype(jnp.float32)
        mix = hq[at, :].astype(jnp.float32) * (filtered + gain[...] * direct)
        out[at, :] = mix.astype(jnp.bfloat16)
        full[at, :] = mix.astype(jnp.bfloat16)


def hyena(info, hq, hk, hv, halo, taps, gain, chunk, width, group, genomes, full):
    rows, channels = hk.shape
    first = chunk * width // BLOCK
    here = lambda r: pl.BlockSpec((r, BLOCK), lambda j: (0, j + first))
    in_specs = [
        pl.BlockSpec(memory_space=pltpu.SMEM),
        here(rows),
        here(rows),
        here(rows),
        here(BLOCK),
        pl.BlockSpec((BLOCK // group, 2 * BLOCK), lambda j: (j + first, 0)),
        here(1),
    ]
    operands = [info, hq, hk, hv, halo, taps, gain]
    aliases = {}
    if full is not None:
        in_specs.append(pl.BlockSpec(memory_space=pl.ANY))
        operands.append(full)
        aliases = {len(operands) - 1: 1}
    return pl.pallas_call(
        partial(hyena_kernel, genomes, group),
        grid=(width // BLOCK,),
        in_specs=in_specs,
        out_specs=[pl.BlockSpec((rows, BLOCK), lambda j: (0, j)), here(rows)],
        out_shape=[
            jax.ShapeDtypeStruct((rows, width), jnp.bfloat16),
            jax.ShapeDtypeStruct((rows, channels), jnp.bfloat16),
        ],
        scratch_shapes=[
            pltpu.VMEM((rows + BLOCK, BLOCK), jnp.bfloat16),
            pltpu.VMEM((BLOCK // group, BLOCK, 2 * BLOCK), jnp.bfloat16),
            pltpu.VMEM((rows // BLOCK, BLOCK, 2 * BLOCK), jnp.bfloat16),
        ],
        input_output_aliases=aliases,
        compiler_params=pltpu.CompilerParams(vmem_limit_bytes=VMEM_LIMIT),
        cost_estimate=pl.CostEstimate(
            flops=2 * rows * width * 2 * BLOCK * 8,
            bytes_accessed=2 * rows * width * 5,
            transcendentals=0,
        ),
        name="hyena_mix",
    )(*operands)


def attend_kernel(genomes, sizes, info, q, k, v, *rest):
    rows = q.shape[0]
    na, nb, nk = sizes
    rest = list(rest)
    qa = rest.pop(0) if na else None
    qb = rest.pop(0) if nb else None
    rk, rv = (rest.pop(0), rest.pop(0)) if nk else (None, None)
    jobs = [(rows, q, 0, 0, None)]
    if na:
        jobs.append((na, qa, rows, 1, 2))
    if nb:
        jobs.append((nb, qb, rows + na, 3, 4))
    outs = [(rest.pop(0), rest.pop(0)) for _ in jobs]
    bias, stat = rest
    starts = [info[7 + i] for i in range(genomes)]
    head = pl.program_id(0)
    own, k_at, k_on = info[0], info[5], info[6]

    @pl.when(head == 0)
    def _():
        for count, _, at, where, _ in jobs:
            for i in range(count // BLOCK):
                sl = pl.ds(at + i * BLOCK, BLOCK)
                for base, width, left in ((own, rows, 0), (k_at, nk, rows)):
                    if width:
                        row = info[where] + i * BLOCK
                        row = row + lax.broadcasted_iota(jnp.int32, (BLOCK, width), 0)
                        col = base + lax.broadcasted_iota(jnp.int32, (BLOCK, width), 1)
                        seen = (col <= row) & (col >= begin_of(row, starts))
                        bias[sl, left : left + width] = jnp.where(seen, 0.0, FAR)

    lane = lax.broadcasted_iota(jnp.int32, (BLOCK, BLOCK), 1)

    def piece(queries, out, sl, at, near, far):
        q_block = queries[sl, :]
        sets = [(k[:near, :], v[:near, :], bias[at, :near])]
        if far:
            sets.append((rk[...], rv[...], bias[at, rows:]))
        scores = [
            lax.dot_general(
                q_block, keys, (((1,), (1,)), ((), ())), preferred_element_type=jnp.float32
            )
            + hidden
            for keys, _, hidden in sets
        ]
        top = jnp.max(scores[0], axis=1, keepdims=True)
        for s in scores[1:]:
            top = jnp.maximum(top, jnp.max(s, axis=1, keepdims=True))
        weights = [jnp.exp2((s - top) * TO_LOG2) for s in scores]
        total = sum(jnp.sum(w, axis=1, keepdims=True) for w in weights)
        mixed = sum(
            jnp.dot(w.astype(jnp.bfloat16), values, preferred_element_type=jnp.float32)
            for w, (_, values, _) in zip(weights, sets)
        )
        out[sl, :] = (mixed / total).astype(jnp.bfloat16)
        stat[at, :] = jnp.where(lane == head, top * TO_LOG2 + jnp.log2(total), stat[at, :])

    for (count, queries, at, where, flag), (out, _) in zip(jobs, outs):
        for i in range(count // BLOCK):
            sl = pl.ds(i * BLOCK, BLOCK)
            both = pl.ds(at + i * BLOCK, BLOCK)
            begin = begin_of(info[where] + i * BLOCK, starts)
            near = (i + 1) * BLOCK if flag is None else rows
            on = True if flag is None else (info[flag] != 0) & (begin < own + rows)
            if nk:
                far = (k_on != 0) & (begin < own)

                @pl.when(on & far)
                def _():
                    piece(queries, out, sl, both, near, True)

                near_only = on & jnp.logical_not(far)
            else:
                near_only = on

            if near_only is True:
                piece(queries, out, sl, both, near, False)
            else:

                @pl.when(near_only)
                def _():
                    piece(queries, out, sl, both, near, False)

            if flag is not None:

                @pl.when(jnp.logical_not(on))
                def _():
                    out[sl, :] = jnp.zeros((BLOCK, HEAD_DIM), jnp.bfloat16)
                    stat[both, :] = jnp.full((BLOCK, BLOCK), FAR, jnp.float32)

    @pl.when(head == pl.num_programs(0) - 1)
    def _():
        for (count, _, at, _, _), (_, out) in zip(jobs, outs):
            heads = out.shape[0]
            for i in range(count // BLOCK):
                turned = stat[pl.ds(at + i * BLOCK, BLOCK), :].T
                out[:, i * BLOCK : (i + 1) * BLOCK] = turned[:heads, :]


def padded_heads(heads):
    return -(-heads // 8) * 8


def attend(info, q, k, v, qa, qb, rk, rv, chunk, genomes):
    rows, width = v.shape
    heads = width // HEAD_DIM
    first = chunk * heads
    na, nb, nk = (x.shape[0] if x is not None else 0 for x in (qa, qb, rk))
    here = lambda r: pl.BlockSpec((r, HEAD_DIM), lambda h: (0, h))
    whole = lambda r: pl.BlockSpec((r, HEAD_DIM), lambda h: (0, h + first))
    in_specs = [pl.BlockSpec(memory_space=pltpu.SMEM), whole(rows), whole(rows), here(rows)]
    operands = [info, q, k, v]
    for x in (qa, qb, rk, rv):
        if x is not None:
            in_specs.append(here(x.shape[0]))
            operands.append(x)
    out_specs, out_shape = [], []
    hp = padded_heads(heads)
    for count in (rows, na, nb):
        if count:
            out_specs += [here(count), pl.BlockSpec((hp, count), lambda h: (0, 0))]
            out_shape += [
                jax.ShapeDtypeStruct((count, width), jnp.bfloat16),
                jax.ShapeDtypeStruct((hp, count), jnp.float32),
            ]
    queries, keys = rows + na + nb, rows + nk
    return pl.pallas_call(
        partial(attend_kernel, genomes, (na, nb, nk)),
        grid=(heads,),
        in_specs=in_specs,
        out_specs=out_specs,
        out_shape=out_shape,
        scratch_shapes=[
            pltpu.VMEM((queries, keys), jnp.float32),
            pltpu.VMEM((queries, BLOCK), jnp.float32),
        ],
        compiler_params=pltpu.CompilerParams(vmem_limit_bytes=VMEM_LIMIT),
        cost_estimate=pl.CostEstimate(
            flops=8 * heads * queries * keys * HEAD_DIM,
            bytes_accessed=4 * width * (queries + keys),
            transcendentals=heads * queries * keys,
        ),
        name="attend_parts",
    )(*operands)


def join_kernel(sizes, info, o, s, *rest):
    na, nb = sizes
    rest = list(rest)
    parts = [(rest.pop(0), rest.pop(0), n, i) for i, n in enumerate((na, nb)) if n]
    out = rest[-1]
    rows, width = o.shape
    for i in range(rows // BLOCK):
        sl = pl.ds(i * BLOCK, BLOCK)
        cols = slice(i * BLOCK, (i + 1) * BLOCK)
        present = [(o, s[:, cols])]
        for po, ps, n, flag in parts:
            if i * BLOCK < n:
                present.append((po, jnp.where(info[flag] != 0, ps[:, cols], FAR)))
        if len(present) == 1:
            out[sl, :] = o[sl, :]
            continue
        top = present[0][1]
        for _, x in present[1:]:
            top = jnp.maximum(top, x)
        weights = [jnp.exp2(x - top) for _, x in present]
        total = sum(weights)
        weights = [(w / total).T for w in weights]
        for h in range(width // HEAD_DIM):
            lanes = slice(h * HEAD_DIM, (h + 1) * HEAD_DIM)
            mixed = sum(
                w[:, h : h + 1] * part[sl, lanes].astype(jnp.float32)
                for w, (part, _) in zip(weights, present)
            )
            out[sl, lanes] = mixed.astype(jnp.bfloat16)


def join(info, o, s, others, chunk, channels, full):
    rows, width = o.shape
    operands = [info, o, s]
    sizes = []
    for other in others:
        sizes.append(other[0].shape[0] if other is not None else 0)
        if other is not None:
            operands += list(other)
    whole = lambda x: pl.BlockSpec(x.shape, lambda i: (0, 0))
    in_specs = [pl.BlockSpec(memory_space=pltpu.SMEM)] + [whole(x) for x in operands[1:]]
    aliases = {}
    if full is not None:
        in_specs.append(pl.BlockSpec(memory_space=pl.ANY))
        operands.append(full)
        aliases = {len(operands) - 1: 0}
    return pl.pallas_call(
        partial(join_kernel, sizes),
        grid=(1,),
        in_specs=in_specs,
        out_specs=pl.BlockSpec((rows, width), lambda i: (0, chunk)),
        out_shape=jax.ShapeDtypeStruct((rows, channels), jnp.bfloat16),
        input_output_aliases=aliases,
        compiler_params=pltpu.CompilerParams(vmem_limit_bytes=VMEM_LIMIT),
        cost_estimate=pl.CostEstimate(
            flops=6 * rows * width, bytes_accessed=8 * rows * width, transcendentals=0
        ),
        name="join_parts",
    )(*operands)


class Plan:
    def __init__(self, down_1, rows_1, down_2, rows_2, up, rows_up):
        self.a = [(l + 1, l) for l in down_1]
        self.b = [(d + 2, d) for d in down_2]
        self.k = [(l, l + 1) for l in up]
        self.na = rows_1 if down_1 else 0
        self.nb = rows_2 if down_2 else 0
        self.nk = rows_up if up else 0


def table(flags, me):
    return jnp.asarray(flags, jnp.int32)[me]


def run_plan(plan, hq, hk, hv, taps, gain, q, k, starts, group):
    n = lax.axis_size("ctx")
    me = lax.axis_index("ctx")
    rows, channels = hk.shape
    genomes = starts.shape[0]
    own = (me * rows).astype(jnp.int32)
    halo = (
        hk[rows - BLOCK :].astype(jnp.float32) * hv[rows - BLOCK :].astype(jnp.float32)
    ).astype(jnp.bfloat16)
    halo = lax.ppermute(halo, "ctx", [(i, i + 1) for i in range(n - 1)])

    hyena_info = jnp.concatenate([own[None], starts])
    takes = lambda pairs: [int(any(t == d for _, t in pairs)) for d in range(n)]
    gives = lambda pairs: [int(any(s == d for s, _ in pairs)) for d in range(n)]
    back = lambda pairs: [(t, s) for s, t in pairs]
    attend_info = jnp.concatenate(
        [
            jnp.stack(
                [
                    own,
                    own + rows,
                    table(takes(plan.a), me),
                    own + 2 * rows,
                    table(takes(plan.b), me),
                    own - plan.nk,
                    table(takes(plan.k), me),
                ]
            ),
            starts,
        ]
    )
    join_info = jnp.stack([table(gives(plan.a), me), table(gives(plan.b), me)])

    width = channels // CHUNKS
    mix_full, out_full = None, None
    for c in range(CHUNKS):
        cols = slice(c * width, (c + 1) * width)
        qa = lax.ppermute(q[: plan.na, cols], "ctx", plan.a) if plan.na else None
        qb = lax.ppermute(q[: plan.nb, cols], "ctx", plan.b) if plan.nb else None
        rk = lax.ppermute(k[rows - plan.nk :, cols], "ctx", plan.k) if plan.nk else None
        mix, mix_full = hyena(
            hyena_info, hq, hk, hv, halo, taps, gain, c, width, group, genomes, mix_full
        )
        rv = lax.ppermute(mix[rows - plan.nk :], "ctx", plan.k) if plan.nk else None
        parts = attend(attend_info, q, k, mix, qa, qb, rk, rv, c, genomes)
        o, s = parts[:2]
        parts = parts[2:]
        others = []
        for count, pairs in ((plan.na, plan.a), (plan.nb, plan.b)):
            if count:
                others.append([lax.ppermute(x, "ctx", back(pairs)) for x in parts[:2]])
                parts = parts[2:]
            else:
                others.append(None)
        out_full = join(join_info, o, s, others, c, channels, out_full)
    return mix_full, out_full


def attend_update(queries, query_pos, query_begin, key_heads, value_heads, key_pos):
    score_scale = 1.0 / math.sqrt(HEAD_DIM)
    scores = (
        jnp.einsum("qhd,khd->hqk", queries, key_heads, preferred_element_type=jnp.float32)
        * score_scale
    )
    visible = (key_pos[None, :] <= query_pos[:, None]) & (key_pos[None, :] >= query_begin[:, None])
    new_max = jnp.max(jnp.where(visible[None], scores, FAR), axis=2)
    weights = jnp.exp(jnp.where(visible[None], scores - new_max[:, :, None], FAR))
    mixed = jnp.einsum(
        "hqk,khd->hqd",
        weights.astype(jnp.bfloat16),
        value_heads,
        preferred_element_type=jnp.float32,
    )
    return mixed / jnp.sum(weights, axis=2)[:, :, None]


def run_gathered(hq, hk, hv, taps, gain, q, k, starts, group):
    n = lax.axis_size("ctx")
    me = lax.axis_index("ctx")
    rows, channels = hk.shape
    heads = channels // HEAD_DIM
    own = (me * rows).astype(jnp.int32)
    halo = (
        hk[rows - BLOCK :].astype(jnp.float32) * hv[rows - BLOCK :].astype(jnp.float32)
    ).astype(jnp.bfloat16)
    halo = lax.ppermute(halo, "ctx", [(i, i + 1) for i in range(n - 1)])
    info = jnp.concatenate([own[None], starts])
    _, mix = hyena(
        info, hq, hk, hv, halo, taps, gain, 0, channels, group, starts.shape[0], None
    )
    keys = lax.all_gather(k, "ctx", axis=0, tiled=True)
    values = lax.all_gather(mix, "ctx", axis=0, tiled=True)
    key_pos = jnp.arange(n * rows, dtype=jnp.int32)
    pos = own + jnp.arange(rows, dtype=jnp.int32)
    mixed = attend_update(
        q.reshape(rows, heads, HEAD_DIM),
        pos,
        begin_of(pos, [starts[i] for i in range(starts.shape[0])]),
        keys.reshape(n * rows, heads, HEAD_DIM),
        values.reshape(n * rows, heads, HEAD_DIM),
        key_pos,
    )
    return mix, mixed.astype(jnp.bfloat16).transpose(1, 0, 2).reshape(rows, channels)


def per_device(hq, hk, hv, filters, skip_gain, q, k, starts):
    rows, channels = hk.shape
    group = channels // filters.shape[0]
    taps = jnp.pad(filters[:, ::-1].astype(jnp.float32), ((0, 0), (1, BLOCK - 1)))
    gain = skip_gain[None, :]
    if lax.axis_size("ctx") != 4:
        return run_gathered(hq, hk, hv, taps, gain, q, k, starts, group)
    plan = Plan([1, 2], rows, [1], rows - BLOCK, [0], rows)
    return run_plan(plan, hq, hk, hv, taps, gain, q, k, starts, group)


def solution(mesh):
    split = P(("rep", "ctx"), ("ch", "sub"))
    return jax.shard_map(
        per_device,
        mesh=mesh,
        in_specs=(
            split,
            split,
            split,
            P(("ch", "sub"), None),
            P(("ch", "sub")),
            split,
            split,
            P("rep"),
        ),
        out_specs=(split, split),
        check_vma=False,
    )
```

```python
from functools import partial
import math

import jax
import jax.numpy as jnp
from jax import lax
from jax.experimental import pallas as pl
from jax.experimental.pallas import tpu as pltpu
from jax.sharding import PartitionSpec as P

HEAD_DIM = 128
BLOCK = 128
FAR = -1e30
TO_LOG2 = math.log2(math.e) / math.sqrt(HEAD_DIM)
VMEM_LIMIT = 48 * 1024 * 1024
HEADS_AT_ONCE = 4
STAT_ROWS = 32


def begin_of(pos, starts):
    begin = jnp.zeros_like(pos)
    for start in starts:
        begin = jnp.where(pos >= start, start, begin)
    return begin


def compiler_params():
    return pltpu.CompilerParams(vmem_limit_bytes=VMEM_LIMIT)


def rounded_product(key, value):
    return (key.astype(jnp.float32) * value.astype(jnp.float32)).astype(jnp.bfloat16)


def halo_kernel(hk, hv, out):
    out[...] = rounded_product(hk[...], hv[...])


def halo_product(hk, hv):
    rows, channels = hk.shape
    width = min(channels, 512)
    last = pl.BlockSpec((BLOCK, width), lambda j: (rows // BLOCK - 1, j))
    return pl.pallas_call(
        halo_kernel,
        grid=(channels // width,),
        in_specs=[last, last],
        out_specs=pl.BlockSpec((BLOCK, width), lambda j: (0, j)),
        out_shape=jax.ShapeDtypeStruct((BLOCK, channels), jnp.bfloat16),
        compiler_params=compiler_params(),
        cost_estimate=pl.CostEstimate(
            flops=BLOCK * channels, bytes_accessed=6 * BLOCK * channels, transcendentals=0
        ),
        name="halo_product",
    )(hk, hv)


def hyena_kernel(genomes, group, info, hq, hk, hv, halo, filters, gain, out, lines, ext, tall):
    rows, width = out.shape
    blocks = rows // BLOCK
    groups = width // group
    starts = [info[i] for i in range(genomes)]
    step = pl.program_id(0)
    first = lax.axis_index("ctx") * rows

    @pl.when(step == 0)
    def _():
        tap = lax.broadcasted_iota(jnp.int32, (BLOCK, 2 * BLOCK), 0)
        col = lax.broadcasted_iota(jnp.int32, (BLOCK, 2 * BLOCK), 1)
        turn = jnp.where(tap + col == BLOCK, 1.0, 0.0).astype(jnp.bfloat16)
        lines[...] = jnp.dot(filters[...], turn, preferred_element_type=jnp.float32)

    ext[:BLOCK] = halo[...]
    ext[BLOCK:] = rounded_product(hk[...], hv[...])
    ours = lines[pl.ds(pl.multiple_of(step * groups, groups), groups), :]
    for g in range(groups):
        line = jnp.broadcast_to(ours[g : g + 1, :], (16, 2 * BLOCK))
        few = pltpu.roll(line, 0, 1, stride=1, stride_axis=0).astype(jnp.bfloat16)
        for a in range(BLOCK // 16):
            at = g * BLOCK + a * 16
            tall[at : at + 16, :] = few if a == 0 else pltpu.roll(few, 16 * a, 1)
    lane_group = lax.broadcasted_iota(jnp.int32, (BLOCK, width), 1) // group

    def finish(b, parts):
        filtered = parts[0]
        for g in range(1, groups):
            filtered = jnp.where(lane_group == g, parts[g], filtered)
        at = pl.ds(b * BLOCK, BLOCK)
        direct = ext[(b + 1) * BLOCK : (b + 2) * BLOCK, :].astype(jnp.float32)
        mix = hq[at, :].astype(jnp.float32) * (filtered + gain[...] * direct)
        out[at, :] = mix.astype(jnp.bfloat16)

    for b in range(blocks):
        here = first + b * BLOCK
        window = ext[b * BLOCK : (b + 2) * BLOCK, :]
        cut = begin_of(here + BLOCK - 1, starts) > here - BLOCK

        @pl.when(jnp.logical_not(cut))
        def _():
            every = jnp.dot(tall[...], window, preferred_element_type=jnp.float32)
            finish(b, [every[g * BLOCK : (g + 1) * BLOCK] for g in range(groups)])

        @pl.when(cut)
        def _():
            row = here + lax.broadcasted_iota(jnp.int32, (BLOCK, 2 * BLOCK), 0)
            col = here - BLOCK + lax.broadcasted_iota(jnp.int32, (BLOCK, 2 * BLOCK), 1)
            seen = jnp.where(col >= begin_of(row, starts), 1.0, 0.0).astype(jnp.bfloat16)
            finish(
                b,
                [
                    jnp.dot(
                        tall[g * BLOCK : (g + 1) * BLOCK, :] * seen,
                        window,
                        preferred_element_type=jnp.float32,
                    )
                    for g in range(groups)
                ],
            )


def hyena(starts, hq, hk, hv, halo, filters, gain):
    rows, channels = hk.shape
    group = channels // filters.shape[0]
    here = lambda r: pl.BlockSpec((r, BLOCK), lambda j: (0, j))
    return pl.pallas_call(
        partial(hyena_kernel, starts.shape[0], group),
        grid=(channels // BLOCK,),
        in_specs=[
            pl.BlockSpec(memory_space=pltpu.SMEM),
            here(rows),
            here(rows),
            here(rows),
            here(BLOCK),
            pl.BlockSpec(filters.shape, lambda j: (0, 0)),
            here(1),
        ],
        out_specs=here(rows),
        out_shape=jax.ShapeDtypeStruct((rows, channels), jnp.bfloat16),
        scratch_shapes=[
            pltpu.VMEM((filters.shape[0], 2 * BLOCK), jnp.float32),
            pltpu.VMEM((rows + BLOCK, BLOCK), jnp.bfloat16),
            pltpu.VMEM((BLOCK // group * BLOCK, 2 * BLOCK), jnp.bfloat16),
        ],
        compiler_params=compiler_params(),
        cost_estimate=pl.CostEstimate(
            flops=2 * rows * channels * 2 * BLOCK * 8,
            bytes_accessed=2 * rows * channels * 4,
            transcendentals=0,
        ),
        name="hyena_mix",
    )(starts, hq, hk, hv, halo, filters, gain)


def one_of(flags, me):
    on = me < 0
    for d, flag in enumerate(flags):
        if flag:
            on = on | (me == d)
    return on


def attend_kernel(genomes, plan, info, q, k, v, *rest):
    rows, width = q.shape
    me = lax.axis_index("ctx")
    own = me * rows
    rest = list(rest)
    jobs = [(rows, q, own, None)]
    if plan.na:
        jobs.append((plan.na, rest.pop(0), own + rows, one_of(plan.a_to, me)))
    if plan.nb:
        jobs.append((plan.nb, rest.pop(0), own + 2 * rows, one_of(plan.b_to, me)))
    rk, rv = (rest.pop(0), rest.pop(0)) if plan.nk else (None, None)
    out, stats = rest.pop(0), rest.pop(0)
    outs = [out] + rest
    starts = [info[i] for i in range(genomes)]
    heads = width // HEAD_DIM
    lane = lax.broadcasted_iota(jnp.int32, (BLOCK, BLOCK), 1)

    def seen(row_at, col_at, columns):
        row = row_at + lax.broadcasted_iota(jnp.int32, (BLOCK, columns), 0)
        col = col_at + lax.broadcasted_iota(jnp.int32, (BLOCK, columns), 1)
        begin = begin_of(row_at + lax.broadcasted_iota(jnp.int32, (BLOCK, 1), 0), starts)
        return (col <= row) & (col >= begin)

    def piece(queries, out, i, row_at, near, far, put):
        sl = pl.ds(i * BLOCK, BLOCK)
        sets = [(k, v, near, seen(row_at, own, near))]
        if far:
            sets.append((rk, rv, plan.nk, seen(row_at, own - plan.nk, plan.nk)))
        stat = jnp.zeros((BLOCK, BLOCK), jnp.float32)
        for h in range(heads):
            lanes = slice(h * HEAD_DIM, (h + 1) * HEAD_DIM)
            q_block = queries[sl, lanes]
            scores = [
                jnp.where(
                    visible,
                    lax.dot_general(
                        q_block,
                        keys[:count, lanes],
                        (((1,), (1,)), ((), ())),
                        preferred_element_type=jnp.float32,
                    ),
                    FAR,
                )
                for keys, _, count, visible in sets
            ]
            top = jnp.max(scores[0], axis=1, keepdims=True)
            for s in scores[1:]:
                top = jnp.maximum(top, jnp.max(s, axis=1, keepdims=True))
            weights = [jnp.exp2((s - top) * TO_LOG2) for s in scores]
            total = sum(jnp.sum(w, axis=1, keepdims=True) for w in weights)
            mixed = sum(
                jnp.dot(
                    w.astype(jnp.bfloat16),
                    values[:count, lanes],
                    preferred_element_type=jnp.float32,
                )
                for w, (_, values, count, _) in zip(weights, sets)
            )
            out[sl, lanes] = (mixed / total).astype(jnp.bfloat16)
            stat = jnp.where(lane == h, top * TO_LOG2 + jnp.log2(total), stat)
        put(stat.T[:8, :])

    for (count, queries, at, on), out in zip(jobs, outs):
        for i in range(count // BLOCK):
            cols = slice(i * BLOCK, (i + 1) * BLOCK)
            row_at = at + i * BLOCK
            begin = begin_of(row_at, starts)
            if on is None:
                near = (i + 1) * BLOCK

                def put(stat):
                    stats[:, cols] = stat

                far = begin < own
                block_on = True
            else:
                near = rows

                def put(stat):
                    high = stat.astype(jnp.bfloat16).astype(jnp.float32)
                    middle = (stat - high).astype(jnp.bfloat16).astype(jnp.float32)
                    low = stat - high - middle
                    carried = jnp.concatenate([high, middle, low, jnp.zeros_like(low)])
                    out[count : count + STAT_ROWS, cols] = carried.astype(jnp.bfloat16)

                block_on = on & (begin < own + rows)
                far = on & (begin < own)
            if plan.nk:
                far = far & one_of(plan.k_to, me)

                @pl.when(far)
                def _():
                    piece(queries, out, i, row_at, near, True, put)

                near_only = block_on & jnp.logical_not(far)
            else:
                near_only = block_on
            if near_only is True:
                piece(queries, out, i, row_at, near, False, put)
            else:

                @pl.when(near_only)
                def _():
                    piece(queries, out, i, row_at, near, False, put)

            if on is not None:

                @pl.when(jnp.logical_not(block_on))
                def _():
                    out[pl.ds(i * BLOCK, BLOCK), :] = jnp.zeros((BLOCK, width), jnp.bfloat16)
                    put(jnp.full((8, BLOCK), FAR, jnp.float32))


def attend(plan, starts, q, k, v, qa, qb, rk, rv, first, heads):
    rows = q.shape[0]
    width = HEADS_AT_ONCE * HEAD_DIM
    steps = heads // HEADS_AT_ONCE
    skip = first // HEADS_AT_ONCE
    here = lambda r: pl.BlockSpec((r, width), lambda h: (0, h))
    whole = lambda r: pl.BlockSpec((r, width), lambda h: (0, h + skip))
    in_specs = [pl.BlockSpec(memory_space=pltpu.SMEM), whole(rows), whole(rows), whole(rows)]
    operands = [starts, q, k, v]
    for x in (qa, qb, rk, rv):
        if x is not None:
            in_specs.append(here(x.shape[0]))
            operands.append(x)
    out_specs = [here(rows), pl.BlockSpec((8, rows), lambda h: (h, 0))]
    out_shape = [
        jax.ShapeDtypeStruct((rows, heads * HEAD_DIM), jnp.bfloat16),
        jax.ShapeDtypeStruct((steps * 8, rows), jnp.float32),
    ]
    for count in (plan.na, plan.nb):
        if count:
            out_specs.append(here(count + STAT_ROWS))
            out_shape.append(
                jax.ShapeDtypeStruct((count + STAT_ROWS, heads * HEAD_DIM), jnp.bfloat16)
            )
    queries, keys = rows + plan.na + plan.nb, rows + plan.nk
    return pl.pallas_call(
        partial(attend_kernel, starts.shape[0], plan),
        grid=(steps,),
        in_specs=in_specs,
        out_specs=out_specs,
        out_shape=out_shape,
        compiler_params=compiler_params(),
        cost_estimate=pl.CostEstimate(
            flops=4 * heads * queries * keys * HEAD_DIM,
            bytes_accessed=4 * heads * HEAD_DIM * (queries + keys),
            transcendentals=heads * queries * keys,
        ),
        name="attend_parts",
    )(*operands)


def join_kernel(plan, o, s, *rest):
    rest = list(rest)
    me = lax.axis_index("ctx")
    parts = []
    if plan.na:
        parts.append((rest.pop(0), plan.na, one_of(plan.a_from, me)))
    if plan.nb:
        parts.append((rest.pop(0), plan.nb, one_of(plan.b_from, me)))
    out = rest[-1]
    rows, width = o.shape
    for i in range(rows // BLOCK):
        sl = pl.ds(i * BLOCK, BLOCK)
        cols = slice(i * BLOCK, (i + 1) * BLOCK)
        present = [(o, s[:, cols])]
        for part, count, on in parts:
            if i * BLOCK < count:
                carried = part[count : count + STAT_ROWS, cols].astype(jnp.float32)
                stat = carried[:8] + carried[8:16] + carried[16:24]
                present.append((part, jnp.where(on, stat, FAR)))
        if len(present) == 1:
            out[sl, :] = o[sl, :]
            continue
        top = present[0][1]
        for _, x in present[1:]:
            top = jnp.maximum(top, x)
        weights = [jnp.exp2(x - top) for _, x in present]
        total = sum(weights)
        weights = [(w / total).T for w in weights]
        for h in range(width // HEAD_DIM):
            lanes = slice(h * HEAD_DIM, (h + 1) * HEAD_DIM)
            mixed = sum(
                w[:, h : h + 1] * part[sl, lanes].astype(jnp.float32)
                for w, (part, _) in zip(weights, present)
            )
            out[sl, lanes] = mixed.astype(jnp.bfloat16)


def join(plan, o, s, others, first, channels, full):
    rows, wide = o.shape
    width = HEADS_AT_ONCE * HEAD_DIM
    skip = first // HEADS_AT_ONCE
    here = lambda r: pl.BlockSpec((r, width), lambda h: (0, h))
    operands = [o, s] + others
    in_specs = [here(rows), pl.BlockSpec((8, rows), lambda h: (h, 0))]
    in_specs += [here(x.shape[0]) for x in others]
    aliases = {}
    if full is not None:
        in_specs.append(pl.BlockSpec(memory_space=pl.ANY))
        operands.append(full)
        aliases = {len(operands) - 1: 0}
    return pl.pallas_call(
        partial(join_kernel, plan),
        grid=(wide // width,),
        in_specs=in_specs,
        out_specs=pl.BlockSpec((rows, width), lambda h: (0, h + skip)),
        out_shape=jax.ShapeDtypeStruct((rows, channels), jnp.bfloat16),
        input_output_aliases=aliases,
        compiler_params=compiler_params(),
        cost_estimate=pl.CostEstimate(
            flops=6 * rows * wide, bytes_accessed=8 * rows * wide, transcendentals=0
        ),
        name="join_parts",
    )(*operands)


class Plan:
    def __init__(self, n, down_1, rows_1, down_2, rows_2, up, rows_up, heads):
        self.a = [(l + 1, l) for l in down_1]
        self.b = [(d + 2, d) for d in down_2]
        self.k = [(l, l + 1) for l in up]
        self.na = rows_1 if down_1 else 0
        self.nb = rows_2 if down_2 else 0
        self.nk = rows_up if up else 0
        self.heads = heads
        ends = lambda pairs, side: [int(any(p[side] == d for p in pairs)) for d in range(n)]
        self.a_from, self.a_to = ends(self.a, 0), ends(self.a, 1)
        self.b_from, self.b_to = ends(self.b, 0), ends(self.b, 1)
        self.k_to = ends(self.k, 1)


def after(value, *earlier):
    return lax.optimization_barrier((value, *earlier))[0]


def run_plan(plan, hq, hk, hv, filters, gain, q, k, starts):
    n = lax.axis_size("ctx")
    rows, channels = hk.shape
    send = lambda x, pairs: lax.ppermute(x, "ctx", pairs)
    back = lambda pairs: [(t, s) for s, t in pairs]
    halo = send(halo_product(hk, hv), [(i, i + 1) for i in range(n - 1)])
    mix = hyena(starts, hq, hk, hv, halo, filters, gain)

    first, out = 0, None
    qa = qb = rk = rv = None
    for heads in plan.heads:
        cols = slice(first * HEAD_DIM, (first + heads) * HEAD_DIM)
        if plan.na:
            queries = q[: plan.na, cols]
            qa = send(queries if qa is None else after(queries, qa), plan.a)
        if plan.nb:
            queries = q[: plan.nb, cols]
            qb = send(queries if qb is None else after(queries, qb), plan.b)
        if plan.nk:
            keys, values = k[rows - plan.nk :, cols], mix[rows - plan.nk :, cols]
            rk = send(keys if rk is None else after(keys, rk), plan.k)
            rv = send(values if rv is None else after(values, rv), plan.k)
        o, s, *parts = attend(plan, starts, q, k, mix, qa, qb, rk, rv, first, heads)
        pairs = [p for p in (plan.a, plan.b) if p]
        others = [send(x, back(p)) for x, p in zip(parts, pairs)]
        out = join(plan, o, s, others, first, channels, out)
        first += heads
    return mix, out


def attend_update(queries, query_pos, query_begin, key_heads, value_heads, key_pos):
    score_scale = 1.0 / math.sqrt(HEAD_DIM)
    scores = (
        jnp.einsum("qhd,khd->hqk", queries, key_heads, preferred_element_type=jnp.float32)
        * score_scale
    )
    visible = (key_pos[None, :] <= query_pos[:, None]) & (key_pos[None, :] >= query_begin[:, None])
    new_max = jnp.max(jnp.where(visible[None], scores, FAR), axis=2)
    weights = jnp.exp(jnp.where(visible[None], scores - new_max[:, :, None], FAR))
    mixed = jnp.einsum(
        "hqk,khd->hqd",
        weights.astype(jnp.bfloat16),
        value_heads,
        preferred_element_type=jnp.float32,
    )
    return mixed / jnp.sum(weights, axis=2)[:, :, None]


def run_gathered(hq, hk, hv, filters, gain, q, k, starts):
    n = lax.axis_size("ctx")
    rows, channels = hk.shape
    heads = channels // HEAD_DIM
    own = (lax.axis_index("ctx") * rows).astype(jnp.int32)
    halo = lax.ppermute(halo_product(hk, hv), "ctx", [(i, i + 1) for i in range(n - 1)])
    mix = hyena(starts, hq, hk, hv, halo, filters, gain)
    keys = lax.all_gather(k, "ctx", axis=0, tiled=True)
    values = lax.all_gather(mix, "ctx", axis=0, tiled=True)
    key_pos = jnp.arange(n * rows, dtype=jnp.int32)
    pos = own + jnp.arange(rows, dtype=jnp.int32)
    mixed = attend_update(
        q.reshape(rows, heads, HEAD_DIM),
        pos,
        begin_of(pos, [starts[i] for i in range(starts.shape[0])]),
        keys.reshape(n * rows, heads, HEAD_DIM),
        values.reshape(n * rows, heads, HEAD_DIM),
        key_pos,
    )
    return mix, mixed.astype(jnp.bfloat16).transpose(1, 0, 2).reshape(rows, channels)


def per_device(hq, hk, hv, filters, skip_gain, q, k, starts):
    rows, channels = hk.shape
    n = lax.axis_size("ctx")
    gain = skip_gain[None, :]
    if n != 4:
        return run_gathered(hq, hk, hv, filters, gain, q, k, starts)
    plan = Plan(n, [1, 2], rows, [1], rows - BLOCK, [0], rows, [4, 4, 4, 4])
    return run_plan(plan, hq, hk, hv, filters, gain, q, k, starts)


def solution(mesh):
    split = P(("rep", "ctx"), ("ch", "sub"))
    return jax.shard_map(
        per_device,
        mesh=mesh,
        in_specs=(
            split,
            split,
            split,
            P(("ch", "sub"), None),
            P(("ch", "sub")),
            split,
            split,
            P("rep"),
        ),
        out_specs=(split, split),
        check_vma=False,
    )
```

```python
from functools import partial
import math

import jax
import jax.numpy as jnp
from jax import lax
from jax.experimental import pallas as pl
from jax.experimental.pallas import tpu as pltpu
from jax.sharding import PartitionSpec as P

HEAD_DIM = 128
BLOCK = 128
FAR = -1e30
TO_LOG2 = math.log2(math.e) / math.sqrt(HEAD_DIM)
VMEM_LIMIT = 48 * 1024 * 1024
STAT_ROWS = 32


def begin_of(pos, starts):
    begin = jnp.zeros_like(pos)
    for start in starts:
        begin = jnp.where(pos >= start, start, begin)
    return begin


def compiler_params():
    return pltpu.CompilerParams(vmem_limit_bytes=VMEM_LIMIT)


def rounded_product(key, value):
    return (key.astype(jnp.float32) * value.astype(jnp.float32)).astype(jnp.bfloat16)


def halo_kernel(hk, hv, out):
    out[...] = rounded_product(hk[...], hv[...])


def halo_product(hk, hv):
    rows, channels = hk.shape
    width = min(channels, 512)
    last = pl.BlockSpec((BLOCK, width), lambda j: (rows // BLOCK - 1, j))
    return pl.pallas_call(
        halo_kernel,
        grid=(channels // width,),
        in_specs=[last, last],
        out_specs=pl.BlockSpec((BLOCK, width), lambda j: (0, j)),
        out_shape=jax.ShapeDtypeStruct((BLOCK, channels), jnp.bfloat16),
        compiler_params=compiler_params(),
        cost_estimate=pl.CostEstimate(
            flops=BLOCK * channels, bytes_accessed=6 * BLOCK * channels, transcendentals=0
        ),
        name="halo_product",
    )(hk, hv)


def hyena_kernel(genomes, group, info, hq, hk, hv, halo, filters, gain, out, lines, ext, tall):
    rows, width = out.shape
    blocks = rows // BLOCK
    groups = width // group
    starts = [info[i] for i in range(genomes)]
    step = pl.program_id(0)
    first = lax.axis_index("ctx") * rows

    @pl.when(step == 0)
    def _():
        tap = lax.broadcasted_iota(jnp.int32, (BLOCK, BLOCK), 0)
        col = lax.broadcasted_iota(jnp.int32, (BLOCK, BLOCK), 1)
        turn = jnp.where((tap + col) % BLOCK == 0, 1.0, 0.0).astype(jnp.bfloat16)
        lines[...] = jnp.dot(filters[...], turn, preferred_element_type=jnp.float32)

    ext[:BLOCK] = halo[...]
    ext[BLOCK:] = rounded_product(hk[...], hv[...])
    ours = lines[pl.ds(pl.multiple_of(step * groups, groups), groups), :]
    row = lax.broadcasted_iota(jnp.int32, (BLOCK, BLOCK), 0)
    col = lax.broadcasted_iota(jnp.int32, (BLOCK, BLOCK), 1)
    before = jnp.where(col > row, 1.0, 0.0).astype(jnp.bfloat16)
    within = jnp.where(col <= row, 1.0, 0.0).astype(jnp.bfloat16)
    for g in range(groups):
        line = jnp.broadcast_to(ours[g : g + 1, :], (BLOCK, BLOCK))
        circulant = pltpu.roll(line, 0, 1, stride=1, stride_axis=0).astype(jnp.bfloat16)
        at = slice(g * BLOCK, (g + 1) * BLOCK)
        tall[at, :BLOCK] = circulant * before
        tall[at, BLOCK:] = circulant * within
    lane_group = lax.broadcasted_iota(jnp.int32, (BLOCK, width), 1) // group

    def finish(b, parts):
        filtered = parts[0]
        for g in range(1, groups):
            filtered = jnp.where(lane_group == g, parts[g], filtered)
        at = pl.ds(b * BLOCK, BLOCK)
        direct = ext[(b + 1) * BLOCK : (b + 2) * BLOCK, :].astype(jnp.float32)
        mix = hq[at, :].astype(jnp.float32) * (filtered + gain[...] * direct)
        out[at, :] = mix.astype(jnp.bfloat16)

    for b in range(blocks):
        here = first + b * BLOCK
        window = ext[b * BLOCK : (b + 2) * BLOCK, :]
        cut = begin_of(here + BLOCK - 1, starts) > here - BLOCK

        @pl.when(jnp.logical_not(cut))
        def _():
            finish(
                b,
                [
                    jnp.dot(
                        tall[g * BLOCK : (g + 1) * BLOCK, :],
                        window,
                        preferred_element_type=jnp.float32,
                    )
                    for g in range(groups)
                ],
            )

        @pl.when(cut)
        def _():
            row = here + lax.broadcasted_iota(jnp.int32, (BLOCK, 2 * BLOCK), 0)
            col = here - BLOCK + lax.broadcasted_iota(jnp.int32, (BLOCK, 2 * BLOCK), 1)
            seen = jnp.where(col >= begin_of(row, starts), 1.0, 0.0).astype(jnp.bfloat16)
            finish(
                b,
                [
                    jnp.dot(
                        tall[g * BLOCK : (g + 1) * BLOCK, :] * seen,
                        window,
                        preferred_element_type=jnp.float32,
                    )
                    for g in range(groups)
                ],
            )


def hyena(starts, hq, hk, hv, halo, filters, gain):
    rows, channels = hk.shape
    group = channels // filters.shape[0]
    here = lambda r: pl.BlockSpec((r, BLOCK), lambda j: (0, j))
    return pl.pallas_call(
        partial(hyena_kernel, starts.shape[0], group),
        grid=(channels // BLOCK,),
        in_specs=[
            pl.BlockSpec(memory_space=pltpu.SMEM),
            here(rows),
            here(rows),
            here(rows),
            here(BLOCK),
            pl.BlockSpec(filters.shape, lambda j: (0, 0)),
            here(1),
        ],
        out_specs=here(rows),
        out_shape=jax.ShapeDtypeStruct((rows, channels), jnp.bfloat16),
        scratch_shapes=[
            pltpu.VMEM((filters.shape[0], BLOCK), jnp.float32),
            pltpu.VMEM((rows + BLOCK, BLOCK), jnp.bfloat16),
            pltpu.VMEM((BLOCK // group * BLOCK, 2 * BLOCK), jnp.bfloat16),
        ],
        compiler_params=compiler_params(),
        cost_estimate=pl.CostEstimate(
            flops=2 * rows * channels * 2 * BLOCK * 8,
            bytes_accessed=2 * rows * channels * 4,
            transcendentals=0,
        ),
        name="hyena_mix",
    )(starts, hq, hk, hv, halo, filters, gain)


def one_of(flags, me):
    on = me < 0
    for d, flag in enumerate(flags):
        if flag:
            on = on | (me == d)
    return on


def attend_kernel(genomes, plan, info, q, k, v, *rest):
    rows = q.shape[0]
    me = lax.axis_index("ctx")
    own = me * rows
    rest = list(rest)
    turned, wide = rest[-2:]
    jobs = [(rows, q, own, None)]
    if plan.na:
        jobs.append((plan.na, rest.pop(0), own + rows, one_of(plan.a_to, me)))
    if plan.nb:
        jobs.append((plan.nb, rest.pop(0), own + 2 * rows, one_of(plan.b_to, me)))
    rk, rv = (rest.pop(0), rest.pop(0)) if plan.nk else (None, None)
    out, stats = rest.pop(0), rest.pop(0)
    outs = [out] + rest[: len(jobs) - 1]
    starts = [info[i] for i in range(genomes)]

    turned[:, :rows] = k[...].T
    wide[:rows, :HEAD_DIM] = v[...]
    if plan.nk:
        turned[:, rows:] = rk[...].T
        wide[rows:, :HEAD_DIM] = rv[...]
    wide[:, HEAD_DIM:] = jnp.ones((rows + plan.nk, HEAD_DIM), jnp.bfloat16)

    def seen(row_at, count, col_at, columns):
        row = row_at + lax.broadcasted_iota(jnp.int32, (count, columns), 0)
        col = col_at + lax.broadcasted_iota(jnp.int32, (count, columns), 1)
        begin = begin_of(row_at + lax.broadcasted_iota(jnp.int32, (count, 1), 0), starts)
        return (col <= row) & (col >= begin)

    def piece(queries, out, count, row_at, far, put):
        keys = rows + plan.nk if far else rows
        scores = jnp.dot(queries[...], turned[:, :keys], preferred_element_type=jnp.float32)
        visible = seen(row_at, count, own, rows)
        if far:
            other = seen(row_at, count, own - plan.nk, plan.nk)
            visible = jnp.concatenate([visible, other], axis=1)
        scores = jnp.where(visible, scores, FAR)
        top = jnp.max(scores, axis=1, keepdims=True)
        weights = jnp.exp2((scores - top) * TO_LOG2).astype(jnp.bfloat16)
        mixed = jnp.dot(weights, wide[:keys, :], preferred_element_type=jnp.float32)
        total = mixed[:, HEAD_DIM:]
        out[:count, :] = (mixed[:, :HEAD_DIM] / total).astype(jnp.bfloat16)
        put(as_rows(top * TO_LOG2 + jnp.log2(total)))

    for (count, queries, at, on), out in zip(jobs, outs):
        if on is None:
            put = partial(stats.__setitem__, ...)
        else:
            put = partial(carry, out, count)

        begin = begin_of(at, starts)
        on = True if on is None else on & (begin < own + rows)
        near_only = on
        if plan.nk:
            far = on & (begin < own) & one_of(plan.k_to, me)
            near_only = on & jnp.logical_not(far)

            @pl.when(far)
            def _():
                piece(queries, out, count, at, True, put)

        if near_only is True:
            piece(queries, out, count, at, False, put)
        else:

            @pl.when(near_only)
            def _():
                piece(queries, out, count, at, False, put)

        if on is not True:

            @pl.when(jnp.logical_not(on))
            def _():
                out[:count, :] = jnp.zeros((count, HEAD_DIM), jnp.bfloat16)
                put(jnp.full((8, BLOCK), FAR, jnp.float32))


def as_rows(column):
    row = lax.broadcasted_iota(jnp.int32, (BLOCK, BLOCK), 0)
    lane = lax.broadcasted_iota(jnp.int32, (BLOCK, BLOCK), 1)
    rows = [
        jnp.sum(jnp.where(row == lane, column[i : i + BLOCK], 0.0), axis=0, keepdims=True)
        for i in range(0, column.shape[0], BLOCK)
    ]
    return jnp.concatenate(rows + [jnp.zeros_like(rows[0])] * (8 - len(rows)))


def carry(out, count, stat):
    high = stat.astype(jnp.bfloat16).astype(jnp.float32)
    middle = (stat - high).astype(jnp.bfloat16).astype(jnp.float32)
    low = stat - high - middle
    parts = jnp.concatenate([high, middle, low, jnp.zeros_like(low)])
    out[count:, :] = parts.astype(jnp.bfloat16)


def attend(plan, starts, q, k, v, qa, qb, rk, rv, first, heads):
    rows = q.shape[0]
    here = lambda r: pl.BlockSpec((r, HEAD_DIM), lambda h: (0, h))
    whole = lambda r: pl.BlockSpec((r, HEAD_DIM), lambda h: (0, h + first))
    in_specs = [pl.BlockSpec(memory_space=pltpu.SMEM), whole(rows), whole(rows), whole(rows)]
    operands = [starts, q, k, v]
    for x, skip in (qa, qb, rk, rv):
        if x is not None:
            in_specs.append(
                pl.BlockSpec((x.shape[0], HEAD_DIM), partial(lambda skip, h: (0, h + skip), skip))
            )
            operands.append(x)
    out_specs = [here(rows), pl.BlockSpec((8, BLOCK), lambda h: (h, 0))]
    out_shape = [
        jax.ShapeDtypeStruct((rows, heads * HEAD_DIM), jnp.bfloat16),
        jax.ShapeDtypeStruct((heads * 8, BLOCK), jnp.float32),
    ]
    for count in (plan.na, plan.nb):
        if count:
            out_specs.append(here(count + STAT_ROWS))
            out_shape.append(
                jax.ShapeDtypeStruct((count + STAT_ROWS, heads * HEAD_DIM), jnp.bfloat16)
            )
    queries, keys = rows + plan.na + plan.nb, rows + plan.nk
    return pl.pallas_call(
        partial(attend_kernel, starts.shape[0], plan),
        grid=(heads,),
        in_specs=in_specs,
        out_specs=out_specs,
        out_shape=out_shape,
        scratch_shapes=[
            pltpu.VMEM((HEAD_DIM, keys), jnp.bfloat16),
            pltpu.VMEM((keys, 2 * HEAD_DIM), jnp.bfloat16),
        ],
        compiler_params=compiler_params(),
        cost_estimate=pl.CostEstimate(
            flops=4 * heads * queries * keys * HEAD_DIM,
            bytes_accessed=4 * heads * HEAD_DIM * (queries + keys),
            transcendentals=heads * queries * keys,
        ),
        name="attend_parts",
    )(*operands)


def join_kernel(plan, o, s, *rest):
    rest = list(rest)
    me = lax.axis_index("ctx")
    out = rest[-1]
    rows = o.shape[0]
    block = lax.broadcasted_iota(jnp.int32, (8, BLOCK), 0)
    parts, stats = [(o, rows)], [s[...]]
    for count, flags in ((plan.na, plan.a_from), (plan.nb, plan.b_from)):
        if count:
            part = rest.pop(0)
            carried = part[count:, :].astype(jnp.float32)
            stat = carried[:8] + carried[8:16] + carried[16:24]
            on = one_of(flags, me) & (block < count // BLOCK)
            parts.append((part, count))
            stats.append(jnp.where(on, stat, FAR))
    top = stats[0]
    for x in stats[1:]:
        top = jnp.maximum(top, x)
    weights = [jnp.exp2(x - top) for x in stats]
    total = sum(weights)
    weights = [(w / total).T for w in weights]
    for i in range(rows // BLOCK):
        sl = slice(i * BLOCK, (i + 1) * BLOCK)
        mixed = sum(
            w[:, i : i + 1] * part[sl, :].astype(jnp.float32)
            for w, (part, count) in zip(weights, parts)
            if i * BLOCK < count
        )
        out[sl, :] = mixed.astype(jnp.bfloat16)


def join(plan, o, s, others, first, channels, full):
    rows, wide = o.shape
    here = lambda r: pl.BlockSpec((r, HEAD_DIM), lambda h: (0, h))
    operands = [o, s] + others
    in_specs = [here(rows), pl.BlockSpec((8, BLOCK), lambda h: (h, 0))]
    in_specs += [here(x.shape[0]) for x in others]
    aliases = {}
    if full is not None:
        in_specs.append(pl.BlockSpec(memory_space=pl.ANY))
        operands.append(full)
        aliases = {len(operands) - 1: 0}
    return pl.pallas_call(
        partial(join_kernel, plan),
        grid=(wide // HEAD_DIM,),
        in_specs=in_specs,
        out_specs=pl.BlockSpec((rows, HEAD_DIM), lambda h: (0, h + first)),
        out_shape=jax.ShapeDtypeStruct((rows, channels), jnp.bfloat16),
        input_output_aliases=aliases,
        compiler_params=compiler_params(),
        cost_estimate=pl.CostEstimate(
            flops=6 * rows * wide, bytes_accessed=8 * rows * wide, transcendentals=0
        ),
        name="join_parts",
    )(*operands)


class Plan:
    def __init__(self, n, down_1, rows_1, down_2, rows_2, up, rows_up, heads, ahead):
        self.a = [(l + 1, l) for l in down_1]
        self.b = [(d + 2, d) for d in down_2]
        self.k = [(l, l + 1) for l in up]
        self.na = rows_1 if down_1 else 0
        self.nb = rows_2 if down_2 else 0
        self.nk = rows_up if up else 0
        self.heads, self.ahead = heads, ahead
        ends = lambda pairs, side: [int(any(p[side] == d for p in pairs)) for d in range(n)]
        self.a_from, self.a_to = ends(self.a, 0), ends(self.a, 1)
        self.b_from, self.b_to = ends(self.b, 0), ends(self.b, 1)
        self.k_to = ends(self.k, 1)


def after(value, *earlier):
    return lax.optimization_barrier((value, *earlier))[0]


def run_plan(plan, hq, hk, hv, filters, gain, q, k, starts):
    n = lax.axis_size("ctx")
    rows, channels = hk.shape
    send = lambda x, pairs: lax.ppermute(x, "ctx", pairs)
    back = lambda pairs: [(t, s) for s, t in pairs]
    halo = send(halo_product(hk, hv), [(i, i + 1) for i in range(n - 1)])
    mix = hyena(starts, hq, hk, hv, halo, filters, gain)

    def ahead(whole, heads, pairs, waits):
        cols = slice(heads[0] * HEAD_DIM, (heads[0] + heads[1]) * HEAD_DIM)
        return send(after(whole[:, cols], *waits), pairs)

    groups, at = [], 0
    for heads in plan.ahead:
        groups.append((at, heads))
        at += heads
    sent = []
    first, out, waits = 0, None, []
    rv, earlier = None, None
    for heads in plan.heads:
        if len(sent) < len(groups) and first == groups[len(sent)][0]:
            group = groups[len(sent)]
            got = [
                ahead(x, group, pairs, waits) if pairs else None
                for x, pairs in (
                    (q[: plan.na], plan.a),
                    (q[: plan.nb], plan.b),
                    (k[rows - plan.nk :], plan.k),
                )
            ]
            sent.append((group[0], got))
        start, (qa, qb, rk) = sent[-1]
        skip = first - start
        if plan.nk:
            cols = slice(first * HEAD_DIM, (first + heads) * HEAD_DIM)
            rv = send(after(mix[rows - plan.nk :, cols], *waits), plan.k)
        waits = [x for x in (rv, qa, qb, rk, earlier) if x is not None]
        o, s, *parts = attend(
            plan,
            starts,
            q,
            k,
            mix,
            (qa, skip),
            (qb, skip),
            (rk, skip),
            (rv, 0),
            first,
            heads,
        )
        earlier = s
        pairs = [p for p in (plan.a, plan.b) if p]
        others = [send(x, back(p)) for x, p in zip(parts, pairs)]
        out = join(plan, o, s, others, first, channels, out)
        first += heads
    return mix, out


def attend_update(queries, query_pos, query_begin, key_heads, value_heads, key_pos):
    score_scale = 1.0 / math.sqrt(HEAD_DIM)
    scores = (
        jnp.einsum("qhd,khd->hqk", queries, key_heads, preferred_element_type=jnp.float32)
        * score_scale
    )
    visible = (key_pos[None, :] <= query_pos[:, None]) & (key_pos[None, :] >= query_begin[:, None])
    new_max = jnp.max(jnp.where(visible[None], scores, FAR), axis=2)
    weights = jnp.exp(jnp.where(visible[None], scores - new_max[:, :, None], FAR))
    mixed = jnp.einsum(
        "hqk,khd->hqd",
        weights.astype(jnp.bfloat16),
        value_heads,
        preferred_element_type=jnp.float32,
    )
    return mixed / jnp.sum(weights, axis=2)[:, :, None]


def run_gathered(hq, hk, hv, filters, gain, q, k, starts):
    n = lax.axis_size("ctx")
    rows, channels = hk.shape
    heads = channels // HEAD_DIM
    own = (lax.axis_index("ctx") * rows).astype(jnp.int32)
    halo = lax.ppermute(halo_product(hk, hv), "ctx", [(i, i + 1) for i in range(n - 1)])
    mix = hyena(starts, hq, hk, hv, halo, filters, gain)
    keys = lax.all_gather(k, "ctx", axis=0, tiled=True)
    values = lax.all_gather(mix, "ctx", axis=0, tiled=True)
    key_pos = jnp.arange(n * rows, dtype=jnp.int32)
    pos = own + jnp.arange(rows, dtype=jnp.int32)
    mixed = attend_update(
        q.reshape(rows, heads, HEAD_DIM),
        pos,
        begin_of(pos, [starts[i] for i in range(starts.shape[0])]),
        keys.reshape(n * rows, heads, HEAD_DIM),
        values.reshape(n * rows, heads, HEAD_DIM),
        key_pos,
    )
    return mix, mixed.astype(jnp.bfloat16).transpose(1, 0, 2).reshape(rows, channels)


def per_device(hq, hk, hv, filters, skip_gain, q, k, starts):
    rows, channels = hk.shape
    n = lax.axis_size("ctx")
    gain = skip_gain[None, :]
    if n != 4:
        return run_gathered(hq, hk, hv, filters, gain, q, k, starts)
    plan = Plan(n, [1, 2], rows, [1], rows - BLOCK, [0], rows, [4, 4, 4, 4], [8, 8])
    return run_plan(plan, hq, hk, hv, filters, gain, q, k, starts)


def solution(mesh):
    split = P(("rep", "ctx"), ("ch", "sub"))
    return jax.shard_map(
        per_device,
        mesh=mesh,
        in_specs=(
            split,
            split,
            split,
            P(("ch", "sub"), None),
            P(("ch", "sub")),
            split,
            split,
            P("rep"),
        ),
        out_specs=(split, split),
        check_vma=False,
    )
```

```python
from functools import partial
import math

import jax
import jax.numpy as jnp
from jax import lax
from jax.experimental import pallas as pl
from jax.experimental.pallas import tpu as pltpu
from jax.sharding import PartitionSpec as P

HEAD_DIM = 128
BLOCK = 128
FAR = -1e30
TO_LOG2 = math.log2(math.e) / math.sqrt(HEAD_DIM)
VMEM_LIMIT = 48 * 1024 * 1024
HEADS_AT_ONCE = 2
STAT_ROWS = 32


def begin_of(pos, starts):
    begin = jnp.zeros_like(pos)
    for start in starts:
        begin = jnp.where(pos >= start, start, begin)
    return begin


def compiler_params():
    return pltpu.CompilerParams(vmem_limit_bytes=VMEM_LIMIT)


def rounded_product(key, value):
    return (key.astype(jnp.float32) * value.astype(jnp.float32)).astype(jnp.bfloat16)


def halo_kernel(hk, hv, out):
    out[...] = rounded_product(hk[...], hv[...])


def halo_product(hk, hv):
    rows, channels = hk.shape
    width = min(channels, 512)
    last = pl.BlockSpec((BLOCK, width), lambda j: (rows // BLOCK - 1, j))
    return pl.pallas_call(
        halo_kernel,
        grid=(channels // width,),
        in_specs=[last, last],
        out_specs=pl.BlockSpec((BLOCK, width), lambda j: (0, j)),
        out_shape=jax.ShapeDtypeStruct((BLOCK, channels), jnp.bfloat16),
        compiler_params=compiler_params(),
        cost_estimate=pl.CostEstimate(
            flops=BLOCK * channels, bytes_accessed=6 * BLOCK * channels, transcendentals=0
        ),
        name="halo_product",
    )(hk, hv)


def hyena_kernel(genomes, group, info, hq, hk, hv, halo, filters, gain, out, lines, ext, mask):
    rows, width = out.shape
    blocks = rows // BLOCK
    groups = BLOCK // group
    tiles = width // BLOCK
    starts = [info[i] for i in range(genomes)]
    step = pl.program_id(0)
    first = lax.axis_index("ctx") * rows
    row = lax.broadcasted_iota(jnp.int32, (BLOCK, BLOCK), 0)
    col = lax.broadcasted_iota(jnp.int32, (BLOCK, BLOCK), 1)

    @pl.when(step == 0)
    def _():
        turn = jnp.where((row + col) % BLOCK == 0, 1.0, 0.0).astype(jnp.bfloat16)
        lines[...] = jnp.dot(filters[...], turn, preferred_element_type=jnp.float32)
        for b in range(blocks):
            here = first + b * BLOCK
            begin = begin_of(here + row, starts)
            before = (col > row) & (here - BLOCK + col >= begin)
            within = (col <= row) & (here + col >= begin)
            mask[b, :, :BLOCK] = jnp.where(before, 1.0, 0.0).astype(jnp.bfloat16)
            mask[b, :, BLOCK:] = jnp.where(within, 1.0, 0.0).astype(jnp.bfloat16)

    ext[:BLOCK, :] = halo[...]
    ext[BLOCK:, :] = rounded_product(hk[...], hv[...])
    ours = lines[pl.ds(pl.multiple_of(step * groups * tiles, groups * tiles), groups * tiles), :]
    lane_group = col // group
    for t in range(tiles):
        lanes = slice(t * BLOCK, (t + 1) * BLOCK)
        turned = []
        for g in range(groups):
            line = jnp.broadcast_to(ours[t * groups + g, :][None, :], (BLOCK, BLOCK))
            turned.append(pltpu.roll(line, 0, 1, stride=1, stride_axis=0).astype(jnp.bfloat16))
        for b in range(blocks):
            tall = jnp.concatenate(
                [
                    jnp.concatenate([one * mask[b, :, :BLOCK], one * mask[b, :, BLOCK:]], axis=1)
                    for one in turned
                ],
                axis=0,
            )
            window = ext[b * BLOCK : (b + 2) * BLOCK, lanes]
            every = jnp.dot(tall, window, preferred_element_type=jnp.float32)
            filtered = every[:BLOCK]
            for g in range(1, groups):
                filtered = jnp.where(
                    lane_group == g, every[g * BLOCK : (g + 1) * BLOCK], filtered
                )
            at = slice(b * BLOCK, (b + 1) * BLOCK)
            direct = ext[(b + 1) * BLOCK : (b + 2) * BLOCK, lanes].astype(jnp.float32)
            mix = hq[at, lanes].astype(jnp.float32) * (filtered + gain[:, lanes] * direct)
            out[at, lanes] = mix.astype(jnp.bfloat16)


def hyena(starts, hq, hk, hv, halo, filters, gain):
    rows, channels = hk.shape
    group = channels // filters.shape[0]
    width = 2 * BLOCK
    here = lambda r: pl.BlockSpec((r, width), lambda j: (0, j))
    return pl.pallas_call(
        partial(hyena_kernel, starts.shape[0], group),
        grid=(channels // width,),
        in_specs=[
            pl.BlockSpec(memory_space=pltpu.SMEM),
            here(rows),
            here(rows),
            here(rows),
            here(BLOCK),
            pl.BlockSpec(filters.shape, lambda j: (0, 0)),
            here(1),
        ],
        out_specs=here(rows),
        out_shape=jax.ShapeDtypeStruct((rows, channels), jnp.bfloat16),
        scratch_shapes=[
            pltpu.VMEM((filters.shape[0], BLOCK), jnp.float32),
            pltpu.VMEM((rows + BLOCK, width), jnp.bfloat16),
            pltpu.VMEM((rows // BLOCK, BLOCK, 2 * BLOCK), jnp.bfloat16),
        ],
        compiler_params=compiler_params(),
        cost_estimate=pl.CostEstimate(
            flops=2 * rows * channels * 2 * BLOCK * 8,
            bytes_accessed=2 * rows * channels * 4,
            transcendentals=0,
        ),
        name="hyena_mix",
    )(starts, hq, hk, hv, halo, filters, gain)


def one_of(flags, me):
    on = me < 0
    for d, flag in enumerate(flags):
        if flag:
            on = on | (me == d)
    return on


def attend_kernel(genomes, plan, info, q, k, v, *rest):
    rows = q.shape[0]
    me = lax.axis_index("ctx")
    own = me * rows
    rest = list(rest)
    jobs = [(rows, q, own, None)]
    if plan.na:
        jobs.append((plan.na, rest.pop(0), own + rows, one_of(plan.a_to, me)))
    if plan.nb:
        jobs.append((plan.nb, rest.pop(0), own + 2 * rows, one_of(plan.b_to, me)))
    rk, rv = (rest.pop(0), rest.pop(0)) if plan.nk else (None, None)
    out, stats = rest.pop(0), rest.pop(0)
    outs = [out] + rest[: len(jobs) - 1]
    starts = [info[i] for i in range(genomes)]

    def seen(row_at, count, col_at, columns):
        row = row_at + lax.broadcasted_iota(jnp.int32, (count, columns), 0)
        col = col_at + lax.broadcasted_iota(jnp.int32, (count, columns), 1)
        begin = begin_of(row_at + lax.broadcasted_iota(jnp.int32, (count, 1), 0), starts)
        return (col <= row) & (col >= begin)

    def piece(queries, out, count, row_at, far, put):
        sets = [(k, v, seen(row_at, count, own, rows))]
        if far:
            sets.append((rk, rv, seen(row_at, count, own - plan.nk, plan.nk)))
        for h in range(q.shape[1] // HEAD_DIM):
            lanes = slice(h * HEAD_DIM, (h + 1) * HEAD_DIM)
            scores = [
                jnp.where(
                    visible,
                    lax.dot_general(
                        queries[:, lanes],
                        keys[:, lanes],
                        (((1,), (1,)), ((), ())),
                        preferred_element_type=jnp.float32,
                    ),
                    FAR,
                )
                for keys, _, visible in sets
            ]
            top = jnp.max(scores[0], axis=1, keepdims=True)
            for one in scores[1:]:
                top = jnp.maximum(top, jnp.max(one, axis=1, keepdims=True))
            mixed = 0.0
            for one, (_, values, _) in zip(scores, sets):
                weights = jnp.exp2((one - top) * TO_LOG2).astype(jnp.bfloat16)
                wide = [values[:, lanes], jnp.ones((values.shape[0], HEAD_DIM), jnp.bfloat16)]
                mixed = mixed + jnp.dot(
                    weights, jnp.concatenate(wide, axis=1), preferred_element_type=jnp.float32
                )
            total = mixed[:, HEAD_DIM:]
            out[:count, lanes] = (mixed[:, :HEAD_DIM] / total).astype(jnp.bfloat16)
            put(h, as_rows(top * TO_LOG2 + jnp.log2(total)))

    for (count, queries, at, on), out in zip(jobs, outs):
        put = partial(keep, stats) if on is None else partial(carry, out, count)

        begin = begin_of(at, starts)
        on = True if on is None else on & (begin < own + rows)
        near_only = on
        if plan.nk:
            far = on & (begin < own) & one_of(plan.k_to, me)
            near_only = on & jnp.logical_not(far)

            @pl.when(far)
            def _():
                piece(queries, out, count, at, True, put)

        if near_only is True:
            piece(queries, out, count, at, False, put)
        else:

            @pl.when(near_only)
            def _():
                piece(queries, out, count, at, False, put)

        if on is not True:

            @pl.when(jnp.logical_not(on))
            def _():
                out[:count, :] = jnp.zeros((count, out.shape[1]), jnp.bfloat16)
                for h in range(out.shape[1] // HEAD_DIM):
                    put(h, jnp.full((8, BLOCK), FAR, jnp.float32))


def as_rows(column):
    row = lax.broadcasted_iota(jnp.int32, (BLOCK, BLOCK), 0)
    lane = lax.broadcasted_iota(jnp.int32, (BLOCK, BLOCK), 1)
    rows = [
        jnp.sum(jnp.where(row == lane, column[i : i + BLOCK], 0.0), axis=0, keepdims=True)
        for i in range(0, column.shape[0], BLOCK)
    ]
    return jnp.concatenate(rows + [jnp.zeros_like(rows[0])] * (8 - len(rows)))


def keep(out, h, stat):
    out[h * 8 : (h + 1) * 8, :] = stat


def carry(out, count, h, stat):
    high = stat.astype(jnp.bfloat16).astype(jnp.float32)
    middle = (stat - high).astype(jnp.bfloat16).astype(jnp.float32)
    low = stat - high - middle
    parts = jnp.concatenate([high, middle, low, jnp.zeros_like(low)])
    out[count:, h * HEAD_DIM : (h + 1) * HEAD_DIM] = parts.astype(jnp.bfloat16)


def attend(plan, starts, q, k, v, qa, qb, rk, rv, first, heads):
    rows = q.shape[0]
    width = HEADS_AT_ONCE * HEAD_DIM
    here = lambda r: pl.BlockSpec((r, width), lambda h: (0, h))
    later = lambda r, skip: pl.BlockSpec((r, width), lambda h: (0, h + skip // HEADS_AT_ONCE))
    whole = lambda r: later(r, first)
    in_specs = [pl.BlockSpec(memory_space=pltpu.SMEM), whole(rows), whole(rows), whole(rows)]
    operands = [starts, q, k, v]
    for x, skip in (qa, qb, rk, rv):
        if x is not None:
            in_specs.append(later(x.shape[0], skip))
            operands.append(x)
    out_specs = [here(rows), pl.BlockSpec((HEADS_AT_ONCE * 8, BLOCK), lambda h: (h, 0))]
    out_shape = [
        jax.ShapeDtypeStruct((rows, heads * HEAD_DIM), jnp.bfloat16),
        jax.ShapeDtypeStruct((heads * 8, BLOCK), jnp.float32),
    ]
    for count in (plan.na, plan.nb):
        if count:
            out_specs.append(here(count + STAT_ROWS))
            out_shape.append(
                jax.ShapeDtypeStruct((count + STAT_ROWS, heads * HEAD_DIM), jnp.bfloat16)
            )
    queries, keys = rows + plan.na + plan.nb, rows + plan.nk
    return pl.pallas_call(
        partial(attend_kernel, starts.shape[0], plan),
        grid=(heads // HEADS_AT_ONCE,),
        in_specs=in_specs,
        out_specs=out_specs,
        out_shape=out_shape,
        compiler_params=compiler_params(),
        cost_estimate=pl.CostEstimate(
            flops=4 * heads * queries * keys * HEAD_DIM,
            bytes_accessed=4 * heads * HEAD_DIM * (queries + keys),
            transcendentals=heads * queries * keys,
        ),
        name="attend_parts",
    )(*operands)


def join_kernel(plan, o, s, *rest):
    rest = list(rest)
    me = lax.axis_index("ctx")
    out = rest[-1]
    rows = o.shape[0]
    block = lax.broadcasted_iota(jnp.int32, (8, BLOCK), 0)
    parts = [(o, rows, None)]
    for count, flags in ((plan.na, plan.a_from), (plan.nb, plan.b_from)):
        if count:
            parts.append((rest.pop(0), count, one_of(flags, me) & (block < count // BLOCK)))
    for h in range(o.shape[1] // HEAD_DIM):
        lanes = slice(h * HEAD_DIM, (h + 1) * HEAD_DIM)
        stats = [s[h * 8 : (h + 1) * 8, :]]
        for part, count, on in parts[1:]:
            carried = part[count:, lanes].astype(jnp.float32)
            stats.append(jnp.where(on, carried[:8] + carried[8:16] + carried[16:24], FAR))
        top = stats[0]
        for x in stats[1:]:
            top = jnp.maximum(top, x)
        weights = [jnp.exp2(x - top) for x in stats]
        total = sum(weights)
        weights = [(w / total).T for w in weights]
        for i in range(rows // BLOCK):
            sl = slice(i * BLOCK, (i + 1) * BLOCK)
            mixed = sum(
                w[:, i : i + 1] * part[sl, lanes].astype(jnp.float32)
                for w, (part, count, _) in zip(weights, parts)
                if i * BLOCK < count
            )
            out[sl, lanes] = mixed.astype(jnp.bfloat16)


def join(plan, o, s, others, first, channels, full):
    rows, wide = o.shape
    width = HEADS_AT_ONCE * HEAD_DIM
    skip = first // HEADS_AT_ONCE
    here = lambda r: pl.BlockSpec((r, width), lambda h: (0, h))
    operands = [o, s] + others
    in_specs = [here(rows), pl.BlockSpec((HEADS_AT_ONCE * 8, BLOCK), lambda h: (h, 0))]
    in_specs += [here(x.shape[0]) for x in others]
    aliases = {}
    if full is not None:
        in_specs.append(pl.BlockSpec(memory_space=pl.ANY))
        operands.append(full)
        aliases = {len(operands) - 1: 0}
    return pl.pallas_call(
        partial(join_kernel, plan),
        grid=(wide // width,),
        in_specs=in_specs,
        out_specs=pl.BlockSpec((rows, width), lambda h: (0, h + skip)),
        out_shape=jax.ShapeDtypeStruct((rows, channels), jnp.bfloat16),
        input_output_aliases=aliases,
        compiler_params=compiler_params(),
        cost_estimate=pl.CostEstimate(
            flops=6 * rows * wide, bytes_accessed=8 * rows * wide, transcendentals=0
        ),
        name="join_parts",
    )(*operands)


class Plan:
    def __init__(self, n, down_1, rows_1, down_2, rows_2, up, rows_up, heads, ahead):
        self.a = [(l + 1, l) for l in down_1]
        self.b = [(d + 2, d) for d in down_2]
        self.k = [(l, l + 1) for l in up]
        self.na = rows_1 if down_1 else 0
        self.nb = rows_2 if down_2 else 0
        self.nk = rows_up if up else 0
        self.heads, self.ahead = heads, ahead
        ends = lambda pairs, side: [int(any(p[side] == d for p in pairs)) for d in range(n)]
        self.a_from, self.a_to = ends(self.a, 0), ends(self.a, 1)
        self.b_from, self.b_to = ends(self.b, 0), ends(self.b, 1)
        self.k_to = ends(self.k, 1)


def after(value, *earlier):
    return lax.optimization_barrier((value, *earlier))[0]


def run_plan(plan, hq, hk, hv, filters, gain, q, k, starts):
    n = lax.axis_size("ctx")
    rows, channels = hk.shape
    send = lambda x, pairs: lax.ppermute(x, "ctx", pairs)
    back = lambda pairs: [(t, s) for s, t in pairs]
    halo = send(halo_product(hk, hv), [(i, i + 1) for i in range(n - 1)])
    mix = hyena(starts, hq, hk, hv, halo, filters, gain)

    def ahead(whole, heads, pairs, waits):
        cols = slice(heads[0] * HEAD_DIM, (heads[0] + heads[1]) * HEAD_DIM)
        return send(after(whole[:, cols], *waits), pairs)

    groups, at = [], 0
    for heads in plan.ahead:
        groups.append((at, heads))
        at += heads
    sent = []
    first, out, waits = 0, None, []
    rv, earlier, came_back = None, None, []
    for heads in plan.heads:
        if len(sent) < len(groups) and first == groups[len(sent)][0]:
            group = groups[len(sent)]
            got = [
                ahead(x, group, pairs, waits) if pairs else None
                for x, pairs in (
                    (q[: plan.na], plan.a),
                    (q[: plan.nb], plan.b),
                    (k[rows - plan.nk :], plan.k),
                )
            ]
            sent.append((group[0], got))
        start, (qa, qb, rk) = sent[-1]
        skip = first - start
        if plan.nk:
            cols = slice(first * HEAD_DIM, (first + heads) * HEAD_DIM)
            rv = send(after(mix[rows - plan.nk :, cols], *waits), plan.k)
        waits = [x for x in (rv, qa, qb, rk, earlier) if x is not None]
        o, s, *parts = attend(
            plan,
            after(starts, *(came_back[-2] if len(came_back) > 1 else [])),
            q,
            k,
            mix,
            (qa, skip),
            (qb, skip),
            (rk, skip),
            (rv, 0),
            first,
            heads,
        )
        earlier = s
        pairs = [p for p in (plan.a, plan.b) if p]
        others = [send(x, back(p)) for x, p in zip(parts, pairs)]
        came_back.append(others)
        out = join(plan, o, s, others, first, channels, out)
        first += heads
    return mix, out


def attend_update(queries, query_pos, query_begin, key_heads, value_heads, key_pos):
    score_scale = 1.0 / math.sqrt(HEAD_DIM)
    scores = (
        jnp.einsum("qhd,khd->hqk", queries, key_heads, preferred_element_type=jnp.float32)
        * score_scale
    )
    visible = (key_pos[None, :] <= query_pos[:, None]) & (key_pos[None, :] >= query_begin[:, None])
    new_max = jnp.max(jnp.where(visible[None], scores, FAR), axis=2)
    weights = jnp.exp(jnp.where(visible[None], scores - new_max[:, :, None], FAR))
    mixed = jnp.einsum(
        "hqk,khd->hqd",
        weights.astype(jnp.bfloat16),
        value_heads,
        preferred_element_type=jnp.float32,
    )
    return mixed / jnp.sum(weights, axis=2)[:, :, None]


def run_gathered(hq, hk, hv, filters, gain, q, k, starts):
    n = lax.axis_size("ctx")
    rows, channels = hk.shape
    heads = channels // HEAD_DIM
    own = (lax.axis_index("ctx") * rows).astype(jnp.int32)
    halo = lax.ppermute(halo_product(hk, hv), "ctx", [(i, i + 1) for i in range(n - 1)])
    mix = hyena(starts, hq, hk, hv, halo, filters, gain)
    keys = lax.all_gather(k, "ctx", axis=0, tiled=True)
    values = lax.all_gather(mix, "ctx", axis=0, tiled=True)
    key_pos = jnp.arange(n * rows, dtype=jnp.int32)
    pos = own + jnp.arange(rows, dtype=jnp.int32)
    mixed = attend_update(
        q.reshape(rows, heads, HEAD_DIM),
        pos,
        begin_of(pos, [starts[i] for i in range(starts.shape[0])]),
        keys.reshape(n * rows, heads, HEAD_DIM),
        values.reshape(n * rows, heads, HEAD_DIM),
        key_pos,
    )
    return mix, mixed.astype(jnp.bfloat16).transpose(1, 0, 2).reshape(rows, channels)


def per_device(hq, hk, hv, filters, skip_gain, q, k, starts):
    rows, channels = hk.shape
    n = lax.axis_size("ctx")
    gain = skip_gain[None, :]
    if n != 4:
        return run_gathered(hq, hk, hv, filters, gain, q, k, starts)
    plan = Plan(n, [1, 2], rows, [1], rows - BLOCK, [0], rows, [4, 4, 4, 4], [8, 8])
    return run_plan(plan, hq, hk, hv, filters, gain, q, k, starts)


def solution(mesh):
    split = P(("rep", "ctx"), ("ch", "sub"))
    return jax.shard_map(
        per_device,
        mesh=mesh,
        in_specs=(
            split,
            split,
            split,
            P(("ch", "sub"), None),
            P(("ch", "sub")),
            split,
            split,
            P("rep"),
        ),
        out_specs=(split, split),
        check_vma=False,
    )
```

```python
from functools import partial
import math

import jax
import jax.numpy as jnp
from jax import lax
from jax.experimental import pallas as pl
from jax.experimental.pallas import tpu as pltpu
from jax.sharding import PartitionSpec as P

HEAD_DIM = 128
BLOCK = 128
FAR = -1e30
TO_LOG2 = math.log2(math.e) / math.sqrt(HEAD_DIM)
VMEM_LIMIT = 48 * 1024 * 1024
HEADS_AT_ONCE = 2
SMALL = pl.CostEstimate(flops=1024, bytes_accessed=1024, transcendentals=0)
STAT_ROWS = 32


def begin_of(pos, starts):
    begin = jnp.zeros_like(pos)
    for start in starts:
        begin = jnp.where(pos >= start, start, begin)
    return begin


def compiler_params():
    return pltpu.CompilerParams(vmem_limit_bytes=VMEM_LIMIT)


def rounded_product(key, value):
    return (key.astype(jnp.float32) * value.astype(jnp.float32)).astype(jnp.bfloat16)


def halo_kernel(hk, hv, out):
    out[...] = rounded_product(hk[...], hv[...])


def halo_product(hk, hv):
    rows, channels = hk.shape
    width = min(channels, 512)
    last = pl.BlockSpec((BLOCK, width), lambda j: (rows // BLOCK - 1, j))
    return pl.pallas_call(
        halo_kernel,
        grid=(channels // width,),
        in_specs=[last, last],
        out_specs=pl.BlockSpec((BLOCK, width), lambda j: (0, j)),
        out_shape=jax.ShapeDtypeStruct((BLOCK, channels), jnp.bfloat16),
        compiler_params=compiler_params(),
        cost_estimate=SMALL,
        name="halo_product",
    )(hk, hv)


def hyena_kernel(genomes, group, info, hq, hk, hv, halo, filters, gain, out, lines, ext, mask):
    rows, width = out.shape
    blocks = rows // BLOCK
    groups = BLOCK // group
    tiles = width // BLOCK
    starts = [info[i] for i in range(genomes)]
    step = pl.program_id(0)
    first = lax.axis_index("ctx") * rows
    row = lax.broadcasted_iota(jnp.int32, (BLOCK, BLOCK), 0)
    col = lax.broadcasted_iota(jnp.int32, (BLOCK, BLOCK), 1)

    @pl.when(step == 0)
    def _():
        turn = jnp.where((row + col) % BLOCK == 0, 1.0, 0.0).astype(jnp.bfloat16)
        lines[...] = jnp.dot(filters[...], turn, preferred_element_type=jnp.float32)
        for b in range(blocks):
            here = first + b * BLOCK
            begin = begin_of(here + row, starts)
            before = (col > row) & (here - BLOCK + col >= begin)
            within = (col <= row) & (here + col >= begin)
            mask[b, :, :BLOCK] = jnp.where(before, 1.0, 0.0).astype(jnp.bfloat16)
            mask[b, :, BLOCK:] = jnp.where(within, 1.0, 0.0).astype(jnp.bfloat16)

    ext[:BLOCK, :] = halo[...]
    ext[BLOCK:, :] = rounded_product(hk[...], hv[...])
    ours = lines[pl.ds(pl.multiple_of(step * groups * tiles, groups * tiles), groups * tiles), :]
    lane_group = col // group
    for t in range(tiles):
        lanes = slice(t * BLOCK, (t + 1) * BLOCK)
        turned = []
        for g in range(groups):
            line = jnp.broadcast_to(ours[t * groups + g, :][None, :], (BLOCK, BLOCK))
            turned.append(pltpu.roll(line, 0, 1, stride=1, stride_axis=0).astype(jnp.bfloat16))
        for b in range(blocks):
            tall = jnp.concatenate(
                [
                    jnp.concatenate([one * mask[b, :, :BLOCK], one * mask[b, :, BLOCK:]], axis=1)
                    for one in turned
                ],
                axis=0,
            )
            window = ext[b * BLOCK : (b + 2) * BLOCK, lanes]
            every = jnp.dot(tall, window, preferred_element_type=jnp.float32)
            filtered = every[:BLOCK]
            for g in range(1, groups):
                filtered = jnp.where(
                    lane_group == g, every[g * BLOCK : (g + 1) * BLOCK], filtered
                )
            at = slice(b * BLOCK, (b + 1) * BLOCK)
            direct = ext[(b + 1) * BLOCK : (b + 2) * BLOCK, lanes].astype(jnp.float32)
            mix = hq[at, lanes].astype(jnp.float32) * (filtered + gain[:, lanes] * direct)
            out[at, lanes] = mix.astype(jnp.bfloat16)


def hyena(starts, hq, hk, hv, halo, filters, gain):
    rows, channels = hk.shape
    group = channels // filters.shape[0]
    width = 2 * BLOCK
    here = lambda r: pl.BlockSpec((r, width), lambda j: (0, j))
    return pl.pallas_call(
        partial(hyena_kernel, starts.shape[0], group),
        grid=(channels // width,),
        in_specs=[
            pl.BlockSpec(memory_space=pltpu.SMEM),
            here(rows),
            here(rows),
            here(rows),
            here(BLOCK),
            pl.BlockSpec(filters.shape, lambda j: (0, 0)),
            here(1),
        ],
        out_specs=here(rows),
        out_shape=jax.ShapeDtypeStruct((rows, channels), jnp.bfloat16),
        scratch_shapes=[
            pltpu.VMEM((filters.shape[0], BLOCK), jnp.float32),
            pltpu.VMEM((rows + BLOCK, width), jnp.bfloat16),
            pltpu.VMEM((rows // BLOCK, BLOCK, 2 * BLOCK), jnp.bfloat16),
        ],
        compiler_params=compiler_params(),
        cost_estimate=SMALL,
        name="hyena_mix",
    )(starts, hq, hk, hv, halo, filters, gain)


def one_of(flags, me):
    on = me < 0
    for d, flag in enumerate(flags):
        if flag:
            on = on | (me == d)
    return on


def attend_kernel(genomes, plan, info, q, k, v, *rest):
    rows = q.shape[0]
    me = lax.axis_index("ctx")
    own = me * rows
    rest = list(rest)
    jobs = [(rows, q, own, None)]
    if plan.na:
        jobs.append((plan.na, rest.pop(0), own + rows, one_of(plan.a_to, me)))
    if plan.nb:
        jobs.append((plan.nb, rest.pop(0), own + 2 * rows, one_of(plan.b_to, me)))
    rk, rv = (rest.pop(0), rest.pop(0)) if plan.nk else (None, None)
    out, stats = rest.pop(0), rest.pop(0)
    outs = [out] + rest[: len(jobs) - 1]
    starts = [info[i] for i in range(genomes)]

    def seen(row_at, count, col_at, columns):
        row = row_at + lax.broadcasted_iota(jnp.int32, (count, columns), 0)
        col = col_at + lax.broadcasted_iota(jnp.int32, (count, columns), 1)
        begin = begin_of(row_at + lax.broadcasted_iota(jnp.int32, (count, 1), 0), starts)
        return (col <= row) & (col >= begin)

    def piece(queries, out, count, row_at, far, put):
        sets = [(k, v, seen(row_at, count, own, rows))]
        if far:
            sets.append((rk, rv, seen(row_at, count, own - plan.nk, plan.nk)))
        for h in range(q.shape[1] // HEAD_DIM):
            lanes = slice(h * HEAD_DIM, (h + 1) * HEAD_DIM)
            scores = [
                jnp.where(
                    visible,
                    lax.dot_general(
                        queries[:, lanes],
                        keys[:, lanes],
                        (((1,), (1,)), ((), ())),
                        preferred_element_type=jnp.float32,
                    ),
                    FAR,
                )
                for keys, _, visible in sets
            ]
            top = jnp.max(scores[0], axis=1, keepdims=True)
            for one in scores[1:]:
                top = jnp.maximum(top, jnp.max(one, axis=1, keepdims=True))
            mixed = 0.0
            for one, (_, values, _) in zip(scores, sets):
                weights = jnp.exp2((one - top) * TO_LOG2).astype(jnp.bfloat16)
                wide = [values[:, lanes], jnp.ones((values.shape[0], HEAD_DIM), jnp.bfloat16)]
                mixed = mixed + jnp.dot(
                    weights, jnp.concatenate(wide, axis=1), preferred_element_type=jnp.float32
                )
            total = mixed[:, HEAD_DIM:]
            out[:count, lanes] = (mixed[:, :HEAD_DIM] / total).astype(jnp.bfloat16)
            put(h, as_rows(top * TO_LOG2 + jnp.log2(total)))

    for (count, queries, at, on), out in zip(jobs, outs):
        put = partial(keep, stats) if on is None else partial(carry, out, count)

        begin = begin_of(at, starts)
        on = True if on is None else on & (begin < own + rows)
        near_only = on
        if plan.nk:
            far = on & (begin < own) & one_of(plan.k_to, me)
            near_only = on & jnp.logical_not(far)

            @pl.when(far)
            def _():
                piece(queries, out, count, at, True, put)

        if near_only is True:
            piece(queries, out, count, at, False, put)
        else:

            @pl.when(near_only)
            def _():
                piece(queries, out, count, at, False, put)

        if on is not True:

            @pl.when(jnp.logical_not(on))
            def _():
                out[:count, :] = jnp.zeros((count, out.shape[1]), jnp.bfloat16)
                for h in range(out.shape[1] // HEAD_DIM):
                    put(h, jnp.full((8, BLOCK), FAR, jnp.float32))


def as_rows(column):
    row = lax.broadcasted_iota(jnp.int32, (BLOCK, BLOCK), 0)
    lane = lax.broadcasted_iota(jnp.int32, (BLOCK, BLOCK), 1)
    rows = [
        jnp.sum(jnp.where(row == lane, column[i : i + BLOCK], 0.0), axis=0, keepdims=True)
        for i in range(0, column.shape[0], BLOCK)
    ]
    return jnp.concatenate(rows + [jnp.zeros_like(rows[0])] * (8 - len(rows)))


def keep(out, h, stat):
    out[h * 8 : (h + 1) * 8, :] = stat


def carry(out, count, h, stat):
    high = stat.astype(jnp.bfloat16).astype(jnp.float32)
    middle = (stat - high).astype(jnp.bfloat16).astype(jnp.float32)
    low = stat - high - middle
    parts = jnp.concatenate([high, middle, low, jnp.zeros_like(low)])
    out[count:, h * HEAD_DIM : (h + 1) * HEAD_DIM] = parts.astype(jnp.bfloat16)


def attend(plan, starts, q, k, v, qa, qb, rk, rv, first, heads):
    rows = q.shape[0]
    width = HEADS_AT_ONCE * HEAD_DIM
    here = lambda r: pl.BlockSpec((r, width), lambda h: (0, h))
    later = lambda r, skip: pl.BlockSpec((r, width), lambda h: (0, h + skip // HEADS_AT_ONCE))
    whole = lambda r: later(r, first)
    in_specs = [pl.BlockSpec(memory_space=pltpu.SMEM), whole(rows), whole(rows), whole(rows)]
    operands = [starts, q, k, v]
    for x, skip in (qa, qb, rk, rv):
        if x is not None:
            in_specs.append(later(x.shape[0], skip))
            operands.append(x)
    out_specs = [here(rows), pl.BlockSpec((HEADS_AT_ONCE * 8, BLOCK), lambda h: (h, 0))]
    out_shape = [
        jax.ShapeDtypeStruct((rows, heads * HEAD_DIM), jnp.bfloat16),
        jax.ShapeDtypeStruct((heads * 8, BLOCK), jnp.float32),
    ]
    for count in (plan.na, plan.nb):
        if count:
            out_specs.append(here(count + STAT_ROWS))
            out_shape.append(
                jax.ShapeDtypeStruct((count + STAT_ROWS, heads * HEAD_DIM), jnp.bfloat16)
            )
    queries, keys = rows + plan.na + plan.nb, rows + plan.nk
    return pl.pallas_call(
        partial(attend_kernel, starts.shape[0], plan),
        grid=(heads // HEADS_AT_ONCE,),
        in_specs=in_specs,
        out_specs=out_specs,
        out_shape=out_shape,
        compiler_params=compiler_params(),
        cost_estimate=SMALL,
        name="attend_parts",
    )(*operands)


def join_kernel(plan, o, s, *rest):
    rest = list(rest)
    me = lax.axis_index("ctx")
    out = rest[-1]
    rows = o.shape[0]
    block = lax.broadcasted_iota(jnp.int32, (8, BLOCK), 0)
    parts = [(o, rows, None)]
    for count, flags in ((plan.na, plan.a_from), (plan.nb, plan.b_from)):
        if count:
            parts.append((rest.pop(0), count, one_of(flags, me) & (block < count // BLOCK)))
    for h in range(o.shape[1] // HEAD_DIM):
        lanes = slice(h * HEAD_DIM, (h + 1) * HEAD_DIM)
        stats = [s[h * 8 : (h + 1) * 8, :]]
        for part, count, on in parts[1:]:
            carried = part[count:, lanes].astype(jnp.float32)
            stats.append(jnp.where(on, carried[:8] + carried[8:16] + carried[16:24], FAR))
        top = stats[0]
        for x in stats[1:]:
            top = jnp.maximum(top, x)
        weights = [jnp.exp2(x - top) for x in stats]
        total = sum(weights)
        weights = [(w / total).T for w in weights]
        for i in range(rows // BLOCK):
            sl = slice(i * BLOCK, (i + 1) * BLOCK)
            mixed = sum(
                w[:, i : i + 1] * part[sl, lanes].astype(jnp.float32)
                for w, (part, count, _) in zip(weights, parts)
                if i * BLOCK < count
            )
            out[sl, lanes] = mixed.astype(jnp.bfloat16)


def join(plan, o, s, others, first, channels, full):
    rows, wide = o.shape
    width = HEADS_AT_ONCE * HEAD_DIM
    skip = first // HEADS_AT_ONCE
    here = lambda r: pl.BlockSpec((r, width), lambda h: (0, h))
    operands = [o, s] + others
    in_specs = [here(rows), pl.BlockSpec((HEADS_AT_ONCE * 8, BLOCK), lambda h: (h, 0))]
    in_specs += [here(x.shape[0]) for x in others]
    aliases = {}
    if full is not None:
        in_specs.append(pl.BlockSpec(memory_space=pl.ANY))
        operands.append(full)
        aliases = {len(operands) - 1: 0}
    return pl.pallas_call(
        partial(join_kernel, plan),
        grid=(wide // width,),
        in_specs=in_specs,
        out_specs=pl.BlockSpec((rows, width), lambda h: (0, h + skip)),
        out_shape=jax.ShapeDtypeStruct((rows, channels), jnp.bfloat16),
        input_output_aliases=aliases,
        compiler_params=compiler_params(),
        cost_estimate=SMALL,
        name="join_parts",
    )(*operands)


class Plan:
    def __init__(self, rows, n, down, up, heads, ahead):
        shard = rows // BLOCK
        self.down, self.up = down, up
        self.a = [(l + 1, l) for l in down]
        self.b = [(l + 2, l) for l in down if down[l] > shard and l + 2 < n]
        self.k = [(l, l + 1) for l in up]
        self.na = BLOCK * min(shard, max(down.values()))
        self.nb = BLOCK * max(0, max(down.values()) - shard)
        self.nk = BLOCK * max([0, *up.values()])
        self.heads, self.ahead = heads, ahead
        ends = lambda pairs, side: [int(any(p[side] == d for p in pairs)) for d in range(n)]
        self.a_from, self.a_to = ends(self.a, 0), ends(self.a, 1)
        self.b_from, self.b_to = ends(self.b, 0), ends(self.b, 1)
        self.k_to = ends(self.k, 1)

    def fits(self, needs):
        good = True
        for l, (behind, before) in enumerate(needs):
            if l in self.down:
                good = good & (behind <= BLOCK * self.down[l])
            else:
                good = good & (before <= BLOCK * self.up[l])
        return good


def plans_of(rows, n):
    last = rows // BLOCK - 1
    some, four = [8, 8], [4, 4, 4, 4]
    plans = [
        Plan(rows, n, {0: 3, 1: 3, 2: last}, {}, four, some),
        Plan(rows, n, {1: 3, 2: last}, {0: 2}, four, some),
        Plan(rows, n, {0: 3, 2: last}, {1: 2}, four, some),
        Plan(rows, n, {2: last}, {0: 2, 1: 2}, four, some),
        Plan(rows, n, {0: 4, 1: 4, 2: last}, {}, four, some),
        Plan(rows, n, {1: 4, 2: last}, {0: 2}, four, some),
        Plan(rows, n, {0: 4, 2: last}, {1: 2}, four, some),
        Plan(rows, n, {1: 3 + last, 2: last}, {0: 3}, [4, 4, 4, 2, 2], some),
    ]
    return plans


def choose_kernel(plans, rows, genomes, info, out):
    n = lax.axis_size("ctx")
    starts = [info[i] for i in range(genomes)]
    needs = []
    for boundary in range(rows, n * rows, rows):
        begin, end = 0, n * rows
        for start in starts:
            begin = jnp.where(start < boundary, start, begin)
        for start in reversed(starts):
            end = jnp.where(start >= boundary, start, end)
        crossing = end > boundary
        needs.append(
            (jnp.where(crossing, end - boundary, 0), jnp.where(crossing, boundary - begin, 0))
        )
    choice = len(plans) - 1
    for i in reversed(range(len(plans) - 1)):
        choice = jnp.where(plans[i].fits(needs), i, choice)
    out[0] = choice


def choose(plans, rows, starts):
    return pl.pallas_call(
        partial(choose_kernel, plans, rows, starts.shape[0]),
        in_specs=[pl.BlockSpec(memory_space=pltpu.SMEM)],
        out_specs=pl.BlockSpec(memory_space=pltpu.SMEM),
        out_shape=jax.ShapeDtypeStruct((1,), jnp.int32),
        cost_estimate=SMALL,
        name="choose_plan",
    )(starts)[0]


def after(value, *earlier):
    earlier = [x for x in earlier if x is not None]
    return lax.optimization_barrier((value, *earlier))[0] if earlier else value


def run_plan(plan, hq, hk, hv, filters, gain, q, k, starts):
    n = lax.axis_size("ctx")
    rows, channels = hk.shape
    send = lambda x, pairs: lax.ppermute(x, "ctx", pairs)
    back = lambda pairs: [(t, s) for s, t in pairs]
    halo = send(halo_product(hk, hv), [(i, i + 1) for i in range(n - 1)])
    mix = hyena(starts, hq, hk, hv, halo, filters, gain)

    def columns(x, first, heads):
        return x[:, first * HEAD_DIM : (first + heads) * HEAD_DIM]

    groups, at = [], 0
    for heads in plan.ahead:
        groups.append((at, heads))
        at += heads
    pairs = [p for p in (plan.a, plan.b) if p]
    first, out = 0, None
    qa = qb = rk = rv = None
    came_back, told = [()], [None]
    for heads in plan.heads:
        if groups and first == groups[0][0]:
            start, many = groups.pop(0)
            turn = (qa, qb, rk, rv)
            if plan.na:
                qa = send(after(columns(q[: plan.na], start, many), *turn), plan.a)
            if plan.nb:
                qb = send(after(columns(q[: plan.nb], start, many), *turn), plan.b)
            if plan.nk:
                keys = columns(k[rows - plan.nk :], start, many)
                rk = send(after(keys, halo, *turn), plan.k)
        skip = first - start
        if plan.nk:
            values = columns(mix[rows - plan.nk :], first, heads)
            turn = (rv, told[-2] if len(told) > 2 else None)
            turn += tuple(came_back[-3]) if len(came_back) > 3 else ()
            rv = send(after(values, *turn), plan.k)
        o, s, *parts = attend(
            plan,
            after(starts, *(came_back[-2] if len(came_back) > 2 else ())),
            q,
            k,
            mix,
            (qa, skip),
            (qb, skip),
            (rk, skip),
            (rv, 0),
            first,
            heads,
        )
        told.append(s)
        others = [send(x, back(p)) for x, p in zip(parts, pairs)]
        came_back.append(others)
        out = join(plan, o, s, others, first, channels, out)
        first += heads
    return mix, out


def attend_update(queries, query_pos, query_begin, key_heads, value_heads, key_pos):
    score_scale = 1.0 / math.sqrt(HEAD_DIM)
    scores = (
        jnp.einsum("qhd,khd->hqk", queries, key_heads, preferred_element_type=jnp.float32)
        * score_scale
    )
    visible = (key_pos[None, :] <= query_pos[:, None]) & (key_pos[None, :] >= query_begin[:, None])
    new_max = jnp.max(jnp.where(visible[None], scores, FAR), axis=2)
    weights = jnp.exp(jnp.where(visible[None], scores - new_max[:, :, None], FAR))
    mixed = jnp.einsum(
        "hqk,khd->hqd",
        weights.astype(jnp.bfloat16),
        value_heads,
        preferred_element_type=jnp.float32,
    )
    return mixed / jnp.sum(weights, axis=2)[:, :, None]


def run_gathered(hq, hk, hv, filters, gain, q, k, starts):
    n = lax.axis_size("ctx")
    rows, channels = hk.shape
    heads = channels // HEAD_DIM
    own = (lax.axis_index("ctx") * rows).astype(jnp.int32)
    halo = lax.ppermute(halo_product(hk, hv), "ctx", [(i, i + 1) for i in range(n - 1)])
    mix = hyena(starts, hq, hk, hv, halo, filters, gain)
    keys = lax.all_gather(k, "ctx", axis=0, tiled=True)
    values = lax.all_gather(mix, "ctx", axis=0, tiled=True)
    key_pos = jnp.arange(n * rows, dtype=jnp.int32)
    pos = own + jnp.arange(rows, dtype=jnp.int32)
    mixed = attend_update(
        q.reshape(rows, heads, HEAD_DIM),
        pos,
        begin_of(pos, [starts[i] for i in range(starts.shape[0])]),
        keys.reshape(n * rows, heads, HEAD_DIM),
        values.reshape(n * rows, heads, HEAD_DIM),
        key_pos,
    )
    return mix, mixed.astype(jnp.bfloat16).transpose(1, 0, 2).reshape(rows, channels)


def per_device(hq, hk, hv, filters, skip_gain, q, k, starts):
    rows, channels = hk.shape
    n = lax.axis_size("ctx")
    gain = skip_gain[None, :]
    if n != 4:
        return run_gathered(hq, hk, hv, filters, gain, q, k, starts)
    plans = plans_of(rows, n)
    branches = [partial(run_plan, plan) for plan in plans]
    operands = (hq, hk, hv, filters, gain, q, k, starts)
    return lax.switch(choose(plans, rows, starts), branches, *operands)


def solution(mesh):
    split = P(("rep", "ctx"), ("ch", "sub"))
    return jax.shard_map(
        per_device,
        mesh=mesh,
        in_specs=(
            split,
            split,
            split,
            P(("ch", "sub"), None),
            P(("ch", "sub")),
            split,
            split,
            P("rep"),
        ),
        out_specs=(split, split),
        check_vma=False,
    )
```

```python
from functools import partial
import math

import jax
import jax.numpy as jnp
from jax import lax
from jax.experimental import pallas as pl
from jax.experimental.pallas import tpu as pltpu
from jax.sharding import PartitionSpec as P

HEAD_DIM = 128
BLOCK = 128
FAR = -1e30
TO_LOG2 = math.log2(math.e) / math.sqrt(HEAD_DIM)
VMEM_LIMIT = 48 * 1024 * 1024
HEADS_AT_ONCE = 2
SMALL = pl.CostEstimate(flops=1024, bytes_accessed=1024, transcendentals=0)
STAT_ROWS = 32


def begin_of(pos, starts):
    begin = jnp.zeros_like(pos)
    for start in starts:
        begin = jnp.where(pos >= start, start, begin)
    return begin


def compiler_params():
    return pltpu.CompilerParams(vmem_limit_bytes=VMEM_LIMIT)


def rounded_product(key, value):
    return (key.astype(jnp.float32) * value.astype(jnp.float32)).astype(jnp.bfloat16)


def halo_kernel(hk, hv, out):
    out[...] = rounded_product(hk[...], hv[...])


def halo_product(hk, hv):
    rows, channels = hk.shape
    width = min(channels, 512)
    last = pl.BlockSpec((BLOCK, width), lambda j: (rows // BLOCK - 1, j))
    return pl.pallas_call(
        halo_kernel,
        grid=(channels // width,),
        in_specs=[last, last],
        out_specs=pl.BlockSpec((BLOCK, width), lambda j: (0, j)),
        out_shape=jax.ShapeDtypeStruct((BLOCK, channels), jnp.bfloat16),
        compiler_params=compiler_params(),
        cost_estimate=SMALL,
        name="halo_product",
    )(hk, hv)


def hyena_kernel(genomes, group, info, hq, hk, hv, halo, filters, gain, out, lines, ext, mask):
    rows, width = out.shape
    blocks = rows // BLOCK
    groups = BLOCK // group
    tiles = width // BLOCK
    starts = [info[i] for i in range(genomes)]
    step = pl.program_id(0)
    first = lax.axis_index("ctx") * rows
    row = lax.broadcasted_iota(jnp.int32, (BLOCK, BLOCK), 0)
    col = lax.broadcasted_iota(jnp.int32, (BLOCK, BLOCK), 1)

    @pl.when(step == 0)
    def _():
        turn = jnp.where((row + col) % BLOCK == 0, 1.0, 0.0).astype(jnp.bfloat16)
        lines[...] = jnp.dot(filters[...], turn, preferred_element_type=jnp.float32)
        for b in range(blocks):
            here = first + b * BLOCK
            begin = begin_of(here + row, starts)
            before = (col > row) & (here - BLOCK + col >= begin)
            within = (col <= row) & (here + col >= begin)
            mask[b, :, :BLOCK] = jnp.where(before, 1.0, 0.0).astype(jnp.bfloat16)
            mask[b, :, BLOCK:] = jnp.where(within, 1.0, 0.0).astype(jnp.bfloat16)

    ext[:BLOCK, :] = halo[...]
    ext[BLOCK:, :] = rounded_product(hk[...], hv[...])
    ours = lines[pl.ds(pl.multiple_of(step * groups * tiles, groups * tiles), groups * tiles), :]
    lane_group = col // group
    for t in range(tiles):
        lanes = slice(t * BLOCK, (t + 1) * BLOCK)
        turned = []
        for g in range(groups):
            line = jnp.broadcast_to(ours[t * groups + g, :][None, :], (BLOCK, BLOCK))
            turned.append(pltpu.roll(line, 0, 1, stride=1, stride_axis=0).astype(jnp.bfloat16))
        for b in range(blocks):
            tall = jnp.concatenate(
                [
                    jnp.concatenate([one * mask[b, :, :BLOCK], one * mask[b, :, BLOCK:]], axis=1)
                    for one in turned
                ],
                axis=0,
            )
            window = ext[b * BLOCK : (b + 2) * BLOCK, lanes]
            every = jnp.dot(tall, window, preferred_element_type=jnp.float32)
            filtered = every[:BLOCK]
            for g in range(1, groups):
                filtered = jnp.where(
                    lane_group == g, every[g * BLOCK : (g + 1) * BLOCK], filtered
                )
            at = slice(b * BLOCK, (b + 1) * BLOCK)
            direct = ext[(b + 1) * BLOCK : (b + 2) * BLOCK, lanes].astype(jnp.float32)
            mix = hq[at, lanes].astype(jnp.float32) * (filtered + gain[:, lanes] * direct)
            out[at, lanes] = mix.astype(jnp.bfloat16)


def hyena(starts, hq, hk, hv, halo, filters, gain):
    rows, channels = hk.shape
    group = channels // filters.shape[0]
    width = 2 * BLOCK
    here = lambda r: pl.BlockSpec((r, width), lambda j: (0, j))
    return pl.pallas_call(
        partial(hyena_kernel, starts.shape[0], group),
        grid=(channels // width,),
        in_specs=[
            pl.BlockSpec(memory_space=pltpu.SMEM),
            here(rows),
            here(rows),
            here(rows),
            here(BLOCK),
            pl.BlockSpec(filters.shape, lambda j: (0, 0)),
            here(1),
        ],
        out_specs=here(rows),
        out_shape=jax.ShapeDtypeStruct((rows, channels), jnp.bfloat16),
        scratch_shapes=[
            pltpu.VMEM((filters.shape[0], BLOCK), jnp.float32),
            pltpu.VMEM((rows + BLOCK, width), jnp.bfloat16),
            pltpu.VMEM((rows // BLOCK, BLOCK, 2 * BLOCK), jnp.bfloat16),
        ],
        compiler_params=compiler_params(),
        cost_estimate=SMALL,
        name="hyena_mix",
    )(starts, hq, hk, hv, halo, filters, gain)


def one_of(flags, me):
    on = me < 0
    for d, flag in enumerate(flags):
        if flag:
            on = on | (me == d)
    return on


def attend_kernel(genomes, plan, info, q, k, v, *rest):
    rows = q.shape[0]
    me = lax.axis_index("ctx")
    own = me * rows
    rest = list(rest)
    jobs = [(rows, q, own, None)]
    if plan.na:
        jobs.append((plan.na, rest.pop(0), own + rows, one_of(plan.a_to, me)))
    if plan.nb:
        jobs.append((plan.nb, rest.pop(0), own + 2 * rows, one_of(plan.b_to, me)))
    rk, rv = (rest.pop(0), rest.pop(0)) if plan.nk else (None, None)
    out, stats = rest.pop(0), rest.pop(0)
    outs = [out] + rest[: len(jobs) - 1]
    starts = [info[i] for i in range(genomes)]

    def seen(row_at, count, col_at, columns):
        row = row_at + lax.broadcasted_iota(jnp.int32, (count, columns), 0)
        col = col_at + lax.broadcasted_iota(jnp.int32, (count, columns), 1)
        begin = begin_of(row_at + lax.broadcasted_iota(jnp.int32, (count, 1), 0), starts)
        return (col <= row) & (col >= begin)

    def piece(queries, out, count, row_at, far, put):
        sets = [(k, v, seen(row_at, count, own, rows))]
        if far:
            sets.append((rk, rv, seen(row_at, count, own - plan.nk, plan.nk)))
        for h in range(q.shape[1] // HEAD_DIM):
            lanes = slice(h * HEAD_DIM, (h + 1) * HEAD_DIM)
            scores = [
                jnp.where(
                    visible,
                    lax.dot_general(
                        queries[:, lanes],
                        keys[:, lanes],
                        (((1,), (1,)), ((), ())),
                        preferred_element_type=jnp.float32,
                    ),
                    FAR,
                )
                for keys, _, visible in sets
            ]
            top = jnp.max(scores[0], axis=1, keepdims=True)
            for one in scores[1:]:
                top = jnp.maximum(top, jnp.max(one, axis=1, keepdims=True))
            mixed = 0.0
            for one, (_, values, _) in zip(scores, sets):
                weights = jnp.exp2((one - top) * TO_LOG2).astype(jnp.bfloat16)
                wide = [values[:, lanes], jnp.ones((values.shape[0], HEAD_DIM), jnp.bfloat16)]
                mixed = mixed + jnp.dot(
                    weights, jnp.concatenate(wide, axis=1), preferred_element_type=jnp.float32
                )
            total = mixed[:, HEAD_DIM:]
            out[:count, lanes] = (mixed[:, :HEAD_DIM] / total).astype(jnp.bfloat16)
            put(h, as_rows(top * TO_LOG2 + jnp.log2(total)))

    for (count, queries, at, on), out in zip(jobs, outs):
        put = partial(keep, stats) if on is None else partial(carry, out, count)

        begin = begin_of(at, starts)
        on = True if on is None else on & (begin < own + rows)
        near_only = on
        if plan.nk:
            far = on & (begin < own) & one_of(plan.k_to, me)
            near_only = on & jnp.logical_not(far)

            @pl.when(far)
            def _():
                piece(queries, out, count, at, True, put)

        if near_only is True:
            piece(queries, out, count, at, False, put)
        else:

            @pl.when(near_only)
            def _():
                piece(queries, out, count, at, False, put)

        if on is not True:

            @pl.when(jnp.logical_not(on))
            def _():
                out[:count, :] = jnp.zeros((count, out.shape[1]), jnp.bfloat16)
                for h in range(out.shape[1] // HEAD_DIM):
                    put(h, jnp.full((8, BLOCK), FAR, jnp.float32))


def as_rows(column):
    row = lax.broadcasted_iota(jnp.int32, (BLOCK, BLOCK), 0)
    lane = lax.broadcasted_iota(jnp.int32, (BLOCK, BLOCK), 1)
    rows = [
        jnp.sum(jnp.where(row == lane, column[i : i + BLOCK], 0.0), axis=0, keepdims=True)
        for i in range(0, column.shape[0], BLOCK)
    ]
    return jnp.concatenate(rows + [jnp.zeros_like(rows[0])] * (8 - len(rows)))


def keep(out, h, stat):
    out[h * 8 : (h + 1) * 8, :] = stat


def carry(out, count, h, stat):
    high = stat.astype(jnp.bfloat16).astype(jnp.float32)
    middle = (stat - high).astype(jnp.bfloat16).astype(jnp.float32)
    low = stat - high - middle
    parts = jnp.concatenate([high, middle, low, jnp.zeros_like(low)])
    out[count:, h * HEAD_DIM : (h + 1) * HEAD_DIM] = parts.astype(jnp.bfloat16)


def attend(plan, starts, q, k, v, qa, qb, rk, rv, first, heads):
    rows = q.shape[0]
    width = HEADS_AT_ONCE * HEAD_DIM
    here = lambda r: pl.BlockSpec((r, width), lambda h: (0, h))
    later = lambda r, skip, row=0: pl.BlockSpec(
        (r, width), lambda h: (row, h + skip // HEADS_AT_ONCE)
    )
    whole = lambda r: later(r, first)
    in_specs = [pl.BlockSpec(memory_space=pltpu.SMEM), whole(rows), whole(rows), whole(rows)]
    operands = [starts, q, k, v]
    counts = (plan.na, plan.nb, plan.nk, plan.nk)
    for (x, *at), count in zip((qa, qb, rk, rv), counts):
        in_specs.append(later(count, *at))
        operands.append(x)
    out_specs = [here(rows), pl.BlockSpec((HEADS_AT_ONCE * 8, BLOCK), lambda h: (h, 0))]
    out_shape = [
        jax.ShapeDtypeStruct((rows, heads * HEAD_DIM), jnp.bfloat16),
        jax.ShapeDtypeStruct((heads * 8, BLOCK), jnp.float32),
    ]
    for count in (plan.na, plan.nb):
        if count:
            out_specs.append(here(count + STAT_ROWS))
            out_shape.append(
                jax.ShapeDtypeStruct((count + STAT_ROWS, heads * HEAD_DIM), jnp.bfloat16)
            )
    queries, keys = rows + plan.na + plan.nb, rows + plan.nk
    return pl.pallas_call(
        partial(attend_kernel, starts.shape[0], plan),
        grid=(heads // HEADS_AT_ONCE,),
        in_specs=in_specs,
        out_specs=out_specs,
        out_shape=out_shape,
        compiler_params=compiler_params(),
        cost_estimate=SMALL,
        name="attend_parts",
    )(*operands)


def join_kernel(plan, o, s, *rest):
    rest = list(rest)
    me = lax.axis_index("ctx")
    out = rest[-1]
    rows = o.shape[0]
    block = lax.broadcasted_iota(jnp.int32, (8, BLOCK), 0)
    parts = [(o, rows, None)]
    for count, flags in ((plan.na, plan.a_from), (plan.nb, plan.b_from)):
        if count:
            parts.append((rest.pop(0), count, one_of(flags, me) & (block < count // BLOCK)))
    for h in range(o.shape[1] // HEAD_DIM):
        lanes = slice(h * HEAD_DIM, (h + 1) * HEAD_DIM)
        stats = [s[h * 8 : (h + 1) * 8, :]]
        for part, count, on in parts[1:]:
            carried = part[count:, lanes].astype(jnp.float32)
            stats.append(jnp.where(on, carried[:8] + carried[8:16] + carried[16:24], FAR))
        top = stats[0]
        for x in stats[1:]:
            top = jnp.maximum(top, x)
        weights = [jnp.exp2(x - top) for x in stats]
        total = sum(weights)
        weights = [(w / total).T for w in weights]
        for i in range(rows // BLOCK):
            sl = slice(i * BLOCK, (i + 1) * BLOCK)
            mixed = sum(
                w[:, i : i + 1] * part[sl, lanes].astype(jnp.float32)
                for w, (part, count, _) in zip(weights, parts)
                if i * BLOCK < count
            )
            out[sl, lanes] = mixed.astype(jnp.bfloat16)


def join(plan, o, s, others, first, channels, full):
    rows, wide = o.shape
    width = HEADS_AT_ONCE * HEAD_DIM
    skip = first // HEADS_AT_ONCE
    here = lambda r: pl.BlockSpec((r, width), lambda h: (0, h))
    operands = [o, s] + others
    in_specs = [here(rows), pl.BlockSpec((HEADS_AT_ONCE * 8, BLOCK), lambda h: (h, 0))]
    in_specs += [here(x.shape[0]) for x in others]
    aliases = {}
    if full is not None:
        in_specs.append(pl.BlockSpec(memory_space=pl.ANY))
        operands.append(full)
        aliases = {len(operands) - 1: 0}
    return pl.pallas_call(
        partial(join_kernel, plan),
        grid=(wide // width,),
        in_specs=in_specs,
        out_specs=pl.BlockSpec((rows, width), lambda h: (0, h + skip)),
        out_shape=jax.ShapeDtypeStruct((rows, channels), jnp.bfloat16),
        input_output_aliases=aliases,
        compiler_params=compiler_params(),
        cost_estimate=SMALL,
        name="join_parts",
    )(*operands)


class Plan:
    def __init__(self, rows, n, heads):
        self.a, self.b, self.k = [(2, 1), (3, 2)], [(3, 1)], [(0, 1)]
        self.na, self.nb, self.nk = rows, rows - BLOCK, rows
        self.heads = heads
        ends = lambda pairs, side: [int(any(p[side] == d for p in pairs)) for d in range(n)]
        self.a_from, self.a_to = ends(self.a, 0), ends(self.a, 1)
        self.b_from, self.b_to = ends(self.b, 0), ends(self.b, 1)
        self.k_to = ends(self.k, 1)


def after(value, *earlier):
    return lax.optimization_barrier((value, *earlier))[0] if earlier else value


def run_plan(plan, hq, hk, hv, filters, gain, q, k, starts):
    n = lax.axis_size("ctx")
    rows, channels = hk.shape
    send = lambda x, pairs: lax.ppermute(x, "ctx", pairs)
    back = lambda pairs: [(t, s) for s, t in pairs]
    columns = lambda x, first, end: x[:, first * HEAD_DIM : end * HEAD_DIM]

    halo = send(halo_product(hk, hv), [(i, i + 1) for i in range(n - 1)])
    mix = hyena(starts, hq, hk, hv, halo, filters, gain)
    heads, total = plan.heads, channels // HEAD_DIM
    early_keys, early_queries = sum(heads[:2]), sum(heads[:3])
    rk = send(after(columns(k, 0, early_keys), halo), plan.k)
    qa = send(columns(q, 0, early_queries), plan.a)
    qb = send(columns(q[: plan.nb], 0, early_queries), plan.b)

    told, came_back, out = [], [], None
    first = q_at = 0
    for c, many in enumerate(heads):
        end = first + many
        if first == early_queries:
            q_at = first
            qa = send(after(columns(q, first, total), *came_back[0]), plan.a)
            qb = send(after(columns(q[: plan.nb], first, total), *came_back[0]), plan.b)
        if end <= early_keys:
            keys = (rk, first)
            values = (send(columns(mix, first, end), plan.k), 0, 0)
        else:
            pair = jnp.concatenate([columns(k, first, end), columns(mix, first, end)])
            pair = send(after(pair, told[c - 2]), plan.k)
            keys, values = (pair, 0), (pair, 0, 1)
        ready = after(starts, *came_back[c - 2]) if c >= 2 else starts
        o, s, *parts = attend(
            plan, ready, q, k, mix, (qa, first - q_at), (qb, first - q_at), keys, values, first, many
        )
        told.append(s)
        came_back.append([send(x, back(p)) for x, p in zip(parts, (plan.a, plan.b))])
        out = join(plan, o, s, came_back[-1], first, channels, out)
        first = end
    return mix, out


def attend_update(queries, query_pos, query_begin, key_heads, value_heads, key_pos):
    score_scale = 1.0 / math.sqrt(HEAD_DIM)
    scores = (
        jnp.einsum("qhd,khd->hqk", queries, key_heads, preferred_element_type=jnp.float32)
        * score_scale
    )
    visible = (key_pos[None, :] <= query_pos[:, None]) & (key_pos[None, :] >= query_begin[:, None])
    new_max = jnp.max(jnp.where(visible[None], scores, FAR), axis=2)
    weights = jnp.exp(jnp.where(visible[None], scores - new_max[:, :, None], FAR))
    mixed = jnp.einsum(
        "hqk,khd->hqd",
        weights.astype(jnp.bfloat16),
        value_heads,
        preferred_element_type=jnp.float32,
    )
    return mixed / jnp.sum(weights, axis=2)[:, :, None]


def run_gathered(hq, hk, hv, filters, gain, q, k, starts):
    n = lax.axis_size("ctx")
    rows, channels = hk.shape
    heads = channels // HEAD_DIM
    own = (lax.axis_index("ctx") * rows).astype(jnp.int32)
    halo = lax.ppermute(halo_product(hk, hv), "ctx", [(i, i + 1) for i in range(n - 1)])
    mix = hyena(starts, hq, hk, hv, halo, filters, gain)
    keys = lax.all_gather(k, "ctx", axis=0, tiled=True)
    values = lax.all_gather(mix, "ctx", axis=0, tiled=True)
    key_pos = jnp.arange(n * rows, dtype=jnp.int32)
    pos = own + jnp.arange(rows, dtype=jnp.int32)
    mixed = attend_update(
        q.reshape(rows, heads, HEAD_DIM),
        pos,
        begin_of(pos, [starts[i] for i in range(starts.shape[0])]),
        keys.reshape(n * rows, heads, HEAD_DIM),
        values.reshape(n * rows, heads, HEAD_DIM),
        key_pos,
    )
    return mix, mixed.astype(jnp.bfloat16).transpose(1, 0, 2).reshape(rows, channels)


def per_device(hq, hk, hv, filters, skip_gain, q, k, starts):
    rows, channels = hk.shape
    n = lax.axis_size("ctx")
    gain = skip_gain[None, :]
    if n != 4:
        return run_gathered(hq, hk, hv, filters, gain, q, k, starts)
    plan = Plan(rows, n, [4, 4, 4, 4])
    return run_plan(plan, hq, hk, hv, filters, gain, q, k, starts)


def solution(mesh):
    split = P(("rep", "ctx"), ("ch", "sub"))
    return jax.shard_map(
        per_device,
        mesh=mesh,
        in_specs=(
            split,
            split,
            split,
            P(("ch", "sub"), None),
            P(("ch", "sub")),
            split,
            split,
            P("rep"),
        ),
        out_specs=(split, split),
        check_vma=False,
    )
```

```python
from functools import partial
import math

import jax
import jax.numpy as jnp
from jax import lax
from jax.experimental import pallas as pl
from jax.experimental.pallas import tpu as pltpu
from jax.sharding import PartitionSpec as P

HEAD_DIM = 128
BLOCK = 128
FAR = -1e30
TO_LOG2 = math.log2(math.e) / math.sqrt(HEAD_DIM)
VMEM_LIMIT = 48 * 1024 * 1024
HEADS_AT_ONCE = 2
SMALL = pl.CostEstimate(flops=1024, bytes_accessed=1024, transcendentals=0)
STAT_ROWS = 16


def begin_of(pos, starts):
    begin = jnp.zeros_like(pos)
    for start in starts:
        begin = jnp.where(pos >= start, start, begin)
    return begin


def compiler_params():
    return pltpu.CompilerParams(vmem_limit_bytes=VMEM_LIMIT)


def rounded_product(key, value):
    return (key.astype(jnp.float32) * value.astype(jnp.float32)).astype(jnp.bfloat16)


def halo_kernel(hk, hv, out):
    out[...] = rounded_product(hk[...], hv[...])


def halo_product(hk, hv):
    rows, channels = hk.shape
    width = min(channels, 1024)
    last = pl.BlockSpec((BLOCK, width), lambda j: (rows // BLOCK - 1, j))
    return pl.pallas_call(
        halo_kernel,
        grid=(channels // width,),
        in_specs=[last, last],
        out_specs=pl.BlockSpec((BLOCK, width), lambda j: (0, j)),
        out_shape=jax.ShapeDtypeStruct((BLOCK, channels), jnp.bfloat16),
        compiler_params=pltpu.CompilerParams(vmem_limit_bytes=60 * 1024 * 1024),
        cost_estimate=SMALL,
        name="halo_product",
    )(hk, hv)


def hyena_kernel(genomes, group, info, hq, hk, hv, halo, filters, gain, out, lines, ext, mask):
    rows, width = out.shape
    blocks = rows // BLOCK
    groups = BLOCK // group
    tiles = width // BLOCK
    starts = [info[i] for i in range(genomes)]
    step = pl.program_id(0)
    first = lax.axis_index("ctx") * rows
    row = lax.broadcasted_iota(jnp.int32, (BLOCK, BLOCK), 0)
    col = lax.broadcasted_iota(jnp.int32, (BLOCK, BLOCK), 1)

    @pl.when(step == 0)
    def _():
        turn = jnp.where((row + col) % BLOCK == 0, 1.0, 0.0).astype(jnp.bfloat16)
        lines[...] = jnp.dot(filters[...], turn, preferred_element_type=jnp.float32)
        for b in range(blocks):
            here = first + b * BLOCK
            begin = begin_of(here + row, starts)
            before = (col > row) & (here - BLOCK + col >= begin)
            within = (col <= row) & (here + col >= begin)
            mask[b, :, :BLOCK] = jnp.where(before, 1.0, 0.0).astype(jnp.bfloat16)
            mask[b, :, BLOCK:] = jnp.where(within, 1.0, 0.0).astype(jnp.bfloat16)

    ext[:BLOCK, :] = halo[...]
    ext[BLOCK:, :] = rounded_product(hk[...], hv[...])
    ours = lines[pl.ds(pl.multiple_of(step * groups * tiles, groups * tiles), groups * tiles), :]
    lane_group = col // group
    for t in range(tiles):
        lanes = slice(t * BLOCK, (t + 1) * BLOCK)
        turned = []
        for g in range(groups):
            line = jnp.broadcast_to(ours[t * groups + g, :][None, :], (BLOCK, BLOCK))
            turned.append(pltpu.roll(line, 0, 1, stride=1, stride_axis=0).astype(jnp.bfloat16))
        for b in range(blocks):
            tall = jnp.concatenate(
                [
                    jnp.concatenate([one * mask[b, :, :BLOCK], one * mask[b, :, BLOCK:]], axis=1)
                    for one in turned
                ],
                axis=0,
            )
            window = ext[b * BLOCK : (b + 2) * BLOCK, lanes]
            every = jnp.dot(tall, window, preferred_element_type=jnp.float32)
            filtered = every[:BLOCK]
            for g in range(1, groups):
                filtered = jnp.where(
                    lane_group == g, every[g * BLOCK : (g + 1) * BLOCK], filtered
                )
            at = slice(b * BLOCK, (b + 1) * BLOCK)
            direct = ext[(b + 1) * BLOCK : (b + 2) * BLOCK, lanes].astype(jnp.float32)
            mix = hq[at, lanes].astype(jnp.float32) * (filtered + gain[:, lanes] * direct)
            out[at, lanes] = mix.astype(jnp.bfloat16)


def hyena(starts, hq, hk, hv, halo, filters, gain):
    rows, channels = hk.shape
    group = channels // filters.shape[0]
    width = 2 * BLOCK
    here = lambda r: pl.BlockSpec((r, width), lambda j: (0, j))
    return pl.pallas_call(
        partial(hyena_kernel, starts.shape[0], group),
        grid=(channels // width,),
        in_specs=[
            pl.BlockSpec(memory_space=pltpu.SMEM),
            here(rows),
            here(rows),
            here(rows),
            here(BLOCK),
            pl.BlockSpec(filters.shape, lambda j: (0, 0)),
            here(1),
        ],
        out_specs=here(rows),
        out_shape=jax.ShapeDtypeStruct((rows, channels), jnp.bfloat16),
        scratch_shapes=[
            pltpu.VMEM((filters.shape[0], BLOCK), jnp.float32),
            pltpu.VMEM((rows + BLOCK, width), jnp.bfloat16),
            pltpu.VMEM((rows // BLOCK, BLOCK, 2 * BLOCK), jnp.bfloat16),
        ],
        compiler_params=compiler_params(),
        cost_estimate=SMALL,
        name="hyena_mix",
    )(starts, hq, hk, hv, halo, filters, gain)


def one_of(flags, me):
    on = me < 0
    for d, flag in enumerate(flags):
        if flag:
            on = on | (me == d)
    return on


def attend_kernel(genomes, plan, info, q, k, v, *rest):
    rows = q.shape[0]
    me = lax.axis_index("ctx")
    own = me * rows
    rest = list(rest)
    jobs = [(rows, q, own, None)]
    if plan.na:
        jobs.append((plan.na, rest.pop(0), own + rows, one_of(plan.a_to, me)))
    if plan.nb:
        jobs.append((plan.nb, rest.pop(0), own + 2 * rows, one_of(plan.b_to, me)))
    rk, rv = (rest.pop(0), rest.pop(0)) if plan.nk else (None, None)
    out, stats = rest.pop(0), rest.pop(0)
    outs = [out] + rest[: len(jobs) - 1]
    starts = [info[i] for i in range(genomes)]

    def seen(row_at, count, col_at, columns):
        row = row_at + lax.broadcasted_iota(jnp.int32, (count, columns), 0)
        col = col_at + lax.broadcasted_iota(jnp.int32, (count, columns), 1)
        begin = begin_of(row_at + lax.broadcasted_iota(jnp.int32, (count, 1), 0), starts)
        return (col <= row) & (col >= begin)

    def piece(queries, out, count, row_at, far, put):
        sets = [(k, v, seen(row_at, count, own, rows))]
        if far:
            sets.append((rk, rv, seen(row_at, count, own - plan.nk, plan.nk)))
        for h in range(q.shape[1] // HEAD_DIM):
            lanes = slice(h * HEAD_DIM, (h + 1) * HEAD_DIM)
            scores = [
                jnp.where(
                    visible,
                    lax.dot_general(
                        queries[:, lanes],
                        keys[:, lanes],
                        (((1,), (1,)), ((), ())),
                        preferred_element_type=jnp.float32,
                    ),
                    FAR,
                )
                for keys, _, visible in sets
            ]
            top = jnp.max(scores[0], axis=1, keepdims=True)
            for one in scores[1:]:
                top = jnp.maximum(top, jnp.max(one, axis=1, keepdims=True))
            mixed = 0.0
            for one, (_, values, _) in zip(scores, sets):
                weights = jnp.exp2((one - top) * TO_LOG2).astype(jnp.bfloat16)
                wide = [values[:, lanes], jnp.ones((values.shape[0], HEAD_DIM), jnp.bfloat16)]
                mixed = mixed + jnp.dot(
                    weights, jnp.concatenate(wide, axis=1), preferred_element_type=jnp.float32
                )
            total = mixed[:, HEAD_DIM:]
            out[:count, lanes] = (mixed[:, :HEAD_DIM] / total).astype(jnp.bfloat16)
            put(h, as_rows(top * TO_LOG2 + jnp.log2(total)))

    for (count, queries, at, on), out in zip(jobs, outs):
        put = partial(keep, stats) if on is None else partial(carry, out, count)

        begin = begin_of(at, starts)
        on = True if on is None else on & (begin < own + rows)
        near_only = on
        if plan.nk:
            far = on & (begin < own) & one_of(plan.k_to, me)
            near_only = on & jnp.logical_not(far)

            @pl.when(far)
            def _():
                piece(queries, out, count, at, True, put)

        if near_only is True:
            piece(queries, out, count, at, False, put)
        else:

            @pl.when(near_only)
            def _():
                piece(queries, out, count, at, False, put)

        if on is not True:

            @pl.when(jnp.logical_not(on))
            def _():
                out[:count, :] = jnp.zeros((count, out.shape[1]), jnp.bfloat16)
                for h in range(out.shape[1] // HEAD_DIM):
                    put(h, jnp.full((8, BLOCK), FAR, jnp.float32))


def as_rows(column):
    row = lax.broadcasted_iota(jnp.int32, (BLOCK, BLOCK), 0)
    lane = lax.broadcasted_iota(jnp.int32, (BLOCK, BLOCK), 1)
    rows = [
        jnp.sum(jnp.where(row == lane, column[i : i + BLOCK], 0.0), axis=0, keepdims=True)
        for i in range(0, column.shape[0], BLOCK)
    ]
    return jnp.concatenate(rows + [jnp.zeros_like(rows[0])] * (8 - len(rows)))


def keep(out, h, stat):
    out[h * 8 : (h + 1) * 8, :] = stat


def carry(out, count, h, stat):
    row = lax.broadcasted_iota(jnp.int32, stat.shape, 0)
    stat = jnp.where(row < count // BLOCK, stat, 0.0)
    high = stat.astype(jnp.bfloat16).astype(jnp.float32)
    middle = (stat - high).astype(jnp.bfloat16).astype(jnp.float32)
    low = stat - high - middle
    parts = jnp.concatenate([high + pltpu.roll(low, 4, 0), middle])
    out[count:, h * HEAD_DIM : (h + 1) * HEAD_DIM] = parts.astype(jnp.bfloat16)


def attend(plan, starts, q, k, v, qa, qb, rk, rv, first, heads):
    rows = q.shape[0]
    width = HEADS_AT_ONCE * HEAD_DIM
    here = lambda r: pl.BlockSpec((r, width), lambda h: (0, h))
    later = lambda r, skip, row=0: pl.BlockSpec(
        (r, width), lambda h: (row, h + skip // HEADS_AT_ONCE)
    )
    whole = lambda r: later(r, first)
    in_specs = [pl.BlockSpec(memory_space=pltpu.SMEM), whole(rows), whole(rows), whole(rows)]
    operands = [starts, q, k, v]
    counts = (plan.na, plan.nb, plan.nk, plan.nk)
    for (x, *at), count in zip((qa, qb, rk, rv), counts):
        in_specs.append(later(count, *at))
        operands.append(x)
    out_specs = [here(rows), pl.BlockSpec((HEADS_AT_ONCE * 8, BLOCK), lambda h: (h, 0))]
    out_shape = [
        jax.ShapeDtypeStruct((rows, heads * HEAD_DIM), jnp.bfloat16),
        jax.ShapeDtypeStruct((heads * 8, BLOCK), jnp.float32),
    ]
    for count in (plan.na, plan.nb):
        if count:
            out_specs.append(here(count + STAT_ROWS))
            out_shape.append(
                jax.ShapeDtypeStruct((count + STAT_ROWS, heads * HEAD_DIM), jnp.bfloat16)
            )
    queries, keys = rows + plan.na + plan.nb, rows + plan.nk
    return pl.pallas_call(
        partial(attend_kernel, starts.shape[0], plan),
        grid=(heads // HEADS_AT_ONCE,),
        in_specs=in_specs,
        out_specs=out_specs,
        out_shape=out_shape,
        compiler_params=compiler_params(),
        cost_estimate=SMALL,
        name="attend_parts",
    )(*operands)


def join_kernel(plan, o, s, *rest):
    rest = list(rest)
    me = lax.axis_index("ctx")
    out = rest[-1]
    rows = o.shape[0]
    block = lax.broadcasted_iota(jnp.int32, (8, BLOCK), 0)
    parts = [(o, rows, None)]
    for count, flags in ((plan.na, plan.a_from), (plan.nb, plan.b_from)):
        if count:
            parts.append((rest.pop(0), count, one_of(flags, me) & (block < count // BLOCK)))
    for h in range(o.shape[1] // HEAD_DIM):
        lanes = slice(h * HEAD_DIM, (h + 1) * HEAD_DIM)
        stats = [s[h * 8 : (h + 1) * 8, :]]
        for part, count, on in parts[1:]:
            carried = part[count:, lanes].astype(jnp.float32)
            stat = carried[:8] + pltpu.roll(carried[:8], 4, 0) + carried[8:]
            stats.append(jnp.where(on, stat, FAR))
        top = stats[0]
        for x in stats[1:]:
            top = jnp.maximum(top, x)
        weights = [jnp.exp2(x - top) for x in stats]
        total = sum(weights)
        weights = [(w / total).T for w in weights]
        for i in range(rows // BLOCK):
            sl = slice(i * BLOCK, (i + 1) * BLOCK)
            mixed = sum(
                w[:, i : i + 1] * part[sl, lanes].astype(jnp.float32)
                for w, (part, count, _) in zip(weights, parts)
                if i * BLOCK < count
            )
            out[sl, lanes] = mixed.astype(jnp.bfloat16)


def join(plan, o, s, others, first, channels, full):
    rows, wide = o.shape
    width = HEADS_AT_ONCE * HEAD_DIM
    skip = first // HEADS_AT_ONCE
    here = lambda r: pl.BlockSpec((r, width), lambda h: (0, h))
    operands = [o, s] + others
    in_specs = [here(rows), pl.BlockSpec((HEADS_AT_ONCE * 8, BLOCK), lambda h: (h, 0))]
    in_specs += [here(x.shape[0]) for x in others]
    aliases = {}
    if full is not None:
        in_specs.append(pl.BlockSpec(memory_space=pl.ANY))
        operands.append(full)
        aliases = {len(operands) - 1: 0}
    return pl.pallas_call(
        partial(join_kernel, plan),
        grid=(wide // width,),
        in_specs=in_specs,
        out_specs=pl.BlockSpec((rows, width), lambda h: (0, h + skip)),
        out_shape=jax.ShapeDtypeStruct((rows, channels), jnp.bfloat16),
        input_output_aliases=aliases,
        compiler_params=compiler_params(),
        cost_estimate=SMALL,
        name="join_parts",
    )(*operands)


class Plan:
    def __init__(self, rows, n, heads):
        self.a, self.b, self.k = [(2, 1), (3, 2)], [(3, 1)], [(0, 1)]
        self.na, self.nb, self.nk = rows, rows - BLOCK, rows
        self.heads = heads
        ends = lambda pairs, side: [int(any(p[side] == d for p in pairs)) for d in range(n)]
        self.a_from, self.a_to = ends(self.a, 0), ends(self.a, 1)
        self.b_from, self.b_to = ends(self.b, 0), ends(self.b, 1)
        self.k_to = ends(self.k, 1)


def after(value, *earlier):
    return lax.optimization_barrier((value, *earlier))[0] if earlier else value


def run_plan(plan, hq, hk, hv, filters, gain, q, k, starts):
    n = lax.axis_size("ctx")
    rows, channels = hk.shape
    send = lambda x, pairs: lax.ppermute(x, "ctx", pairs)
    back = lambda pairs: [(t, s) for s, t in pairs]
    columns = lambda x, first, end: x[:, first * HEAD_DIM : end * HEAD_DIM]

    halo = send(halo_product(hk, hv), [(i, i + 1) for i in range(n - 1)])
    mix = hyena(starts, hq, hk, hv, halo, filters, gain)
    heads, total = plan.heads, channels // HEAD_DIM
    early = sum(heads[:2])
    rk = send(after(columns(k, 0, early), halo), plan.k)
    qa = send(columns(q, 0, early), plan.a)
    qb = send(columns(q[: plan.nb], 0, early), plan.b)
    later_a = send(after(columns(q, early, total), halo), plan.a)
    later_b = send(after(columns(q[: plan.nb], early, total), halo), plan.b)

    told, came_back, out, go = [], [], None, None
    first = q_at = 0
    for c, many in enumerate(heads):
        end = first + many
        if first == early:
            q_at, qa, qb = first, later_a, later_b
        if end <= early:
            keys = (rk, first)
            values = (send(columns(mix, first, end), plan.k), 0, 0)
            go = values[0] if go is None else go
        else:
            pair = jnp.concatenate([columns(k, first, end), columns(mix, first, end)])
            pair = send(after(pair, told[c - 3] if c >= 3 else go), plan.k)
            keys, values = (pair, 0), (pair, 0, 1)
        ready = after(starts, *came_back[c - 2]) if c >= 2 else starts
        o, s, *parts = attend(
            plan, ready, q, k, mix, (qa, first - q_at), (qb, first - q_at), keys, values, first, many
        )
        told.append(s)
        came_back.append([send(x, back(p)) for x, p in zip(parts, (plan.a, plan.b))])
        out = join(plan, o, s, came_back[-1], first, channels, out)
        first = end
    return mix, out


def attend_update(queries, query_pos, query_begin, key_heads, value_heads, key_pos):
    score_scale = 1.0 / math.sqrt(HEAD_DIM)
    scores = (
        jnp.einsum("qhd,khd->hqk", queries, key_heads, preferred_element_type=jnp.float32)
        * score_scale
    )
    visible = (key_pos[None, :] <= query_pos[:, None]) & (key_pos[None, :] >= query_begin[:, None])
    new_max = jnp.max(jnp.where(visible[None], scores, FAR), axis=2)
    weights = jnp.exp(jnp.where(visible[None], scores - new_max[:, :, None], FAR))
    mixed = jnp.einsum(
        "hqk,khd->hqd",
        weights.astype(jnp.bfloat16),
        value_heads,
        preferred_element_type=jnp.float32,
    )
    return mixed / jnp.sum(weights, axis=2)[:, :, None]


def run_gathered(hq, hk, hv, filters, gain, q, k, starts):
    n = lax.axis_size("ctx")
    rows, channels = hk.shape
    heads = channels // HEAD_DIM
    own = (lax.axis_index("ctx") * rows).astype(jnp.int32)
    halo = lax.ppermute(halo_product(hk, hv), "ctx", [(i, i + 1) for i in range(n - 1)])
    mix = hyena(starts, hq, hk, hv, halo, filters, gain)
    keys = lax.all_gather(k, "ctx", axis=0, tiled=True)
    values = lax.all_gather(mix, "ctx", axis=0, tiled=True)
    key_pos = jnp.arange(n * rows, dtype=jnp.int32)
    pos = own + jnp.arange(rows, dtype=jnp.int32)
    mixed = attend_update(
        q.reshape(rows, heads, HEAD_DIM),
        pos,
        begin_of(pos, [starts[i] for i in range(starts.shape[0])]),
        keys.reshape(n * rows, heads, HEAD_DIM),
        values.reshape(n * rows, heads, HEAD_DIM),
        key_pos,
    )
    return mix, mixed.astype(jnp.bfloat16).transpose(1, 0, 2).reshape(rows, channels)


def per_device(hq, hk, hv, filters, skip_gain, q, k, starts):
    rows, channels = hk.shape
    n = lax.axis_size("ctx")
    gain = skip_gain[None, :]
    if n != 4:
        return run_gathered(hq, hk, hv, filters, gain, q, k, starts)
    plan = Plan(rows, n, [4, 4, 4, 2, 2])
    return run_plan(plan, hq, hk, hv, filters, gain, q, k, starts)


def solution(mesh):
    split = P(("rep", "ctx"), ("ch", "sub"))
    return jax.shard_map(
        per_device,
        mesh=mesh,
        in_specs=(
            split,
            split,
            split,
            P(("ch", "sub"), None),
            P(("ch", "sub")),
            split,
            split,
            P("rep"),
        ),
        out_specs=(split, split),
        check_vma=False,
    )
```

```python
from functools import partial
import math

import jax
import jax.numpy as jnp
from jax import lax
from jax.experimental import pallas as pl
from jax.experimental.pallas import tpu as pltpu
from jax.sharding import PartitionSpec as P

HEAD_DIM = 128
BLOCK = 128
FAR = -1e30
TO_LOG2 = math.log2(math.e) / math.sqrt(HEAD_DIM)
VMEM_LIMIT = 48 * 1024 * 1024
HEADS_AT_ONCE = 2
SMALL = pl.CostEstimate(flops=1024, bytes_accessed=1024, transcendentals=0)
STAT_ROWS = 16


def begin_of(pos, starts):
    begin = jnp.zeros_like(pos)
    for start in starts:
        begin = jnp.where(pos >= start, start, begin)
    return begin


def compiler_params():
    return pltpu.CompilerParams(vmem_limit_bytes=VMEM_LIMIT)


def rounded_product(key, value):
    return (key.astype(jnp.float32) * value.astype(jnp.float32)).astype(jnp.bfloat16)


def halo_kernel(hk, hv, out):
    out[...] = rounded_product(hk[...], hv[...])


def halo_product(hk, hv):
    rows, channels = hk.shape
    width = min(channels, 1024)
    last = pl.BlockSpec((BLOCK, width), lambda j: (rows // BLOCK - 1, j))
    return pl.pallas_call(
        halo_kernel,
        grid=(channels // width,),
        in_specs=[last, last],
        out_specs=pl.BlockSpec((BLOCK, width), lambda j: (0, j)),
        out_shape=jax.ShapeDtypeStruct((BLOCK, channels), jnp.bfloat16),
        compiler_params=pltpu.CompilerParams(vmem_limit_bytes=60 * 1024 * 1024),
        cost_estimate=SMALL,
        name="halo_product",
    )(hk, hv)


def hyena_kernel(genomes, group, info, hq, hk, hv, halo, filters, gain, out, lines, ext, mask):
    rows, width = out.shape
    blocks = rows // BLOCK
    groups = BLOCK // group
    tiles = width // BLOCK
    starts = [info[i] for i in range(genomes)]
    step = pl.program_id(0)
    first = lax.axis_index("ctx") * rows
    row = lax.broadcasted_iota(jnp.int32, (BLOCK, BLOCK), 0)
    col = lax.broadcasted_iota(jnp.int32, (BLOCK, BLOCK), 1)

    @pl.when(step == 0)
    def _():
        turn = jnp.where((row + col) % BLOCK == 0, 1.0, 0.0).astype(jnp.bfloat16)
        lines[...] = jnp.dot(filters[...], turn, preferred_element_type=jnp.float32)
        for b in range(blocks):
            here = first + b * BLOCK
            begin = begin_of(here + row, starts)
            before = (col > row) & (here - BLOCK + col >= begin)
            within = (col <= row) & (here + col >= begin)
            mask[b, :, :BLOCK] = jnp.where(before, 1.0, 0.0).astype(jnp.bfloat16)
            mask[b, :, BLOCK:] = jnp.where(within, 1.0, 0.0).astype(jnp.bfloat16)

    ext[:BLOCK, :] = halo[...]
    ext[BLOCK:, :] = rounded_product(hk[...], hv[...])
    ours = lines[pl.ds(pl.multiple_of(step * groups * tiles, groups * tiles), groups * tiles), :]
    lane_group = col // group
    for t in range(tiles):
        lanes = slice(t * BLOCK, (t + 1) * BLOCK)
        turned = []
        for g in range(groups):
            line = jnp.broadcast_to(ours[t * groups + g, :][None, :], (BLOCK, BLOCK))
            turned.append(pltpu.roll(line, 0, 1, stride=1, stride_axis=0).astype(jnp.bfloat16))
        for b in range(blocks):
            tall = jnp.concatenate(
                [
                    jnp.concatenate([one * mask[b, :, :BLOCK], one * mask[b, :, BLOCK:]], axis=1)
                    for one in turned
                ],
                axis=0,
            )
            window = ext[b * BLOCK : (b + 2) * BLOCK, lanes]
            every = jnp.dot(tall, window, preferred_element_type=jnp.float32)
            filtered = every[:BLOCK]
            for g in range(1, groups):
                filtered = jnp.where(
                    lane_group == g, every[g * BLOCK : (g + 1) * BLOCK], filtered
                )
            at = slice(b * BLOCK, (b + 1) * BLOCK)
            direct = ext[(b + 1) * BLOCK : (b + 2) * BLOCK, lanes].astype(jnp.float32)
            mix = hq[at, lanes].astype(jnp.float32) * (filtered + gain[:, lanes] * direct)
            out[at, lanes] = mix.astype(jnp.bfloat16)


def hyena(starts, hq, hk, hv, halo, filters, gain):
    rows, channels = hk.shape
    group = channels // filters.shape[0]
    width = 2 * BLOCK
    here = lambda r: pl.BlockSpec((r, width), lambda j: (0, j))
    return pl.pallas_call(
        partial(hyena_kernel, starts.shape[0], group),
        grid=(channels // width,),
        in_specs=[
            pl.BlockSpec(memory_space=pltpu.SMEM),
            here(rows),
            here(rows),
            here(rows),
            here(BLOCK),
            pl.BlockSpec(filters.shape, lambda j: (0, 0)),
            here(1),
        ],
        out_specs=here(rows),
        out_shape=jax.ShapeDtypeStruct((rows, channels), jnp.bfloat16),
        scratch_shapes=[
            pltpu.VMEM((filters.shape[0], BLOCK), jnp.float32),
            pltpu.VMEM((rows + BLOCK, width), jnp.bfloat16),
            pltpu.VMEM((rows // BLOCK, BLOCK, 2 * BLOCK), jnp.bfloat16),
        ],
        compiler_params=compiler_params(),
        cost_estimate=SMALL,
        name="hyena_mix",
    )(starts, hq, hk, hv, halo, filters, gain)


def one_of(flags, me):
    on = me < 0
    for d, flag in enumerate(flags):
        if flag:
            on = on | (me == d)
    return on


def attend_kernel(genomes, plan, info, q, k, v, *rest):
    rows = q.shape[0]
    me = lax.axis_index("ctx")
    own = me * rows
    rest = list(rest)
    jobs = [(rows, q, own, None)]
    if plan.na:
        jobs.append((plan.na, rest.pop(0), own + rows, one_of(plan.a_to, me)))
    if plan.nb:
        jobs.append((plan.nb, rest.pop(0), own + 2 * rows, one_of(plan.b_to, me)))
    rk, rv = (rest.pop(0), rest.pop(0)) if plan.nk else (None, None)
    out, stats = rest.pop(0), rest.pop(0)
    outs = [out] + rest[: len(jobs) - 1]
    starts = [info[i] for i in range(genomes)]

    def seen(row_at, count, col_at, columns):
        row = row_at + lax.broadcasted_iota(jnp.int32, (count, columns), 0)
        col = col_at + lax.broadcasted_iota(jnp.int32, (count, columns), 1)
        begin = begin_of(row_at + lax.broadcasted_iota(jnp.int32, (count, 1), 0), starts)
        return (col <= row) & (col >= begin)

    def piece(queries, out, count, row_at, far, put):
        sets = [(k, v, seen(row_at, count, own, rows))]
        if far:
            sets.append((rk, rv, seen(row_at, count, own - plan.nk, plan.nk)))
        for h in range(q.shape[1] // HEAD_DIM):
            lanes = slice(h * HEAD_DIM, (h + 1) * HEAD_DIM)
            scores = [
                jnp.where(
                    visible,
                    lax.dot_general(
                        queries[:, lanes],
                        keys[:, lanes],
                        (((1,), (1,)), ((), ())),
                        preferred_element_type=jnp.float32,
                    ),
                    FAR,
                )
                for keys, _, visible in sets
            ]
            top = jnp.max(scores[0], axis=1, keepdims=True)
            for one in scores[1:]:
                top = jnp.maximum(top, jnp.max(one, axis=1, keepdims=True))
            mixed = 0.0
            for one, (_, values, _) in zip(scores, sets):
                weights = jnp.exp2((one - top) * TO_LOG2).astype(jnp.bfloat16)
                wide = [values[:, lanes], jnp.ones((values.shape[0], HEAD_DIM), jnp.bfloat16)]
                mixed = mixed + jnp.dot(
                    weights, jnp.concatenate(wide, axis=1), preferred_element_type=jnp.float32
                )
            total = mixed[:, HEAD_DIM:]
            out[:count, lanes] = (mixed[:, :HEAD_DIM] / total).astype(jnp.bfloat16)
            put(h, as_rows(top * TO_LOG2 + jnp.log2(total)))

    for (count, queries, at, on), out in zip(jobs, outs):
        put = partial(keep, stats) if on is None else partial(carry, out, count)

        begin = begin_of(at, starts)
        on = True if on is None else on & (begin < own + rows)
        near_only = on
        if plan.nk:
            far = on & (begin < own) & one_of(plan.k_to, me)
            near_only = on & jnp.logical_not(far)

            @pl.when(far)
            def _():
                piece(queries, out, count, at, True, put)

        if near_only is True:
            piece(queries, out, count, at, False, put)
        else:

            @pl.when(near_only)
            def _():
                piece(queries, out, count, at, False, put)

        if on is not True:

            @pl.when(jnp.logical_not(on))
            def _():
                out[:count, :] = jnp.zeros((count, out.shape[1]), jnp.bfloat16)
                for h in range(out.shape[1] // HEAD_DIM):
                    put(h, jnp.full((8, BLOCK), FAR, jnp.float32))


def as_rows(column):
    row = lax.broadcasted_iota(jnp.int32, (BLOCK, BLOCK), 0)
    lane = lax.broadcasted_iota(jnp.int32, (BLOCK, BLOCK), 1)
    rows = [
        jnp.sum(jnp.where(row == lane, column[i : i + BLOCK], 0.0), axis=0, keepdims=True)
        for i in range(0, column.shape[0], BLOCK)
    ]
    return jnp.concatenate(rows + [jnp.zeros_like(rows[0])] * (8 - len(rows)))


def keep(out, h, stat):
    out[h * 8 : (h + 1) * 8, :] = stat


def carry(out, count, h, stat):
    row = lax.broadcasted_iota(jnp.int32, stat.shape, 0)
    stat = jnp.where(row < count // BLOCK, stat, 0.0)
    high = stat.astype(jnp.bfloat16).astype(jnp.float32)
    middle = (stat - high).astype(jnp.bfloat16).astype(jnp.float32)
    low = stat - high - middle
    parts = jnp.concatenate([high + pltpu.roll(low, 4, 0), middle])
    out[count:, h * HEAD_DIM : (h + 1) * HEAD_DIM] = parts.astype(jnp.bfloat16)


def attend(plan, starts, q, k, v, qa, qb, rk, rv, first, heads):
    rows = q.shape[0]
    width = HEADS_AT_ONCE * HEAD_DIM
    here = lambda r: pl.BlockSpec((r, width), lambda h: (0, h))
    later = lambda r, skip, row=0: pl.BlockSpec(
        (r, width), lambda h: (row, h + skip // HEADS_AT_ONCE)
    )
    whole = lambda r: later(r, first)
    in_specs = [pl.BlockSpec(memory_space=pltpu.SMEM), whole(rows), whole(rows), whole(rows)]
    operands = [starts, q, k, v]
    counts = (plan.na, plan.nb, plan.nk, plan.nk)
    for (x, *at), count in zip((qa, qb, rk, rv), counts):
        in_specs.append(later(count, *at))
        operands.append(x)
    out_specs = [here(rows), pl.BlockSpec((HEADS_AT_ONCE * 8, BLOCK), lambda h: (h, 0))]
    out_shape = [
        jax.ShapeDtypeStruct((rows, heads * HEAD_DIM), jnp.bfloat16),
        jax.ShapeDtypeStruct((heads * 8, BLOCK), jnp.float32),
    ]
    for count in (plan.na, plan.nb):
        if count:
            out_specs.append(here(count + STAT_ROWS))
            out_shape.append(
                jax.ShapeDtypeStruct((count + STAT_ROWS, heads * HEAD_DIM), jnp.bfloat16)
            )
    queries, keys = rows + plan.na + plan.nb, rows + plan.nk
    return pl.pallas_call(
        partial(attend_kernel, starts.shape[0], plan),
        grid=(heads // HEADS_AT_ONCE,),
        in_specs=in_specs,
        out_specs=out_specs,
        out_shape=out_shape,
        compiler_params=compiler_params(),
        cost_estimate=SMALL,
        name="attend_parts",
    )(*operands)


def join_kernel(plan, o, s, *rest):
    rest = list(rest)
    me = lax.axis_index("ctx")
    out, done = rest[-2:]
    rows = o.shape[0]
    done[...] = s[:8, :]
    block = lax.broadcasted_iota(jnp.int32, (8, BLOCK), 0)
    parts = [(o, rows, None)]
    for count, flags in ((plan.na, plan.a_from), (plan.nb, plan.b_from)):
        if count:
            parts.append((rest.pop(0), count, one_of(flags, me) & (block < count // BLOCK)))
    for h in range(o.shape[1] // HEAD_DIM):
        lanes = slice(h * HEAD_DIM, (h + 1) * HEAD_DIM)
        stats = [s[h * 8 : (h + 1) * 8, :]]
        for part, count, on in parts[1:]:
            carried = part[count:, lanes].astype(jnp.float32)
            stat = carried[:8] + pltpu.roll(carried[:8], 4, 0) + carried[8:]
            stats.append(jnp.where(on, stat, FAR))
        top = stats[0]
        for x in stats[1:]:
            top = jnp.maximum(top, x)
        weights = [jnp.exp2(x - top) for x in stats]
        total = sum(weights)
        weights = [(w / total).T for w in weights]
        for i in range(rows // BLOCK):
            sl = slice(i * BLOCK, (i + 1) * BLOCK)
            mixed = sum(
                w[:, i : i + 1] * part[sl, lanes].astype(jnp.float32)
                for w, (part, count, _) in zip(weights, parts)
                if i * BLOCK < count
            )
            out[sl, lanes] = mixed.astype(jnp.bfloat16)


def join(plan, o, s, others, first, channels, full):
    rows, wide = o.shape
    width = HEADS_AT_ONCE * HEAD_DIM
    skip = first // HEADS_AT_ONCE
    here = lambda r: pl.BlockSpec((r, width), lambda h: (0, h))
    operands = [o, s] + others
    in_specs = [here(rows), pl.BlockSpec((HEADS_AT_ONCE * 8, BLOCK), lambda h: (h, 0))]
    in_specs += [here(x.shape[0]) for x in others]
    aliases = {}
    if full is not None:
        in_specs.append(pl.BlockSpec(memory_space=pl.ANY))
        operands.append(full)
        aliases = {len(operands) - 1: 0}
    return pl.pallas_call(
        partial(join_kernel, plan),
        grid=(wide // width,),
        in_specs=in_specs,
        out_specs=[
            pl.BlockSpec((rows, width), lambda h: (0, h + skip)),
            pl.BlockSpec((8, BLOCK), lambda h: (0, 0)),
        ],
        out_shape=[
            jax.ShapeDtypeStruct((rows, channels), jnp.bfloat16),
            jax.ShapeDtypeStruct((8, BLOCK), jnp.float32),
        ],
        input_output_aliases=aliases,
        compiler_params=compiler_params(),
        cost_estimate=SMALL,
        name="join_parts",
    )(*operands)


class Plan:
    def __init__(self, rows, n, heads):
        self.a, self.b, self.k = [(2, 1), (3, 2)], [(3, 1)], [(0, 1)]
        self.na, self.nb, self.nk = rows, rows - BLOCK, rows
        self.heads = heads
        ends = lambda pairs, side: [int(any(p[side] == d for p in pairs)) for d in range(n)]
        self.a_from, self.a_to = ends(self.a, 0), ends(self.a, 1)
        self.b_from, self.b_to = ends(self.b, 0), ends(self.b, 1)
        self.k_to = ends(self.k, 1)


def after(value, *earlier):
    return lax.optimization_barrier((value, *earlier))[0] if earlier else value


def run_plan(plan, hq, hk, hv, filters, gain, q, k, starts):
    n = lax.axis_size("ctx")
    rows, channels = hk.shape
    send = lambda x, pairs: lax.ppermute(x, "ctx", pairs)
    back = lambda pairs: [(t, s) for s, t in pairs]
    columns = lambda x, first, end: x[:, first * HEAD_DIM : end * HEAD_DIM]

    halo = send(halo_product(hk, hv), [(i, i + 1) for i in range(n - 1)])
    mix = hyena(starts, hq, hk, hv, halo, filters, gain)
    heads, total = plan.heads, channels // HEAD_DIM
    early = sum(heads[:2])
    rk = send(after(columns(k, 0, early), halo), plan.k)
    qa = send(columns(q, 0, early), plan.a)
    qb = send(columns(q[: plan.nb], 0, early), plan.b)
    later_a = send(after(columns(q, early, total), halo), plan.a)

    told, joined, came_back, out, go = [], [], [], None, None
    first = q_at = 0
    for c, many in enumerate(heads):
        end = first + many
        if first == early:
            q_at, qa = first, later_a
            qb = send(after(columns(q[: plan.nb], early, total), told[0]), plan.b)
        if end <= early:
            keys = (rk, first)
            values = (send(columns(mix, first, end), plan.k), 0, 0)
            go = values[0] if go is None else go
        else:
            pair = jnp.concatenate([columns(k, first, end), columns(mix, first, end)])
            pair = send(after(pair, told[max(0, c - 3)]), plan.k)
            keys, values = (pair, 0), (pair, 0, 1)
        ready = after(starts, *(came_back[c - 2] if c >= 2 else ()), *joined[: max(0, c - 2)])
        o, s, *parts = attend(
            plan, ready, q, k, mix, (qa, first - q_at), (qb, first - q_at), keys, values, first, many
        )
        told.append(s)
        came_back.append([send(x, back(p)) for x, p in zip(parts, (plan.a, plan.b))])
        out, done = join(plan, o, s, came_back[-1], first, channels, out)
        joined.append(done)
        first = end
    return mix, out


def attend_update(queries, query_pos, query_begin, key_heads, value_heads, key_pos):
    score_scale = 1.0 / math.sqrt(HEAD_DIM)
    scores = (
        jnp.einsum("qhd,khd->hqk", queries, key_heads, preferred_element_type=jnp.float32)
        * score_scale
    )
    visible = (key_pos[None, :] <= query_pos[:, None]) & (key_pos[None, :] >= query_begin[:, None])
    new_max = jnp.max(jnp.where(visible[None], scores, FAR), axis=2)
    weights = jnp.exp(jnp.where(visible[None], scores - new_max[:, :, None], FAR))
    mixed = jnp.einsum(
        "hqk,khd->hqd",
        weights.astype(jnp.bfloat16),
        value_heads,
        preferred_element_type=jnp.float32,
    )
    return mixed / jnp.sum(weights, axis=2)[:, :, None]


def run_gathered(hq, hk, hv, filters, gain, q, k, starts):
    n = lax.axis_size("ctx")
    rows, channels = hk.shape
    heads = channels // HEAD_DIM
    own = (lax.axis_index("ctx") * rows).astype(jnp.int32)
    halo = lax.ppermute(halo_product(hk, hv), "ctx", [(i, i + 1) for i in range(n - 1)])
    mix = hyena(starts, hq, hk, hv, halo, filters, gain)
    keys = lax.all_gather(k, "ctx", axis=0, tiled=True)
    values = lax.all_gather(mix, "ctx", axis=0, tiled=True)
    key_pos = jnp.arange(n * rows, dtype=jnp.int32)
    pos = own + jnp.arange(rows, dtype=jnp.int32)
    mixed = attend_update(
        q.reshape(rows, heads, HEAD_DIM),
        pos,
        begin_of(pos, [starts[i] for i in range(starts.shape[0])]),
        keys.reshape(n * rows, heads, HEAD_DIM),
        values.reshape(n * rows, heads, HEAD_DIM),
        key_pos,
    )
    return mix, mixed.astype(jnp.bfloat16).transpose(1, 0, 2).reshape(rows, channels)


def per_device(hq, hk, hv, filters, skip_gain, q, k, starts):
    rows, channels = hk.shape
    n = lax.axis_size("ctx")
    gain = skip_gain[None, :]
    if n != 4:
        return run_gathered(hq, hk, hv, filters, gain, q, k, starts)
    plan = Plan(rows, n, [4, 4, 4, 2, 2])
    return run_plan(plan, hq, hk, hv, filters, gain, q, k, starts)


def solution(mesh):
    split = P(("rep", "ctx"), ("ch", "sub"))
    return jax.shard_map(
        per_device,
        mesh=mesh,
        in_specs=(
            split,
            split,
            split,
            P(("ch", "sub"), None),
            P(("ch", "sub")),
            split,
            split,
            P("rep"),
        ),
        out_specs=(split, split),
        check_vma=False,
    )
```

```python
from functools import partial
import math

import jax
import jax.numpy as jnp
from jax import lax
from jax.experimental import pallas as pl
from jax.experimental.pallas import tpu as pltpu
from jax.sharding import PartitionSpec as P

HEAD_DIM = 128
BLOCK = 128
FAR = -1e30
TO_LOG2 = math.log2(math.e) / math.sqrt(HEAD_DIM)
VMEM_LIMIT = 48 * 1024 * 1024
HEADS_AT_ONCE = 2
SMALL = pl.CostEstimate(flops=1024, bytes_accessed=1024, transcendentals=0)
STAT_ROWS = 16


def begin_of(pos, starts):
    begin = jnp.zeros_like(pos)
    for start in starts:
        begin = jnp.where(pos >= start, start, begin)
    return begin


def compiler_params():
    return pltpu.CompilerParams(vmem_limit_bytes=VMEM_LIMIT)


def rounded_product(key, value):
    return (key.astype(jnp.float32) * value.astype(jnp.float32)).astype(jnp.bfloat16)


def halo_kernel(hk, hv, out):
    out[...] = rounded_product(hk[...], hv[...])


def halo_product(hk, hv):
    rows, channels = hk.shape
    width = min(channels, 1024)
    last = pl.BlockSpec((BLOCK, width), lambda j: (rows // BLOCK - 1, j))
    return pl.pallas_call(
        halo_kernel,
        grid=(channels // width,),
        in_specs=[last, last],
        out_specs=pl.BlockSpec((BLOCK, width), lambda j: (0, j)),
        out_shape=jax.ShapeDtypeStruct((BLOCK, channels), jnp.bfloat16),
        compiler_params=pltpu.CompilerParams(vmem_limit_bytes=60 * 1024 * 1024),
        cost_estimate=SMALL,
        name="halo_product",
    )(hk, hv)


def hyena_kernel(genomes, group, info, hq, hk, hv, halo, filters, gain, out, lines, ext, mask):
    rows, width = out.shape
    blocks = rows // BLOCK
    groups = BLOCK // group
    tiles = width // BLOCK
    starts = [info[i] for i in range(genomes)]
    step = pl.program_id(0)
    first = lax.axis_index("ctx") * rows
    row = lax.broadcasted_iota(jnp.int32, (BLOCK, BLOCK), 0)
    col = lax.broadcasted_iota(jnp.int32, (BLOCK, BLOCK), 1)

    @pl.when(step == 0)
    def _():
        turn = jnp.where((row + col) % BLOCK == 0, 1.0, 0.0).astype(jnp.bfloat16)
        lines[...] = jnp.dot(filters[...], turn, preferred_element_type=jnp.float32)
        for b in range(blocks):
            here = first + b * BLOCK
            begin = begin_of(here + row, starts)
            before = (col > row) & (here - BLOCK + col >= begin)
            within = (col <= row) & (here + col >= begin)
            mask[b, :, :BLOCK] = jnp.where(before, 1.0, 0.0).astype(jnp.bfloat16)
            mask[b, :, BLOCK:] = jnp.where(within, 1.0, 0.0).astype(jnp.bfloat16)

    ext[:BLOCK, :] = halo[...]
    ext[BLOCK:, :] = rounded_product(hk[...], hv[...])
    ours = lines[pl.ds(pl.multiple_of(step * groups * tiles, groups * tiles), groups * tiles), :]
    lane_group = col // group
    for t in range(tiles):
        lanes = slice(t * BLOCK, (t + 1) * BLOCK)
        turned = []
        for g in range(groups):
            line = jnp.broadcast_to(ours[t * groups + g, :][None, :], (BLOCK, BLOCK))
            turned.append(pltpu.roll(line, 0, 1, stride=1, stride_axis=0).astype(jnp.bfloat16))
        for b in range(blocks):
            tall = jnp.concatenate(
                [
                    jnp.concatenate([one * mask[b, :, :BLOCK], one * mask[b, :, BLOCK:]], axis=1)
                    for one in turned
                ],
                axis=0,
            )
            window = ext[b * BLOCK : (b + 2) * BLOCK, lanes]
            every = jnp.dot(tall, window, preferred_element_type=jnp.float32)
            filtered = every[:BLOCK]
            for g in range(1, groups):
                filtered = jnp.where(
                    lane_group == g, every[g * BLOCK : (g + 1) * BLOCK], filtered
                )
            at = slice(b * BLOCK, (b + 1) * BLOCK)
            direct = ext[(b + 1) * BLOCK : (b + 2) * BLOCK, lanes].astype(jnp.float32)
            mix = hq[at, lanes].astype(jnp.float32) * (filtered + gain[:, lanes] * direct)
            out[at, lanes] = mix.astype(jnp.bfloat16)


def hyena(starts, hq, hk, hv, halo, filters, gain):
    rows, channels = hk.shape
    group = channels // filters.shape[0]
    width = 2 * BLOCK
    here = lambda r: pl.BlockSpec((r, width), lambda j: (0, j))
    return pl.pallas_call(
        partial(hyena_kernel, starts.shape[0], group),
        grid=(channels // width,),
        in_specs=[
            pl.BlockSpec(memory_space=pltpu.SMEM),
            here(rows),
            here(rows),
            here(rows),
            here(BLOCK),
            pl.BlockSpec(filters.shape, lambda j: (0, 0)),
            here(1),
        ],
        out_specs=here(rows),
        out_shape=jax.ShapeDtypeStruct((rows, channels), jnp.bfloat16),
        scratch_shapes=[
            pltpu.VMEM((filters.shape[0], BLOCK), jnp.float32),
            pltpu.VMEM((rows + BLOCK, width), jnp.bfloat16),
            pltpu.VMEM((rows // BLOCK, BLOCK, 2 * BLOCK), jnp.bfloat16),
        ],
        compiler_params=compiler_params(),
        cost_estimate=SMALL,
        name="hyena_mix",
    )(starts, hq, hk, hv, halo, filters, gain)


def one_of(flags, me):
    on = me < 0
    for d, flag in enumerate(flags):
        if flag:
            on = on | (me == d)
    return on


def attend_kernel(genomes, plan, info, q, k, v, *rest):
    rows = q.shape[0]
    me = lax.axis_index("ctx")
    own = me * rows
    rest = list(rest)
    jobs = [(rows, q, own, None)]
    if plan.na:
        jobs.append((plan.na, rest.pop(0), own + rows, one_of(plan.a_to, me)))
    if plan.nb:
        jobs.append((plan.nb, rest.pop(0), own + 2 * rows, one_of(plan.b_to, me)))
    rk, rv = (rest.pop(0), rest.pop(0)) if plan.nk else (None, None)
    out, stats = rest.pop(0), rest.pop(0)
    outs = [out] + rest[: len(jobs) - 1]
    starts = [info[i] for i in range(genomes)]

    def seen(row_at, count, col_at, columns):
        row = row_at + lax.broadcasted_iota(jnp.int32, (count, columns), 0)
        col = col_at + lax.broadcasted_iota(jnp.int32, (count, columns), 1)
        begin = begin_of(row_at + lax.broadcasted_iota(jnp.int32, (count, 1), 0), starts)
        return (col <= row) & (col >= begin)

    def piece(queries, out, count, row_at, far, put):
        sets = [(k, v, seen(row_at, count, own, rows))]
        if far:
            sets.append((rk, rv, seen(row_at, count, own - plan.nk, plan.nk)))
        for h in range(q.shape[1] // HEAD_DIM):
            lanes = slice(h * HEAD_DIM, (h + 1) * HEAD_DIM)
            scores = [
                jnp.where(
                    visible,
                    lax.dot_general(
                        queries[:, lanes],
                        keys[:, lanes],
                        (((1,), (1,)), ((), ())),
                        preferred_element_type=jnp.float32,
                    ),
                    FAR,
                )
                for keys, _, visible in sets
            ]
            top = jnp.max(scores[0], axis=1, keepdims=True)
            for one in scores[1:]:
                top = jnp.maximum(top, jnp.max(one, axis=1, keepdims=True))
            mixed = 0.0
            for one, (_, values, _) in zip(scores, sets):
                weights = jnp.exp2((one - top) * TO_LOG2).astype(jnp.bfloat16)
                wide = [values[:, lanes], jnp.ones((values.shape[0], HEAD_DIM), jnp.bfloat16)]
                mixed = mixed + jnp.dot(
                    weights, jnp.concatenate(wide, axis=1), preferred_element_type=jnp.float32
                )
            total = mixed[:, HEAD_DIM:]
            out[:count, lanes] = (mixed[:, :HEAD_DIM] / total).astype(jnp.bfloat16)
            put(h, as_rows(top * TO_LOG2 + jnp.log2(total)))

    for (count, queries, at, on), out in zip(jobs, outs):
        put = partial(keep, stats) if on is None else partial(carry, out, count)

        begin = begin_of(at, starts)
        on = True if on is None else on & (begin < own + rows)
        near_only = on
        if plan.nk:
            far = on & (begin < own) & one_of(plan.k_to, me)
            near_only = on & jnp.logical_not(far)

            @pl.when(far)
            def _():
                piece(queries, out, count, at, True, put)

        if near_only is True:
            piece(queries, out, count, at, False, put)
        else:

            @pl.when(near_only)
            def _():
                piece(queries, out, count, at, False, put)

        if on is not True:

            @pl.when(jnp.logical_not(on))
            def _():
                out[:count, :] = jnp.zeros((count, out.shape[1]), jnp.bfloat16)
                for h in range(out.shape[1] // HEAD_DIM):
                    put(h, jnp.full((8, BLOCK), FAR, jnp.float32))


def as_rows(column):
    row = lax.broadcasted_iota(jnp.int32, (BLOCK, BLOCK), 0)
    lane = lax.broadcasted_iota(jnp.int32, (BLOCK, BLOCK), 1)
    rows = [
        jnp.sum(jnp.where(row == lane, column[i : i + BLOCK], 0.0), axis=0, keepdims=True)
        for i in range(0, column.shape[0], BLOCK)
    ]
    return jnp.concatenate(rows + [jnp.zeros_like(rows[0])] * (8 - len(rows)))


def keep(out, h, stat):
    out[h * 8 : (h + 1) * 8, :] = stat


def carry(out, count, h, stat):
    row = lax.broadcasted_iota(jnp.int32, stat.shape, 0)
    stat = jnp.where(row < count // BLOCK, stat, 0.0)
    high = stat.astype(jnp.bfloat16).astype(jnp.float32)
    middle = (stat - high).astype(jnp.bfloat16).astype(jnp.float32)
    low = stat - high - middle
    parts = jnp.concatenate([high + pltpu.roll(low, 4, 0), middle])
    out[count:, h * HEAD_DIM : (h + 1) * HEAD_DIM] = parts.astype(jnp.bfloat16)


def attend(plan, starts, q, k, v, qa, qb, rk, rv, first, heads):
    rows = q.shape[0]
    width = HEADS_AT_ONCE * HEAD_DIM
    here = lambda r: pl.BlockSpec((r, width), lambda h: (0, h))
    later = lambda r, skip, row=0: pl.BlockSpec(
        (r, width), lambda h: (row, h + skip // HEADS_AT_ONCE)
    )
    whole = lambda r: later(r, first)
    in_specs = [pl.BlockSpec(memory_space=pltpu.SMEM), whole(rows), whole(rows), whole(rows)]
    operands = [starts, q, k, v]
    counts = (plan.na, plan.nb, plan.nk, plan.nk)
    for (x, *at), count in zip((qa, qb, rk, rv), counts):
        in_specs.append(later(count, *at))
        operands.append(x)
    out_specs = [here(rows), pl.BlockSpec((HEADS_AT_ONCE * 8, BLOCK), lambda h: (h, 0))]
    out_shape = [
        jax.ShapeDtypeStruct((rows, heads * HEAD_DIM), jnp.bfloat16),
        jax.ShapeDtypeStruct((heads * 8, BLOCK), jnp.float32),
    ]
    for count in (plan.na, plan.nb):
        if count:
            out_specs.append(here(count + STAT_ROWS))
            out_shape.append(
                jax.ShapeDtypeStruct((count + STAT_ROWS, heads * HEAD_DIM), jnp.bfloat16)
            )
    queries, keys = rows + plan.na + plan.nb, rows + plan.nk
    return pl.pallas_call(
        partial(attend_kernel, starts.shape[0], plan),
        grid=(heads // HEADS_AT_ONCE,),
        in_specs=in_specs,
        out_specs=out_specs,
        out_shape=out_shape,
        compiler_params=compiler_params(),
        cost_estimate=SMALL,
        name="attend_parts",
    )(*operands)


def join_kernel(plan, o, s, *rest):
    rest = list(rest)
    me = lax.axis_index("ctx")
    out, done = rest[-2:]
    rows = o.shape[0]
    done[...] = s[:8, :]
    block = lax.broadcasted_iota(jnp.int32, (8, BLOCK), 0)
    parts = [(o, rows, None)]
    for count, flags in ((plan.na, plan.a_from), (plan.nb, plan.b_from)):
        if count:
            parts.append((rest.pop(0), count, one_of(flags, me) & (block < count // BLOCK)))
    for h in range(o.shape[1] // HEAD_DIM):
        lanes = slice(h * HEAD_DIM, (h + 1) * HEAD_DIM)
        stats = [s[h * 8 : (h + 1) * 8, :]]
        for part, count, on in parts[1:]:
            carried = part[count:, lanes].astype(jnp.float32)
            stat = carried[:8] + pltpu.roll(carried[:8], 4, 0) + carried[8:]
            stats.append(jnp.where(on, stat, FAR))
        top = stats[0]
        for x in stats[1:]:
            top = jnp.maximum(top, x)
        weights = [jnp.exp2(x - top) for x in stats]
        total = sum(weights)
        weights = [(w / total).T for w in weights]
        for i in range(rows // BLOCK):
            sl = slice(i * BLOCK, (i + 1) * BLOCK)
            mixed = sum(
                w[:, i : i + 1] * part[sl, lanes].astype(jnp.float32)
                for w, (part, count, _) in zip(weights, parts)
                if i * BLOCK < count
            )
            out[sl, lanes] = mixed.astype(jnp.bfloat16)


def join(plan, o, s, others, first, channels, full):
    rows, wide = o.shape
    width = HEADS_AT_ONCE * HEAD_DIM
    skip = first // HEADS_AT_ONCE
    here = lambda r: pl.BlockSpec((r, width), lambda h: (0, h))
    operands = [o, s] + others
    in_specs = [here(rows), pl.BlockSpec((HEADS_AT_ONCE * 8, BLOCK), lambda h: (h, 0))]
    in_specs += [here(x.shape[0]) for x in others]
    aliases = {}
    if full is not None:
        in_specs.append(pl.BlockSpec(memory_space=pl.ANY))
        operands.append(full)
        aliases = {len(operands) - 1: 0}
    return pl.pallas_call(
        partial(join_kernel, plan),
        grid=(wide // width,),
        in_specs=in_specs,
        out_specs=[
            pl.BlockSpec((rows, width), lambda h: (0, h + skip)),
            pl.BlockSpec((8, BLOCK), lambda h: (0, 0)),
        ],
        out_shape=[
            jax.ShapeDtypeStruct((rows, channels), jnp.bfloat16),
            jax.ShapeDtypeStruct((8, BLOCK), jnp.float32),
        ],
        input_output_aliases=aliases,
        compiler_params=compiler_params(),
        cost_estimate=SMALL,
        name="join_parts",
    )(*operands)


class Plan:
    def __init__(self, rows, n, heads):
        self.a, self.b, self.k = [(2, 1), (3, 2)], [(3, 1)], [(0, 1)]
        self.na, self.nb, self.nk = rows, rows - BLOCK, rows
        self.heads = heads
        ends = lambda pairs, side: [int(any(p[side] == d for p in pairs)) for d in range(n)]
        self.a_from, self.a_to = ends(self.a, 0), ends(self.a, 1)
        self.b_from, self.b_to = ends(self.b, 0), ends(self.b, 1)
        self.k_to = ends(self.k, 1)


def after(value, *earlier):
    return lax.optimization_barrier((value, *earlier))[0] if earlier else value


def run_plan(plan, hq, hk, hv, filters, gain, q, k, starts):
    n = lax.axis_size("ctx")
    rows, channels = hk.shape
    send = lambda x, pairs: lax.ppermute(x, "ctx", pairs)
    back = lambda pairs: [(t, s) for s, t in pairs]
    columns = lambda x, first, end: x[:, first * HEAD_DIM : end * HEAD_DIM]

    halo = send(halo_product(hk, hv), [(i, i + 1) for i in range(n - 1)])
    mix = hyena(starts, hq, hk, hv, halo, filters, gain)
    heads, total = plan.heads, channels // HEAD_DIM
    early = sum(heads[:2])
    rk = [send(columns(k, 0, heads[0]), plan.k)]
    rk.append(send(after(columns(k, heads[0], early), halo), plan.k))
    qa = send(columns(q, 0, early), plan.a)
    qb = send(columns(q[: plan.nb], 0, early), plan.b)
    later_a = send(after(columns(q, early, total), halo), plan.a)

    told, joined, came_back, out, go = [], [], [], None, None
    first = q_at = 0
    for c, many in enumerate(heads):
        end = first + many
        if first == early:
            q_at, qa = first, later_a
            qb = send(after(columns(q[: plan.nb], early, total), told[0]), plan.b)
        if end <= early:
            keys = (rk[c], 0)
            values = (send(columns(mix, first, end), plan.k), 0, 0)
            go = values[0] if go is None else go
        else:
            pair = jnp.concatenate([columns(k, first, end), columns(mix, first, end)])
            pair = send(after(pair, told[max(0, c - 3)]), plan.k)
            keys, values = (pair, 0), (pair, 0, 1)
        ready = after(starts, *(came_back[c - 2] if c >= 2 else ()), *joined[: max(0, c - 2)])
        o, s, *parts = attend(
            plan, ready, q, k, mix, (qa, first - q_at), (qb, first - q_at), keys, values, first, many
        )
        told.append(s)
        came_back.append([send(x, back(p)) for x, p in zip(parts, (plan.a, plan.b))])
        out, done = join(plan, o, s, came_back[-1], first, channels, out)
        joined.append(done)
        first = end
    return mix, out


def attend_update(queries, query_pos, query_begin, key_heads, value_heads, key_pos):
    score_scale = 1.0 / math.sqrt(HEAD_DIM)
    scores = (
        jnp.einsum("qhd,khd->hqk", queries, key_heads, preferred_element_type=jnp.float32)
        * score_scale
    )
    visible = (key_pos[None, :] <= query_pos[:, None]) & (key_pos[None, :] >= query_begin[:, None])
    new_max = jnp.max(jnp.where(visible[None], scores, FAR), axis=2)
    weights = jnp.exp(jnp.where(visible[None], scores - new_max[:, :, None], FAR))
    mixed = jnp.einsum(
        "hqk,khd->hqd",
        weights.astype(jnp.bfloat16),
        value_heads,
        preferred_element_type=jnp.float32,
    )
    return mixed / jnp.sum(weights, axis=2)[:, :, None]


def run_gathered(hq, hk, hv, filters, gain, q, k, starts):
    n = lax.axis_size("ctx")
    rows, channels = hk.shape
    heads = channels // HEAD_DIM
    own = (lax.axis_index("ctx") * rows).astype(jnp.int32)
    halo = lax.ppermute(halo_product(hk, hv), "ctx", [(i, i + 1) for i in range(n - 1)])
    mix = hyena(starts, hq, hk, hv, halo, filters, gain)
    keys = lax.all_gather(k, "ctx", axis=0, tiled=True)
    values = lax.all_gather(mix, "ctx", axis=0, tiled=True)
    key_pos = jnp.arange(n * rows, dtype=jnp.int32)
    pos = own + jnp.arange(rows, dtype=jnp.int32)
    mixed = attend_update(
        q.reshape(rows, heads, HEAD_DIM),
        pos,
        begin_of(pos, [starts[i] for i in range(starts.shape[0])]),
        keys.reshape(n * rows, heads, HEAD_DIM),
        values.reshape(n * rows, heads, HEAD_DIM),
        key_pos,
    )
    return mix, mixed.astype(jnp.bfloat16).transpose(1, 0, 2).reshape(rows, channels)


def per_device(hq, hk, hv, filters, skip_gain, q, k, starts):
    rows, channels = hk.shape
    n = lax.axis_size("ctx")
    gain = skip_gain[None, :]
    if n != 4:
        return run_gathered(hq, hk, hv, filters, gain, q, k, starts)
    plan = Plan(rows, n, [4, 4, 4, 2, 2])
    return run_plan(plan, hq, hk, hv, filters, gain, q, k, starts)


def solution(mesh):
    split = P(("rep", "ctx"), ("ch", "sub"))
    return jax.shard_map(
        per_device,
        mesh=mesh,
        in_specs=(
            split,
            split,
            split,
            P(("ch", "sub"), None),
            P(("ch", "sub")),
            split,
            split,
            P("rep"),
        ),
        out_specs=(split, split),
        check_vma=False,
    )
```

```python
from functools import partial
import math

import jax
import jax.numpy as jnp
from jax import lax
from jax.experimental import pallas as pl
from jax.experimental.pallas import tpu as pltpu
from jax.sharding import PartitionSpec as P

HEAD_DIM = 128
BLOCK = 128
FAR = -1e30
TO_LOG2 = math.log2(math.e) / math.sqrt(HEAD_DIM)
VMEM_LIMIT = 48 * 1024 * 1024
HEADS_AT_ONCE = 2
SMALL = pl.CostEstimate(flops=1024, bytes_accessed=1024, transcendentals=0)
STAT_ROWS = 16


def begin_of(pos, starts):
    begin = jnp.zeros_like(pos)
    for start in starts:
        begin = jnp.where(pos >= start, start, begin)
    return begin


def compiler_params():
    return pltpu.CompilerParams(vmem_limit_bytes=VMEM_LIMIT)


def rounded_product(key, value):
    return (key.astype(jnp.float32) * value.astype(jnp.float32)).astype(jnp.bfloat16)


def halo_kernel(hk, hv, out):
    out[...] = rounded_product(hk[...], hv[...])


def halo_product(hk, hv):
    rows, channels = hk.shape
    width = min(channels, 1024)
    last = pl.BlockSpec((BLOCK, width), lambda j: (rows // BLOCK - 1, j))
    return pl.pallas_call(
        halo_kernel,
        grid=(channels // width,),
        in_specs=[last, last],
        out_specs=pl.BlockSpec((BLOCK, width), lambda j: (0, j)),
        out_shape=jax.ShapeDtypeStruct((BLOCK, channels), jnp.bfloat16),
        compiler_params=pltpu.CompilerParams(vmem_limit_bytes=60 * 1024 * 1024),
        cost_estimate=SMALL,
        name="halo_product",
    )(hk, hv)


def hyena_kernel(genomes, group, info, hq, hk, hv, halo, filters, gain, out, lines, ext, mask):
    rows, width = out.shape
    blocks = rows // BLOCK
    groups = BLOCK // group
    tiles = width // BLOCK
    starts = [info[i] for i in range(genomes)]
    step = pl.program_id(0)
    first = lax.axis_index("ctx") * rows
    row = lax.broadcasted_iota(jnp.int32, (BLOCK, BLOCK), 0)
    col = lax.broadcasted_iota(jnp.int32, (BLOCK, BLOCK), 1)

    @pl.when(step == 0)
    def _():
        turn = jnp.where((row + col) % BLOCK == 0, 1.0, 0.0).astype(jnp.bfloat16)
        lines[...] = jnp.dot(filters[...], turn, preferred_element_type=jnp.float32)
        for b in range(blocks):
            here = first + b * BLOCK
            begin = begin_of(here + row, starts)
            before = (col > row) & (here - BLOCK + col >= begin)
            within = (col <= row) & (here + col >= begin)
            mask[b, :, :BLOCK] = jnp.where(before, 1.0, 0.0).astype(jnp.bfloat16)
            mask[b, :, BLOCK:] = jnp.where(within, 1.0, 0.0).astype(jnp.bfloat16)

    ext[:BLOCK, :] = halo[...]
    ext[BLOCK:, :] = rounded_product(hk[...], hv[...])
    ours = lines[pl.ds(pl.multiple_of(step * groups * tiles, groups * tiles), groups * tiles), :]
    lane_group = col // group
    for t in range(tiles):
        lanes = slice(t * BLOCK, (t + 1) * BLOCK)
        turned = []
        for g in range(groups):
            line = jnp.broadcast_to(ours[t * groups + g, :][None, :], (BLOCK, BLOCK))
            turned.append(pltpu.roll(line, 0, 1, stride=1, stride_axis=0).astype(jnp.bfloat16))
        for b in range(blocks):
            tall = jnp.concatenate(
                [
                    jnp.concatenate([one * mask[b, :, :BLOCK], one * mask[b, :, BLOCK:]], axis=1)
                    for one in turned
                ],
                axis=0,
            )
            window = ext[b * BLOCK : (b + 2) * BLOCK, lanes]
            every = jnp.dot(tall, window, preferred_element_type=jnp.float32)
            filtered = every[:BLOCK]
            for g in range(1, groups):
                filtered = jnp.where(
                    lane_group == g, every[g * BLOCK : (g + 1) * BLOCK], filtered
                )
            at = slice(b * BLOCK, (b + 1) * BLOCK)
            direct = ext[(b + 1) * BLOCK : (b + 2) * BLOCK, lanes].astype(jnp.float32)
            mix = hq[at, lanes].astype(jnp.float32) * (filtered + gain[:, lanes] * direct)
            out[at, lanes] = mix.astype(jnp.bfloat16)


def hyena(starts, hq, hk, hv, halo, filters, gain):
    rows, channels = hk.shape
    group = channels // filters.shape[0]
    width = 2 * BLOCK
    here = lambda r: pl.BlockSpec((r, width), lambda j: (0, j))
    return pl.pallas_call(
        partial(hyena_kernel, starts.shape[0], group),
        grid=(channels // width,),
        in_specs=[
            pl.BlockSpec(memory_space=pltpu.SMEM),
            here(rows),
            here(rows),
            here(rows),
            here(BLOCK),
            pl.BlockSpec(filters.shape, lambda j: (0, 0)),
            here(1),
        ],
        out_specs=here(rows),
        out_shape=jax.ShapeDtypeStruct((rows, channels), jnp.bfloat16),
        scratch_shapes=[
            pltpu.VMEM((filters.shape[0], BLOCK), jnp.float32),
            pltpu.VMEM((rows + BLOCK, width), jnp.bfloat16),
            pltpu.VMEM((rows // BLOCK, BLOCK, 2 * BLOCK), jnp.bfloat16),
        ],
        compiler_params=compiler_params(),
        cost_estimate=SMALL,
        name="hyena_mix",
    )(starts, hq, hk, hv, halo, filters, gain)


def one_of(flags, me):
    on = me < 0
    for d, flag in enumerate(flags):
        if flag:
            on = on | (me == d)
    return on


def attend_kernel(genomes, plan, info, q, k, v, *rest):
    rows = q.shape[0]
    me = lax.axis_index("ctx")
    own = me * rows
    rest = list(rest)
    jobs = [(rows, q, own, None)]
    if plan.na:
        jobs.append((plan.na, rest.pop(0), own + rows, one_of(plan.a_to, me)))
    if plan.nb:
        jobs.append((plan.nb, rest.pop(0), own + 2 * rows, one_of(plan.b_to, me)))
    rk, rv = (rest.pop(0), rest.pop(0)) if plan.nk else (None, None)
    out, stats = rest.pop(0), rest.pop(0)
    outs = [out] + rest[: len(jobs) - 1]
    starts = [info[i] for i in range(genomes)]

    def seen(row_at, count, col_at, columns):
        row = row_at + lax.broadcasted_iota(jnp.int32, (count, columns), 0)
        col = col_at + lax.broadcasted_iota(jnp.int32, (count, columns), 1)
        begin = begin_of(row_at + lax.broadcasted_iota(jnp.int32, (count, 1), 0), starts)
        return (col <= row) & (col >= begin)

    def piece(queries, out, count, row_at, far, put):
        sets = [(k, v, seen(row_at, count, own, rows))]
        if far:
            sets.append((rk, rv, seen(row_at, count, own - plan.nk, plan.nk)))
        for h in range(q.shape[1] // HEAD_DIM):
            lanes = slice(h * HEAD_DIM, (h + 1) * HEAD_DIM)
            scores = [
                jnp.where(
                    visible,
                    lax.dot_general(
                        queries[:, lanes],
                        keys[:, lanes],
                        (((1,), (1,)), ((), ())),
                        preferred_element_type=jnp.float32,
                    ),
                    FAR,
                )
                for keys, _, visible in sets
            ]
            top = jnp.max(scores[0], axis=1, keepdims=True)
            for one in scores[1:]:
                top = jnp.maximum(top, jnp.max(one, axis=1, keepdims=True))
            mixed = 0.0
            for one, (_, values, _) in zip(scores, sets):
                weights = jnp.exp2((one - top) * TO_LOG2).astype(jnp.bfloat16)
                wide = [values[:, lanes], jnp.ones((values.shape[0], HEAD_DIM), jnp.bfloat16)]
                mixed = mixed + jnp.dot(
                    weights, jnp.concatenate(wide, axis=1), preferred_element_type=jnp.float32
                )
            total = mixed[:, HEAD_DIM:]
            out[:count, lanes] = (mixed[:, :HEAD_DIM] / total).astype(jnp.bfloat16)
            put(h, as_rows(top * TO_LOG2 + jnp.log2(total)))

    for (count, queries, at, on), out in zip(jobs, outs):
        put = partial(keep, stats) if on is None else partial(carry, out, count)

        begin = begin_of(at, starts)
        on = True if on is None else on & (begin < own + rows)
        near_only = on
        if plan.nk:
            far = on & (begin < own) & one_of(plan.k_to, me)
            near_only = on & jnp.logical_not(far)

            @pl.when(far)
            def _():
                piece(queries, out, count, at, True, put)

        if near_only is True:
            piece(queries, out, count, at, False, put)
        else:

            @pl.when(near_only)
            def _():
                piece(queries, out, count, at, False, put)

        if on is not True:

            @pl.when(jnp.logical_not(on))
            def _():
                out[:count, :] = jnp.zeros((count, out.shape[1]), jnp.bfloat16)
                for h in range(out.shape[1] // HEAD_DIM):
                    put(h, jnp.full((8, BLOCK), FAR, jnp.float32))


def as_rows(column):
    row = lax.broadcasted_iota(jnp.int32, (BLOCK, BLOCK), 0)
    lane = lax.broadcasted_iota(jnp.int32, (BLOCK, BLOCK), 1)
    rows = [
        jnp.sum(jnp.where(row == lane, column[i : i + BLOCK], 0.0), axis=0, keepdims=True)
        for i in range(0, column.shape[0], BLOCK)
    ]
    return jnp.concatenate(rows + [jnp.zeros_like(rows[0])] * (8 - len(rows)))


def keep(out, h, stat):
    out[h * 8 : (h + 1) * 8, :] = stat


def carry(out, count, h, stat):
    row = lax.broadcasted_iota(jnp.int32, stat.shape, 0)
    stat = jnp.where(row < count // BLOCK, stat, 0.0)
    high = stat.astype(jnp.bfloat16).astype(jnp.float32)
    middle = (stat - high).astype(jnp.bfloat16).astype(jnp.float32)
    low = stat - high - middle
    parts = jnp.concatenate([high + pltpu.roll(low, 4, 0), middle])
    out[count:, h * HEAD_DIM : (h + 1) * HEAD_DIM] = parts.astype(jnp.bfloat16)


def attend(plan, starts, q, k, v, qa, qb, rk, rv, first, heads):
    rows = q.shape[0]
    width = HEADS_AT_ONCE * HEAD_DIM
    here = lambda r: pl.BlockSpec((r, width), lambda h: (0, h))
    later = lambda r, skip, row=0: pl.BlockSpec(
        (r, width), lambda h: (row, h + skip // HEADS_AT_ONCE)
    )
    whole = lambda r: later(r, first)
    in_specs = [pl.BlockSpec(memory_space=pltpu.SMEM), whole(rows), whole(rows), whole(rows)]
    operands = [starts, q, k, v]
    counts = (plan.na, plan.nb, plan.nk, plan.nk)
    for (x, *at), count in zip((qa, qb, rk, rv), counts):
        in_specs.append(later(count, *at))
        operands.append(x)
    out_specs = [here(rows), pl.BlockSpec((HEADS_AT_ONCE * 8, BLOCK), lambda h: (h, 0))]
    out_shape = [
        jax.ShapeDtypeStruct((rows, heads * HEAD_DIM), jnp.bfloat16),
        jax.ShapeDtypeStruct((heads * 8, BLOCK), jnp.float32),
    ]
    for count in (plan.na, plan.nb):
        if count:
            out_specs.append(here(count + STAT_ROWS))
            out_shape.append(
                jax.ShapeDtypeStruct((count + STAT_ROWS, heads * HEAD_DIM), jnp.bfloat16)
            )
    queries, keys = rows + plan.na + plan.nb, rows + plan.nk
    return pl.pallas_call(
        partial(attend_kernel, starts.shape[0], plan),
        grid=(heads // HEADS_AT_ONCE,),
        in_specs=in_specs,
        out_specs=out_specs,
        out_shape=out_shape,
        compiler_params=compiler_params(),
        cost_estimate=SMALL,
        name="attend_parts",
    )(*operands)


def join_kernel(plan, o, s, *rest):
    rest = list(rest)
    me = lax.axis_index("ctx")
    out, done = rest[-2:]
    rows = o.shape[0]
    done[...] = s[:8, :]
    block = lax.broadcasted_iota(jnp.int32, (8, BLOCK), 0)
    parts = [(o, rows, None)]
    for count, flags in ((plan.na, plan.a_from), (plan.nb, plan.b_from)):
        if count:
            parts.append((rest.pop(0), count, one_of(flags, me) & (block < count // BLOCK)))
    for h in range(o.shape[1] // HEAD_DIM):
        lanes = slice(h * HEAD_DIM, (h + 1) * HEAD_DIM)
        stats = [s[h * 8 : (h + 1) * 8, :]]
        for part, count, on in parts[1:]:
            carried = part[count:, lanes].astype(jnp.float32)
            stat = carried[:8] + pltpu.roll(carried[:8], 4, 0) + carried[8:]
            stats.append(jnp.where(on, stat, FAR))
        top = stats[0]
        for x in stats[1:]:
            top = jnp.maximum(top, x)
        weights = [jnp.exp2(x - top) for x in stats]
        total = sum(weights)
        weights = [(w / total).T for w in weights]
        for i in range(rows // BLOCK):
            sl = slice(i * BLOCK, (i + 1) * BLOCK)
            mixed = sum(
                w[:, i : i + 1] * part[sl, lanes].astype(jnp.float32)
                for w, (part, count, _) in zip(weights, parts)
                if i * BLOCK < count
            )
            out[sl, lanes] = mixed.astype(jnp.bfloat16)


def join(plan, o, s, others, first, channels, full):
    rows, wide = o.shape
    width = HEADS_AT_ONCE * HEAD_DIM
    skip = first // HEADS_AT_ONCE
    here = lambda r: pl.BlockSpec((r, width), lambda h: (0, h))
    operands = [o, s] + others
    in_specs = [here(rows), pl.BlockSpec((HEADS_AT_ONCE * 8, BLOCK), lambda h: (h, 0))]
    in_specs += [here(x.shape[0]) for x in others]
    aliases = {}
    if full is not None:
        in_specs.append(pl.BlockSpec(memory_space=pl.ANY))
        operands.append(full)
        aliases = {len(operands) - 1: 0}
    return pl.pallas_call(
        partial(join_kernel, plan),
        grid=(wide // width,),
        in_specs=in_specs,
        out_specs=[
            pl.BlockSpec((rows, width), lambda h: (0, h + skip)),
            pl.BlockSpec((8, BLOCK), lambda h: (0, 0)),
        ],
        out_shape=[
            jax.ShapeDtypeStruct((rows, channels), jnp.bfloat16),
            jax.ShapeDtypeStruct((8, BLOCK), jnp.float32),
        ],
        input_output_aliases=aliases,
        compiler_params=compiler_params(),
        cost_estimate=SMALL,
        name="join_parts",
    )(*operands)


class Plan:
    def __init__(self, rows, n, heads):
        self.a, self.b, self.k = [(2, 1), (3, 2)], [(3, 1)], [(0, 1)]
        self.na, self.nb, self.nk = rows, rows - BLOCK, rows
        self.heads = heads
        ends = lambda pairs, side: [int(any(p[side] == d for p in pairs)) for d in range(n)]
        self.a_from, self.a_to = ends(self.a, 0), ends(self.a, 1)
        self.b_from, self.b_to = ends(self.b, 0), ends(self.b, 1)
        self.k_to = ends(self.k, 1)


def after(value, *earlier):
    return lax.optimization_barrier((value, *earlier))[0] if earlier else value


def run_plan(plan, hq, hk, hv, filters, gain, q, k, starts):
    n = lax.axis_size("ctx")
    rows, channels = hk.shape
    send = lambda x, pairs: lax.ppermute(x, "ctx", pairs)
    back = lambda pairs: [(t, s) for s, t in pairs]
    columns = lambda x, first, end: x[:, first * HEAD_DIM : end * HEAD_DIM]

    halo = send(halo_product(hk, hv), [(i, i + 1) for i in range(n - 1)])
    mix = hyena(starts, hq, hk, hv, halo, filters, gain)
    heads, total = plan.heads, channels // HEAD_DIM
    early = sum(heads[:2])
    rk = [send(columns(k, 0, heads[0]), plan.k)]
    rk.append(send(after(columns(k, heads[0], early), halo), plan.k))
    qa = send(columns(q, 0, early), plan.a)
    qb = send(columns(q[: plan.nb], 0, early), plan.b)
    later_a = send(after(columns(q, early, total), halo), plan.a)

    told, joined, came_back, out, go = [], [], [], None, None
    first = q_at = 0
    for c, many in enumerate(heads):
        end = first + many
        if first == early:
            q_at, qa = first, later_a
            qb = send(after(columns(q[: plan.nb], early, total), told[0]), plan.b)
        if end <= early:
            keys = (rk[c], 0)
            values = (send(columns(mix, first, end), plan.k), 0, 0)
            go = values[0] if go is None else go
        else:
            pair = jnp.concatenate([columns(k, first, end), columns(mix, first, end)])
            pair = send(after(pair, told[max(0, c - 3)]), plan.k)
            keys, values = (pair, 0), (pair, 0, 1)
        ready = after(starts, *(came_back[c - 2] if c >= 2 else ()), *joined[: 2 if c >= 3 else 0])
        o, s, *parts = attend(
            plan, ready, q, k, mix, (qa, first - q_at), (qb, first - q_at), keys, values, first, many
        )
        told.append(s)
        came_back.append([send(x, back(p)) for x, p in zip(parts, (plan.a, plan.b))])
        out, done = join(plan, o, s, came_back[-1], first, channels, out)
        joined.append(done)
        first = end
    return mix, out


def attend_update(queries, query_pos, query_begin, key_heads, value_heads, key_pos):
    score_scale = 1.0 / math.sqrt(HEAD_DIM)
    scores = (
        jnp.einsum("qhd,khd->hqk", queries, key_heads, preferred_element_type=jnp.float32)
        * score_scale
    )
    visible = (key_pos[None, :] <= query_pos[:, None]) & (key_pos[None, :] >= query_begin[:, None])
    new_max = jnp.max(jnp.where(visible[None], scores, FAR), axis=2)
    weights = jnp.exp(jnp.where(visible[None], scores - new_max[:, :, None], FAR))
    mixed = jnp.einsum(
        "hqk,khd->hqd",
        weights.astype(jnp.bfloat16),
        value_heads,
        preferred_element_type=jnp.float32,
    )
    return mixed / jnp.sum(weights, axis=2)[:, :, None]


def run_gathered(hq, hk, hv, filters, gain, q, k, starts):
    n = lax.axis_size("ctx")
    rows, channels = hk.shape
    heads = channels // HEAD_DIM
    own = (lax.axis_index("ctx") * rows).astype(jnp.int32)
    halo = lax.ppermute(halo_product(hk, hv), "ctx", [(i, i + 1) for i in range(n - 1)])
    mix = hyena(starts, hq, hk, hv, halo, filters, gain)
    keys = lax.all_gather(k, "ctx", axis=0, tiled=True)
    values = lax.all_gather(mix, "ctx", axis=0, tiled=True)
    key_pos = jnp.arange(n * rows, dtype=jnp.int32)
    pos = own + jnp.arange(rows, dtype=jnp.int32)
    mixed = attend_update(
        q.reshape(rows, heads, HEAD_DIM),
        pos,
        begin_of(pos, [starts[i] for i in range(starts.shape[0])]),
        keys.reshape(n * rows, heads, HEAD_DIM),
        values.reshape(n * rows, heads, HEAD_DIM),
        key_pos,
    )
    return mix, mixed.astype(jnp.bfloat16).transpose(1, 0, 2).reshape(rows, channels)


def per_device(hq, hk, hv, filters, skip_gain, q, k, starts):
    rows, channels = hk.shape
    n = lax.axis_size("ctx")
    gain = skip_gain[None, :]
    if n != 4:
        return run_gathered(hq, hk, hv, filters, gain, q, k, starts)
    plan = Plan(rows, n, [4, 4, 4, 2, 2])
    return run_plan(plan, hq, hk, hv, filters, gain, q, k, starts)


def solution(mesh):
    split = P(("rep", "ctx"), ("ch", "sub"))
    return jax.shard_map(
        per_device,
        mesh=mesh,
        in_specs=(
            split,
            split,
            split,
            P(("ch", "sub"), None),
            P(("ch", "sub")),
            split,
            split,
            P("rep"),
        ),
        out_specs=(split, split),
        check_vma=False,
    )
```
